32 devices in a mesh: blk: 8 (over y, x, core), gene: 4 (over z).
Axes of the slice: x: 2, y: 2, z: 4, core: 2. Of those that a mesh axis runs over, the one named last changes fastest.
Arguments:
- logits: float32 [11264, 1024], P(None, 'blk'), may hold values from -6 to 6
- expression: float32 [11264, 2048], P('blk', 'gene'), may hold values from 0.05 to 5
- spatial: float32 [1024, 2048], P('blk', 'gene'), may hold values from 0.05 to 5
- density: float32 [11264], replicated, may hold values from 0.1 to 10
- gene_mask: int32 [4, 2048], P(None, 'gene'), may hold values 0 or 1
- gene_counts: int32 [2048], P('gene'), may hold values from 1 to 10
- slide_ids: int32 [1024], P('blk'), may hold values from 0 to 3
Outputs:
- loss: float32 [], replicated
- logit_grad: float32 [11264, 1024], P(None, 'blk')
- expr_grad: float32 [11264, 2048], P('blk', 'gene')
- rms_map: float32 [], replicated
- rms_pred: float32 [], replicated
The draws below stay inside these ranges and needn't reach their ends.
All inputs are finite; a program needn't handle non-finite values. No bound on the sum of `gene_mask` on one device may be relied on, other than what follows from the above.
Results may differ from the reference program's by a relative error of at most 0.0003.
Values sent between devices are 32-bit elements; how exact they have to be, the bound alone decides.
No kernel may reach another device: no remote copies, remote signals or barrier semaphores. Data moves between devices by JAX's collectives and lax.ppermute only.
A program may use at most 320 MiB of HBM per device.

```python
import math
import jax
import jax.numpy as jnp
from jax import lax

GENES = 2048
SLIDES = 4
CELLS = 11264
SPOTS = 1024


def with_ends(drawn, rng, low, high):
    extent = drawn.shape
    place = [jax.random.randint(jax.random.fold_in(rng, axis), (), 0, extent[axis]) for axis in range(len(extent))]
    drawn = drawn.at[tuple(place)].set(low)
    longest = extent.index(max(extent))
    place[longest] = (place[longest] + 1) % extent[longest]
    return drawn.at[tuple(place)].set(high)


def shard_levels(own_key, dims, cuts, smallest, high):
    loudness = 1.0
    for axis_at, parts in cuts:
        steps = jax.random.uniform(jax.random.fold_in(jax.random.fold_in(own_key, 6), axis_at), (parts,), jnp.float32, smallest / len(cuts), high / len(cuts))
        loudness = loudness * jnp.repeat(jnp.exp(steps), dims[axis_at] // parts).reshape((-1,) + (1,) * (len(dims) - 1 - axis_at))
    return loudness


def gaussian(rng, shape, scale, reach, shards=(), kind=jnp.bfloat16):
    gain = shard_levels(rng, shape, shards, -0.22, 0.18) if shards else 1.0
    entries = jax.random.normal(rng, shape, jnp.float32) * scale * gain
    return jnp.minimum(jnp.maximum(entries, -reach), reach).astype(kind)


def setup_inputs(seed: int = 0) -> dict:
    streams_of = jax.random.split(jax.random.key(seed), 8)
    logits = gaussian(streams_of[0], (CELLS, SPOTS), 1.0, 6.0, ((1, 8),), jnp.float32)
    expression = jnp.clip(jnp.exp(math.log(5.0) - 4.6051702 * jax.random.uniform(streams_of[1], (CELLS, GENES), jnp.float32) ** shard_levels(streams_of[1], (CELLS, GENES), ((0, 8), (1, 4)), -0.2, 0.2)), 0.05, 5.0)
    spatial = jnp.clip(jnp.exp(math.log(5.0) - 4.6051702 * jax.random.uniform(streams_of[2], (SPOTS, GENES), jnp.float32) ** shard_levels(streams_of[2], (SPOTS, GENES), ((0, 8), (1, 4)), -0.2, 0.2)), 0.05, 5.0)
    density = jnp.clip(jnp.exp(jax.random.uniform(streams_of[3], (CELLS,), jnp.float32, math.log(0.1), math.log(10.0))), 0.1, 10.0)
    gene_mask = with_ends((jax.random.randint(streams_of[4], (SLIDES, GENES), 0, 4) < 3).astype(jnp.int32), jax.random.fold_in(streams_of[4], 1), 0, 1)
    gene_counts = with_ends(jax.random.randint(streams_of[5], (GENES,), 1, 11), jax.random.fold_in(streams_of[5], 1), 1, 10).astype(jnp.int32)
    slide_ids = with_ends(jax.random.randint(streams_of[6], (SPOTS,), 0, SLIDES), jax.random.fold_in(streams_of[6], 1), 0, SLIDES - 1).astype(jnp.int32)
    return {"logits": logits, "expression": expression, "spatial": spatial, "density": density, "gene_mask": gene_mask, "gene_counts": gene_counts, "slide_ids": slide_ids}


@jax.custom_vjp
def low(v):
    return lax.optimization_barrier(v.astype(jnp.bfloat16)).astype(jnp.float32)

@jax.custom_vjp
def low_back(v):
    return v

def low_keep(v):
    return (low(v), None)

def low_pass(kept, grad):
    return (grad,)

def back_keep(v):
    return (v, None)

def back_low(kept, grad):
    return (low(grad),)
low.defvjp(low_keep, low_pass)
low_back.defvjp(back_keep, back_low)
HIGH = lax.Precision.HIGHEST

def forward(logits, expression, spatial, density, gene_mask, gene_counts, slide_ids):
    mapping = jax.nn.softmax(logits, axis=0)
    pred = jnp.dot(mapping.T, expression, precision=HIGH, preferred_element_type=jnp.float32)
    onehot = (slide_ids[None, :] == jnp.arange(SLIDES, dtype=jnp.int32)[:, None]).astype(jnp.float32)
    sum_a = jnp.dot(onehot, pred * spatial, precision=HIGH)
    sum_b = jnp.dot(onehot, pred * pred, precision=HIGH)
    sum_c = jnp.dot(onehot, spatial * spatial, precision=HIGH)
    gcos = sum_a * lax.rsqrt(sum_b * sum_c + 1e-06)
    weights = (gene_mask * gene_counts[None, :]).astype(jnp.float32)
    wsum = jnp.sum(weights)
    sum_e = lax.optimization_barrier(jnp.sum(pred * spatial, axis=1))
    sum_f = lax.optimization_barrier(jnp.sum(pred * pred, axis=1))
    sum_h = lax.optimization_barrier(jnp.sum(spatial * spatial, axis=1))
    scos = sum_e * lax.rsqrt(sum_f * sum_h + 1e-06)
    cell_q = lax.optimization_barrier(jnp.sum(mapping, axis=1)) / SPOTS
    target = density / jnp.sum(density)
    kl_term = jnp.sum(target * (jnp.log(target) - jnp.log(cell_q)))
    loss = -jnp.sum(weights * gcos) / wsum - jnp.sum(scos) / SPOTS + kl_term
    rms_map = jnp.sqrt(jnp.sum(mapping * mapping) / (CELLS * SPOTS))
    rms_pred = jnp.sqrt(jnp.sum(pred * pred) / (SPOTS * GENES))
    return (loss, (rms_map, rms_pred))

def reference(logits, expression, spatial, density, gene_mask, gene_counts, slide_ids):

    def closed(lg, ex):
        return forward(lg, ex, spatial, density, gene_mask, gene_counts, slide_ids)
    loss, pullback, extra = jax.vjp(closed, logits, expression, has_aux=True)
    logit_grad, expr_grad = pullback(jnp.ones((), jnp.float32))
    return (loss, logit_grad * CELLS, expr_grad * CELLS, extra[0], extra[1])
```

```python
import jax
import jax.numpy as jnp
from jax import lax
from jax.sharding import PartitionSpec as P

GENES = 2048
SLIDES = 4
HIGH = lax.Precision.HIGH
HIGHEST = lax.Precision.HIGHEST


def after(value, *others):
    return lax.optimization_barrier((value, *others))[0]


def dot(a, b, dims, precision=HIGH):
    return lax.dot_general(
        a, b, ((dims[0], dims[1]), ((), ())), precision=precision, preferred_element_type=jnp.float32
    )


def shards(logits, expression, spatial, density, gene_mask, gene_counts, slide_ids):
    n_blk = lax.axis_size("blk")
    n_gene = lax.axis_size("gene")
    me = lax.axis_index("blk")
    plane = lax.axis_index("gene")
    cells, width = logits.shape
    rows = expression.shape[0]
    spots = width * n_blk

    def swap(x, m):
        return lax.ppermute(x, "blk", [(i, i ^ m) for i in range(n_blk)])

    def across(x, m):
        return lax.ppermute(x, "gene", [(i, i ^ m) for i in range(n_gene)])

    def sum_gene(x):
        return x + sum(across(x, m) for m in range(1, n_gene))

    def sum_blk(x):
        m = 1
        while m < n_blk:
            x = x + swap(x, m)
            m *= 2
        return x

    def block(x, m):
        return lax.dynamic_slice_in_dim(x, (me ^ m) * rows, rows, 0)

    far = sorted(range(2, n_blk), key=lambda m: (-((m >> 1).bit_count()), m & 1, m))
    held = {0: block(logits, 0)}
    for m in [1, *far]:
        held[m] = swap(block(logits, m), m)

    total = jnp.sum(jnp.exp(logits), axis=0)
    inv = 1.0 / total
    share = jnp.exp(logits) * inv[None, :]
    square = jnp.sum(share * share)
    part_q = jnp.sum(share, axis=1) / spots
    joined = jnp.concatenate([part_q.reshape(-1, 128), jnp.full((8, 128), square)], axis=0)
    joined = sum_blk(joined)
    cell_q = joined[: cells // 128].reshape(cells)
    square = joined[cells // 128, 0]
    target = density / jnp.sum(density)
    kl_term = jnp.sum(target * (jnp.log(target) - jnp.log(cell_q)))
    ratio = target / cell_q / spots
    ratio_sum = jnp.sum(share * ratio[:, None], axis=0)

    weights = (gene_mask * gene_counts[None, :]).astype(jnp.float32)
    onehot = (slide_ids[None, :] == jnp.arange(SLIDES, dtype=jnp.int32)[:, None]).astype(jnp.float32)

    expo = {m: jnp.exp(held[m]) for m in range(n_blk)}
    part = {m: dot(expo[m], expression, ((0,), (0,))) for m in range(n_blk)}
    pred = None
    for m in [0, *[m for m in far if m % 2 == 0]]:
        piece = part[m] + swap(part[m ^ 1], 1)
        piece = piece if m == 0 else swap(piece, m)
        pred = piece if pred is None else pred + piece
    pred = pred * inv[:, None]

    products = jnp.concatenate([pred * spatial, pred * pred, spatial * spatial], axis=1)
    slide_sums = sum_blk(dot(onehot, products, ((1,), (0,)), HIGHEST))
    genes = spatial.shape[1]
    sum_a, sum_b, sum_c = (slide_sums[:, i * genes : (i + 1) * genes] for i in range(3))
    spot_sums = sum_gene(
        jnp.stack(
            [
                jnp.sum(pred * spatial, axis=1),
                jnp.sum(pred * pred, axis=1),
                jnp.sum(spatial * spatial, axis=1),
                jnp.full((width,), jnp.sum(weights)),
            ]
        )
    )
    sum_e, sum_f, sum_h = spot_sums[0], spot_sums[1], spot_sums[2]
    wsum = spot_sums[3, 0]
    inv_g = lax.rsqrt(sum_b * sum_c + 1e-06)
    inv_s = lax.rsqrt(sum_f * sum_h + 1e-06)

    gain = weights / wsum
    grad_a = -gain * inv_g
    grad_b = gain * sum_a * sum_c * inv_g * inv_g * inv_g
    spread = dot(onehot, jnp.concatenate([grad_a, grad_b], axis=1), ((0,), (0,)), HIGHEST)
    dpred = (
        spread[:, :genes] * spatial
        + spread[:, genes:] * pred
        - (inv_s[:, None] * spatial - (sum_e * sum_h * inv_s * inv_s * inv_s)[:, None] * pred) / spots
    )
    scaled = dpred * inv[:, None]
    dot_sums = sum_gene(
        jnp.stack([jnp.sum(pred * dpred, axis=1), jnp.full((width,), jnp.sum(weights * sum_a * inv_g))])
    )
    column = (dot_sums[0] - ratio_sum) * inv

    scalars = sum_blk(
        jnp.concatenate([jnp.full((8, 128), jnp.sum(sum_e * inv_s)), jnp.full((8, 128), jnp.sum(sum_f))], axis=0)
    )
    loss = -dot_sums[1, 0] / wsum - scalars[0, 0] / spots + kl_term
    rms_map = jnp.sqrt(square / (cells * spots))
    rms_pred = jnp.sqrt(scalars[8, 0] / (spots * GENES))

    near = [0, 1, *sorted(range(2, n_blk), key=lambda m: ((m >> 1).bit_count(), m & 1, m))]
    grads = {0: scaled}
    for m in near[1:]:
        grads[m] = swap(scaled, m)
    back = {}
    for m in near:
        d = dot(expression, grads[m], ((1,), (1,)))
        back[m] = d if m == 0 else swap(d, m)
    expr_grad = (
        dot(
            jnp.concatenate([expo[m] for m in near], axis=1),
            jnp.concatenate([grads[m] for m in near], axis=0),
            ((1,), (0,)),
        )
        * cells
    )

    pieces = []
    for m in near:
        cut = 2 if m in (near[0], near[-1]) else 1
        for k in range(cut):
            pieces.append((m, k * (rows // cut), rows // cut))
    hop1, hop2, hop3 = [], [], []
    logit_grad = jnp.zeros((cells, width), jnp.float32)
    is_end = (plane == 0) | (plane == n_gene - 1)
    for c, (m, first, size) in enumerate(pieces):
        own = back[m][first : first + size]
        if n_gene == 4:
            waits = []
            if c >= 2:
                waits.append(hop1[c - 2])
            if c >= 3:
                waits.append(hop2[c - 3])
            if c >= 4:
                waits.append(hop3[c - 4])
            if waits:
                own = after(own, *waits)
            got = lax.ppermute(own, "gene", [(0, 1), (3, 2)])
            hop1.append(got)
            half = own + got
            got = lax.ppermute(half, "gene", [(1, 2), (2, 1)])
            hop2.append(got)
            whole = half + got
            got = lax.ppermute(whole, "gene", [(1, 0), (2, 3)])
            hop3.append(got)
            whole = jnp.where(is_end, got, whole)
        else:
            whole = lax.psum(own, "gene")
        at = (me ^ m) * rows + first
        e = jnp.exp(lax.dynamic_slice_in_dim(logits, at, size, 0))
        r = lax.dynamic_slice_in_dim(ratio, at, size, 0)
        value = e * (whole - r[:, None] * inv[None, :] - column[None, :]) * cells
        logit_grad = lax.dynamic_update_slice_in_dim(logit_grad, value, at, 0)
    return (loss, logit_grad, expr_grad, rms_map, rms_pred)


def solution(mesh):
    placed = (
        P(None, "blk"),
        P("blk", "gene"),
        P("blk", "gene"),
        P(),
        P(None, "gene"),
        P("gene"),
        P("blk"),
    )
    return jax.shard_map(
        shards,
        mesh=mesh,
        in_specs=placed,
        out_specs=(P(), P(None, "blk"), P("blk", "gene"), P(), P()),
        check_vma=False,
    )
```

```python
import functools

import jax
import jax.numpy as jnp
from jax import lax
from jax.experimental import pallas as pl
from jax.experimental.pallas import tpu as pltpu
from jax.sharding import PartitionSpec as P

GENES = 2048
SLIDES = 4
LANES = 128
F32 = jnp.float32
BF16 = jnp.bfloat16
PAIR = [(0, 1), (1, 0), (2, 3), (3, 2)]
MIDDLE = [(1, 2), (2, 1)]
LIMIT = pltpu.CompilerParams(vmem_limit_bytes=40 * 1024 * 1024)


class Order:
    def __init__(self):
        self.last = None

    def __call__(self, step, *inputs, wait=()):
        if self.last is not None or wait:
            gate = [x for x in (self.last, *wait) if x is not None]
            inputs = lax.optimization_barrier((*inputs, *gate))[: len(inputs)]
        out = step(*inputs)
        self.last = out[0] if isinstance(out, (tuple, list)) else out
        return out


def split(x):
    high = x.astype(BF16)
    return high, (x - high.astype(F32)).astype(BF16)


def three(a, b, dims):
    def dot(u, v):
        return lax.dot_general(u, v, (dims, ((), ())), preferred_element_type=F32)

    return dot(a[0], b[0]) + (dot(a[0], b[1]) + dot(a[1], b[0]))


def exact(a, b, dims):
    return lax.dot_general(a, b, (dims, ((), ())), precision=lax.Precision.HIGHEST, preferred_element_type=F32)


def cost(flops, size):
    return pl.CostEstimate(flops=int(flops), bytes_accessed=int(size), transcendentals=0)


def pred_kernel(at_ref, l_ref, x_ref, acc_ref, o_ref):
    @pl.when(pl.program_id(0) == 0)
    def _():
        o_ref[...] = acc_ref[...]

    o_ref[...] += three(split(jnp.exp(l_ref[...])), split(x_ref[...]), ((0,), (0,)))


def pred_part(at, l, x, acc, step):
    count, width = l.shape
    genes = x.shape[1]
    return pl.pallas_call(
        pred_kernel,
        grid_spec=pltpu.PrefetchScalarGridSpec(
            num_scalar_prefetch=1,
            grid=(count // step,),
            in_specs=[
                pl.BlockSpec((step, width), lambda i, at: (i, 0)),
                pl.BlockSpec((step, genes), lambda i, at: (at[0] + i, 0)),
                pl.BlockSpec((width, genes), lambda i, at: (0, 0)),
            ],
            out_specs=pl.BlockSpec((width, genes), lambda i, at: (0, 0)),
        ),
        out_shape=jax.ShapeDtypeStruct((width, genes), F32),
        compiler_params=LIMIT,
        cost_estimate=cost(6 * count * width * genes, 4 * count * (width + genes)),
    )(at, l, x, acc)


def column_of(row):
    return jnp.transpose(jnp.broadcast_to(row, (LANES, row.shape[1])))


def sums_kernel(n_parts, *refs):
    parts, (inv_ref, spatial_ref, ids_ref, weights_ref, pred_ref, slide_ref, spot_ref) = refs[:n_parts], refs[n_parts:]
    pred = parts[0][...]
    for part in parts[1:]:
        pred = pred + part[...]
    spatial = spatial_ref[...]
    genes = pred.shape[1]
    pred = pred * jnp.concatenate([column_of(inv_ref[...])] * (genes // LANES), axis=1)
    pred_ref[...] = pred
    onehot = (lax.broadcasted_iota(jnp.int32, (8, LANES), 0) == ids_ref[...]).astype(F32)
    ones = jnp.ones((8, genes), F32)
    rows = lax.broadcasted_iota(jnp.int32, (8, LANES), 0)
    spot = jnp.where(rows == 3, jnp.sum(weights_ref[...]), 0.0)
    for k, product in enumerate((pred * spatial, pred * pred, spatial * spatial)):
        slide_ref[8 * k : 8 * k + 8, :] = exact(onehot, product, ((1,), (0,)))
        spot = jnp.where(rows == k, exact(ones, product, ((1,), (1,))), spot)
    spot_ref[...] = spot


def pred_sums(parts, inv, spatial, ids, weights):
    width, genes = spatial.shape
    return pl.pallas_call(
        functools.partial(sums_kernel, len(parts)),
        out_shape=(
            jax.ShapeDtypeStruct((width, genes), F32),
            jax.ShapeDtypeStruct((24, genes), F32),
            jax.ShapeDtypeStruct((8, width), F32),
        ),
        compiler_params=LIMIT,
        cost_estimate=cost(10 * width * genes * 48, 4 * width * genes * 6),
    )(*parts, inv, spatial, ids, weights)


def dpred_kernel(spots, slide_ref, spot_ref, pred_ref, spatial_ref, ids_ref, weights_ref, inv_ref, d_ref, own_ref, tot_ref):
    genes = pred_ref.shape[1]
    a, b, c = (slide_ref[8 * k : 8 * k + 8, :] for k in range(3))
    e, f, h, wsum = (spot_ref[k : k + 1, :] for k in range(4))
    wsum = jnp.max(wsum)
    gain = weights_ref[...] / wsum
    inv_g = lax.rsqrt(b * c + 1e-06)
    inv_s = lax.rsqrt(f * h + 1e-06)
    grad_a = -gain * inv_g
    grad_b = gain * a * c * inv_g * inv_g * inv_g
    onehot = (lax.broadcasted_iota(jnp.int32, (8, LANES), 0) == ids_ref[...]).astype(F32)
    wide = functools.partial(jnp.concatenate, axis=1)
    by_spatial = exact(onehot, grad_a, ((0,), (0,))) - wide([column_of(inv_s / spots)] * (genes // LANES))
    by_pred = exact(onehot, grad_b, ((0,), (0,))) + wide(
        [column_of(e * h * inv_s * inv_s * inv_s / spots)] * (genes // LANES)
    )
    pred = pred_ref[...]
    dpred = by_spatial * spatial_ref[...] + by_pred * pred
    inv = inv_ref[...]
    d_ref[...] = dpred * wide([column_of(inv)] * (genes // LANES))
    own_ref[...] = exact(jnp.ones((8, genes), F32), pred * dpred, ((1,), (1,))) * inv
    rows = lax.broadcasted_iota(jnp.int32, (8, LANES), 0)
    tot = jnp.where(rows == 0, jnp.sum(weights_ref[...] * a * inv_g), 0.0)
    tot = jnp.where(rows == 1, jnp.sum(e * inv_s), tot)
    tot_ref[...] = jnp.where(rows == 2, jnp.sum(f), tot)


def dpred_scaled(spots, slide, spot, pred, spatial, ids, weights, inv):
    width, genes = spatial.shape
    return pl.pallas_call(
        functools.partial(dpred_kernel, spots),
        out_shape=(
            jax.ShapeDtypeStruct((width, genes), F32),
            jax.ShapeDtypeStruct((8, width), F32),
            jax.ShapeDtypeStruct((8, width), F32),
        ),
        compiler_params=LIMIT,
        cost_estimate=cost(10 * width * genes * 48, 4 * width * genes * 6),
    )(slide, spot, pred, spatial, ids, weights, inv)


def dmap_kernel(x_ref, d_ref, o_ref):
    o_ref[...] = three(split(x_ref[...]), split(d_ref[...]), ((1,), (1,)))


def dmap_block(x, d, step):
    count, genes = x.shape
    width = d.shape[0]
    return pl.pallas_call(
        dmap_kernel,
        grid=(count // step,),
        in_specs=[
            pl.BlockSpec((step, genes), lambda i: (i, 0)),
            pl.BlockSpec((width, genes), lambda i: (0, 0)),
        ],
        out_specs=pl.BlockSpec((step, width), lambda i: (i, 0)),
        out_shape=jax.ShapeDtypeStruct((count, width), F32),
        compiler_params=LIMIT,
        cost_estimate=cost(6 * count * width * genes, 4 * count * (width + genes)),
    )(x, d)


def egrad_kernel(scale, kinds, plane_ref, *refs):
    n = len(kinds)
    ls, ds, (o_ref, dh_ref, dl_ref) = refs[: sum(kinds)], refs[sum(kinds) : sum(kinds) + n], refs[sum(kinds) + n :]

    @pl.when(pl.program_id(0) == 0)
    def _():
        for k, d in enumerate(ds):
            dh_ref[k * LANES : (k + 1) * LANES, :], dl_ref[k * LANES : (k + 1) * LANES, :] = split(d[...])

    blocks, at = [], 0
    for kind in kinds:
        l = ls[at][...]
        if kind == 2:
            l = jnp.where(plane_ref[0] == pl.program_id(0), l, ls[at + 1][...])
        at += kind
        blocks.append(jnp.exp(l))
    e = split(jnp.concatenate(blocks, axis=1))
    o_ref[...] = three(e, (dh_ref[...], dl_ref[...]), ((1,), (0,))) * scale


def egrad_part(plane, held, grads, rows, scale):
    half = rows // 2
    width, genes = grads[0].shape
    flat, specs, kinds = [], [], []
    for pieces in held:
        kinds.append(len(pieces))
        for piece in pieces:
            flat.append(piece)
            whole = len(pieces) == 1
            specs.append(pl.BlockSpec((half, width), (lambda i, p: (i, 0)) if whole else (lambda i, p: (0, 0))))
    specs += [pl.BlockSpec((width, genes), lambda i, p: (0, 0))] * len(grads)
    deep = width * len(grads)
    return pl.pallas_call(
        functools.partial(egrad_kernel, scale, tuple(kinds)),
        grid_spec=pltpu.PrefetchScalarGridSpec(
            num_scalar_prefetch=1,
            grid=(2,),
            in_specs=specs,
            out_specs=pl.BlockSpec((half, genes), lambda i, p: (i, 0)),
            scratch_shapes=[pltpu.VMEM((deep, genes), BF16), pltpu.VMEM((deep, genes), BF16)],
        ),
        out_shape=jax.ShapeDtypeStruct((rows, genes), F32),
        compiler_params=LIMIT,
        cost_estimate=cost(6 * rows * deep * genes, 4 * rows * (deep + genes)),
    )(plane, *flat, *grads)


def ratio_kernel(l_ref, ratio_ref, inv_ref, o_ref, sum_ref):
    @pl.when(pl.program_id(0) == 0)
    def _():
        sum_ref[...] = jnp.zeros_like(sum_ref)

    first = (lax.broadcasted_iota(jnp.int32, (8, LANES), 0) == 0).astype(F32)
    ratio = jnp.broadcast_to(ratio_ref[0], (8, ratio_ref.shape[2]))
    column = exact(ratio, first, ((0,), (0,)))
    inv = inv_ref[...]
    o_ref[...] = column * inv
    sum_ref[...] += jnp.sum(jnp.exp(l_ref[...]) * column, axis=0, keepdims=True) * (inv * inv)


def ratio_part(logits, ratio, inv, step):
    cells, width = logits.shape
    steps = cells // step
    return pl.pallas_call(
        ratio_kernel,
        grid=(steps,),
        in_specs=[
            pl.BlockSpec((step, width), lambda i: (i, 0)),
            pl.BlockSpec((1, 1, step), lambda i: (i, 0, 0)),
            pl.BlockSpec((1, width), lambda i: (0, 0)),
        ],
        out_specs=(
            pl.BlockSpec((step, width), lambda i: (i, 0)),
            pl.BlockSpec((8, width), lambda i: (0, 0)),
        ),
        out_shape=(
            jax.ShapeDtypeStruct((cells, width), F32),
            jax.ShapeDtypeStruct((8, width), F32),
        ),
        compiler_params=LIMIT,
        cost_estimate=cost(cells * width * 100, 8 * cells * width),
    )(logits, ratio.reshape(steps, 1, step), inv)


def shards(logits, expression, spatial, density, gene_mask, gene_counts, slide_ids):
    n_blk = lax.axis_size("blk")
    n_gene = lax.axis_size("gene")
    me = lax.axis_index("blk")
    plane = lax.axis_index("gene")
    cells, width = logits.shape
    rows, genes = expression.shape
    half = rows // 2
    spots = width * n_blk
    order = Order()

    def swap(x, m):
        return lax.ppermute(x, "blk", [(i, i ^ m) for i in range(n_blk)])

    def across(x, m):
        return lax.ppermute(x, "gene", [(i, i ^ m) for i in range(n_gene)])

    def cut(r, first, size):
        return lax.dynamic_slice_in_dim(logits, (me ^ r) * rows + first, size, 0)

    far = sorted(range(2, n_blk, 2), key=lambda m: (m.bit_count(), m))
    helped = (3, 5, 6, 7) if n_blk == 8 and n_gene == 4 else ()
    side = plane % 2
    zero = jnp.zeros((1,), jnp.int32)
    shift = jnp.reshape(side, (1,)).astype(jnp.int32)

    other = swap(expression, 1)
    sent, held = {}, {}
    for r in helped:
        sent[r] = swap(cut(r, side * half, half), r & ~1)
    for r in range(2, n_blk):
        if r not in helped:
            held[r] = swap(cut(r, 0, rows), r & ~1)
    held[0], held[1] = cut(0, 0, rows), cut(1, 0, rows)

    total = order(lambda l: jnp.sum(jnp.exp(l), axis=0), logits)
    inv = (1.0 / total)[None, :]
    weights = (gene_mask * gene_counts[None, :]).astype(F32)
    weights = jnp.concatenate([weights, jnp.zeros((8 - SLIDES, genes), F32)], axis=0)
    ids = slide_ids[None, :]
    acc = {}
    none = jnp.zeros((width, genes), F32)

    def add_pred(r, l, at=zero):
        x = expression if r % 2 == 0 else other
        acc[r & ~1] = order(
            lambda l, x, s: pred_part(at, l, x, s, min(half, l.shape[0])), l, x, acc.get(r & ~1, none)
        )

    add_pred(0, held[0])
    passed = {}
    for r in helped[:2]:
        passed[r] = across(sent[r], 1)
    for r in helped[:2]:
        add_pred(r, sent[r], shift)

    def statistics(l, inv):
        share = jnp.exp(l) * inv
        part = jnp.sum(share, axis=1) / spots
        return part, jnp.sum(share * share)

    part_q, square = order(statistics, logits, inv)
    add_pred(1, held[1])
    for r in helped[2:]:
        passed[r] = across(sent[r], 1)
    for r in helped[2:]:
        add_pred(r, sent[r], shift)
    for r in helped[:2]:
        add_pred(r, passed[r], 1 - shift)
    for r in range(n_blk - 1, 1, -1):
        if r in held:
            add_pred(r, held[r])
    for r in helped[2:]:
        add_pred(r, passed[r], 1 - shift)

    parts = [acc[0]] + [swap(acc[m], m) for m in far]
    pred, slide, spot = order(
        lambda *a: pred_sums(a[:-4], *a[-4:]), *parts, inv, spatial, ids, weights
    )
    spot = spot + (across(spot, 1) + (across(spot, 2) + across(spot, 3)))
    wide = jnp.concatenate(
        [slide.reshape(-1, LANES), part_q.reshape(-1, LANES), jnp.full((8, LANES), square)], axis=0
    )
    m = 1
    while m < n_blk:
        wide = wide + swap(wide, m)
        m *= 2
    n_slide = 24 * genes // LANES
    slide = wide[:n_slide].reshape(24, genes)
    cell_q = wide[n_slide : n_slide + cells // LANES].reshape(cells)
    square = wide[-1, 0]
    grad, own, tot = order(
        functools.partial(dpred_scaled, spots), slide, spot, pred, spatial, ids, weights, inv
    )
    own = own[:1]

    grads = {0: grad}
    for m in far:
        grads[m] = swap(grad, m)
    back = {}

    def dmap(r):
        x = expression if r % 2 == 0 else other
        d = order(lambda x, d: dmap_block(x, d, half), x, grads[r & ~1])
        back[r] = d if r < 2 else swap(d, r & ~1)

    dmap(0)
    dmap(1)
    target = density / jnp.sum(density)
    ratio = target / cell_q / spots
    kl_term = jnp.sum(target * (jnp.log(target) - jnp.log(cell_q)))

    near = [0, 1] + [r for m in far for r in (m, m + 1)]
    if n_blk == 8:
        near = [0, 1, 2, 4, 3, 5, 6, 7]
    pieces = [(r, k * half) for r in near for k in range(2)]
    count, lag = len(pieces), 3
    mine, part, total_of, mid, got = {}, {}, {}, {}, {}
    is_end = (plane == 0) | (plane == n_gene - 1)
    state = {"grad": jnp.zeros((cells, width), F32)}

    def own_piece(t):
        r, first = pieces[t]
        return back[r][first : first + half]

    def send(t):
        if t >= count + lag:
            return
        if t >= lag:
            total_of[t - lag] = order(lambda s, y: s + y, part[t - lag], mid[t - lag])
        if t < lag:
            mine[t] = order(lambda b, o: b - o, own_piece(t), own)
            buffer = mine[t]
        elif t < count:
            mine[t], buffer = order(
                lambda b, o, s: (b - o, jnp.where(is_end, b - o, s)), own_piece(t), own, total_of[t - lag]
            )
        else:
            buffer = total_of[t - lag]
        got[t] = lax.ppermute(buffer, "gene", PAIR)

    def finish(t):
        r, first = pieces[t]
        at = (me ^ r) * rows + first
        l = lax.dynamic_slice_in_dim(logits, at, half, 0)
        w = lax.dynamic_slice_in_dim(state["ratio"], at, half, 0)

        def last(rx, s, l, w, rs, g):
            value = jnp.exp(l) * (jnp.where(is_end, rx, s) - w + rs) * cells
            return lax.dynamic_update_slice_in_dim(g, value, at, 0)

        state["grad"] = order(last, got[t + lag], total_of[t], l, w, state["ratio_sum"], state["grad"])

    def extra(t):
        if t == 0:
            state["ratio"], ratio_sum = order(
                lambda l, q, i: ratio_part(l, q, i, rows), logits, ratio, inv
            )
            state["ratio_sum"] = ratio_sum[:1]
        if t == 1:
            for r in near[2:4]:
                dmap(r)
        if t == 2:
            for r in near[4:6]:
                dmap(r)
        if t == 4:
            for r in near[6:]:
                dmap(r)
        if t == 6:
            pick = lambda r: (sent[r], passed[r]) if r in helped else (held[r],)
            ms = [0] + far
            gs = [grads[m] for m in ms]
            for odd in (1, 0):
                flat = [p for m in ms for p in pick(m + odd)]
                kinds = [len(pick(m + odd)) for m in ms]

                def part_of(*a):
                    ls, out = list(a[: len(flat)]), []
                    for k in kinds:
                        out.append(tuple(ls[:k]))
                        ls = ls[k:]
                    return egrad_part(shift, out, a[len(flat) :], rows, cells)

                state[odd] = order(part_of, *flat, *gs)
                if odd:
                    state["swapped"] = swap(state[1], 1)
        if t == 8:
            state["expr"] = order(lambda a, b: a + b, state[0], state["swapped"])
        if t == 10:
            x = tot * jnp.array([1.0 / n_blk, 1.0 / n_gene, 1.0 / n_gene, 0, 0, 0, 0, 0], F32)[:, None]
            x = x + across(x, 1)
            state["tot"] = x + across(x, 2)
        if t == 12:
            x = state["tot"]
            m = 1
            while m < n_blk:
                x = x + swap(x, m)
                m *= 2
            state["tot"] = x

    send(0)
    for t in range(count + lag):
        extra(t)
        send(t + 1)
        if t < count:
            part[t] = order(lambda a, b: a + b, mine[t], got[t])
            mid[t] = lax.ppermute(part[t], "gene", MIDDLE)
        if t >= lag:
            finish(t - lag)

    tot = state["tot"]
    loss = -tot[0, 0] / spot[3, 0] - tot[1, 0] / spots + kl_term
    rms_map = jnp.sqrt(square / (cells * spots))
    rms_pred = jnp.sqrt(tot[2, 0] / (spots * GENES))
    return (loss, state["grad"], state["expr"], rms_map, rms_pred)


def solution(mesh):
    placed = (
        P(None, "blk"),
        P("blk", "gene"),
        P("blk", "gene"),
        P(),
        P(None, "gene"),
        P("gene"),
        P("blk"),
    )
    return jax.shard_map(
        shards,
        mesh=mesh,
        in_specs=placed,
        out_specs=(P(), P(None, "blk"), P("blk", "gene"), P(), P()),
        check_vma=False,
    )
```

```python
import functools

import jax
import jax.numpy as jnp
from jax import lax
from jax.experimental import pallas as pl
from jax.experimental.pallas import tpu as pltpu
from jax.sharding import PartitionSpec as P

GENES = 2048
SLIDES = 4
LANES = 128
F32 = jnp.float32
BF16 = jnp.bfloat16
PAIR = [(0, 1), (1, 0), (2, 3), (3, 2)]
MIDDLE = [(1, 2), (2, 1)]


def room(mib):
    return pltpu.CompilerParams(vmem_limit_bytes=mib * 1024 * 1024)


class Order:
    def __init__(self):
        self.last = None

    def __call__(self, step, fresh, const=(), wait=()):
        gate = [*wait] if self.last is None else [self.last, *wait]
        if gate:
            fresh = lax.optimization_barrier((*fresh, *gate))[: len(fresh)]
        out = step(*fresh, *const)
        self.last = out[0] if isinstance(out, (tuple, list)) else out
        return out

    def here(self, x):
        return lax.optimization_barrier((x, self.last))[0]


def split(x):
    high = x.astype(BF16)
    return high, (x - high.astype(F32)).astype(BF16)


def three(a, b, dims):
    def dot(u, v):
        return lax.dot_general(u, v, (dims, ((), ())), preferred_element_type=F32)

    return dot(a[0], b[0]) + (dot(a[0], b[1]) + dot(a[1], b[0]))


def exact(a, b, dims):
    return lax.dot_general(a, b, (dims, ((), ())), precision=lax.Precision.HIGHEST, preferred_element_type=F32)


def cost(flops, size):
    del flops, size
    return pl.CostEstimate(flops=1, bytes_accessed=1, transcendentals=0)


def big(*arrays):
    return sum(x.size for x in arrays) * 4 // 2**20 + 1


VMEM = pl.BlockSpec(memory_space=pltpu.VMEM)
SMEM = pl.BlockSpec(memory_space=pltpu.SMEM)
HBM = pl.BlockSpec(memory_space=pltpu.HBM)


def at_rows(i, step, count=1):
    start = i * step
    return pl.ds(start if isinstance(i, int) else pl.multiple_of(start, 16), step * count)


def cut_kernel(layout, step, at_ref, l_ref, *refs):
    outs, sems = refs[:-1], refs[-1]
    copies = []
    for out, places in zip(outs, layout, strict=True):
        for k, place in enumerate(places):
            copies.append(
                pltpu.make_async_copy(
                    l_ref.at[at_rows(at_ref[place], step)], out.at[at_rows(k, step)], sems.at[len(copies)]
                )
            )
    for copy in copies:
        copy.start()
    for copy in copies:
        copy.wait()


def cut_blocks(layout, step, at, logits):
    width = logits.shape[1]
    count = sum(len(places) for places in layout)
    return pl.pallas_call(
        functools.partial(cut_kernel, layout, step),
        in_specs=[SMEM, VMEM],
        out_specs=(HBM,) * len(layout),
        out_shape=tuple(jax.ShapeDtypeStruct((len(places) * step, width), F32) for places in layout),
        scratch_shapes=[pltpu.SemaphoreType.DMA((count,))],
        name="cut",
        compiler_params=room(big(logits) + 2),
        cost_estimate=cost(0, 8 * count * step * width),
    )(at, logits)


def softmax_kernel(spots, scale, l_ref, inv_ref, cell_ref, o_ref, buffer, sem):
    cells, width = l_ref.shape
    genes = cell_ref.shape[1]
    n_q = cells // genes

    def column(k, total):
        e = jnp.exp(l_ref[at_rows(k, genes), :])
        return total + jnp.sum(e.reshape(genes // 8, 8, width), axis=0)

    total = lax.fori_loop(0, n_q, column, jnp.zeros((8, width), F32))
    inv = 1.0 / jnp.sum(total, axis=0, keepdims=True)
    inv_ref[...] = inv
    ones = jnp.ones((16, width), BF16)

    def row(k, square):
        e = jnp.exp(l_ref[at_rows(k, genes), :])
        share = e * inv
        buffer[at_rows(k, genes), :] = e * scale
        pltpu.make_async_copy(buffer.at[at_rows(k, genes)], o_ref.at[at_rows(k, genes)], sem).start()
        high, low = split(share)
        sums = [lax.dot_general(ones, x, (((1,), (1,)), ((), ())), preferred_element_type=F32) for x in (high, low)]
        cell_ref[pl.ds(k, 1), :] = (sums[0] + sums[1])[0:1, :] * (1.0 / spots)
        return square + jnp.sum((share * share).reshape(genes // 8, 8, width), axis=0)

    square = lax.fori_loop(0, n_q, row, jnp.zeros((8, width), F32))
    cell_ref[n_q:, :] = jnp.full((cell_ref.shape[0] - n_q, genes), jnp.sum(square), F32)
    pltpu.make_async_copy(buffer, o_ref, sem).wait()


def softmax_sums(spots, genes, logits):
    cells, width = logits.shape
    n_cells = -(-(cells // genes + 1) // 8) * 8
    return pl.pallas_call(
        functools.partial(softmax_kernel, spots, float(cells)),
        in_specs=[VMEM],
        out_specs=(VMEM, VMEM, HBM),
        out_shape=(
            jax.ShapeDtypeStruct((1, width), F32),
            jax.ShapeDtypeStruct((n_cells, genes), F32),
            pltpu.HBM((cells, width), F32),
        ),
        scratch_shapes=[pltpu.VMEM((cells, width), F32), pltpu.SemaphoreType.DMA],
        name="softmax",
        compiler_params=room(2 * big(logits) + 4),
        cost_estimate=cost(0, 0),
    )(logits)


def parts_kernel(step, x_ref, high_ref, low_ref, buffer, sems):
    count = x_ref.shape[0] // step

    def copy(k):
        return pltpu.make_async_copy(x_ref.at[at_rows(k, step)], buffer.at[at_rows(k, step)], sems.at[k])

    for k in range(count):
        copy(k).start()
    for k in range(count):
        copy(k).wait()
        high_ref[at_rows(k, step), :], low_ref[at_rows(k, step), :] = split(buffer[at_rows(k, step), :])


def parts_of(x, step):
    return pl.pallas_call(
        functools.partial(parts_kernel, step),
        in_specs=[HBM],
        out_specs=(VMEM, VMEM),
        out_shape=(pltpu.VMEM(x.shape, BF16), pltpu.VMEM(x.shape, BF16)),
        scratch_shapes=[pltpu.VMEM(x.shape, F32), pltpu.SemaphoreType.DMA((x.shape[0] // step,))],
        name="parts",
        compiler_params=room(12),
        cost_estimate=cost(4 * x.size, 8 * x.size),
    )(x)


def pred_kernel(jobs, n_acc, step, tail, at_ref, *refs):
    n_l = 1 + max(job[2] for job in jobs)
    n_given = max(job[1] for job in jobs)
    ls, xs, given, outs = refs[:n_l], refs[n_l : n_l + 4], refs[n_l + 4 :][:n_given], refs[-n_acc:]
    place = lambda at: at_ref[at[0]] if isinstance(at, list) else at
    for k in range(n_acc):
        acc = None
        for _, g, l, l_at, x, x_at, count in [job for job in jobs if job[0] == k]:
            if g:
                acc = given[g - 1][...]
            for c in range(count):
                e = split(jnp.exp(ls[l][at_rows(place(l_at) + c, step), :]))
                rows = at_rows(place(x_at) + c, step)
                term = three(e, (xs[2 * x][rows, :], xs[2 * x + 1][rows, :]), ((0,), (0,)))
                acc = term if acc is None else acc + term
        outs[k][: acc.shape[0], :] = acc
        if tail:
            outs[k][acc.shape[0] :, :] = refs[-n_acc - 1][...]


def pred_sums_of(jobs, n_acc, step, at, ls, xs, given, tail=()):
    width, genes = ls[0].shape[1], xs[0].shape[1]
    steps = sum(job[-1] for job in jobs)
    return pl.pallas_call(
        functools.partial(pred_kernel, jobs, n_acc, step, len(tail)),
        in_specs=[SMEM] + [VMEM] * (len(ls) + len(xs) + len(given) + len(tail)),
        out_specs=(VMEM,) * n_acc,
        out_shape=(jax.ShapeDtypeStruct((width + sum(x.shape[0] for x in tail), genes), F32),) * n_acc,
        name="pred",
        compiler_params=room(16),
        cost_estimate=cost(6 * steps * step * width * genes, 4 * steps * step * (width + genes)),
    )(at, *ls, *xs, *given, *tail)


def weights_of(mask_ref, counts_ref):
    weights = (mask_ref[...] * counts_ref[...]).astype(F32)
    return jnp.concatenate([weights, jnp.zeros((8 - SLIDES, weights.shape[1]), F32)], axis=0)


def column_of(row):
    return jnp.transpose(jnp.broadcast_to(row, (LANES, row.shape[1])))


def sums_kernel(n_parts, *refs):
    parts, (cells_ref, inv_ref, spatial_ref, ids_ref, mask_ref, counts_ref, pred_ref, wide_ref, spot_ref, q_ref) = (
        refs[:n_parts],
        refs[n_parts:],
    )
    spatial = spatial_ref[...]
    pred, q = parts[0][...], cells_ref[...]
    for part in parts[1:]:
        pred = pred + part[: pred.shape[0], :]
        q = q + part[pred.shape[0] :, :]
    q_ref[...] = q
    genes = pred.shape[1]
    pred = pred * jnp.concatenate([column_of(inv_ref[...])] * (genes // LANES), axis=1)
    pred_ref[...] = pred
    onehot = (lax.broadcasted_iota(jnp.int32, (8, LANES), 0) == ids_ref[...]).astype(F32)
    ones = jnp.ones((8, genes), F32)
    rows = lax.broadcasted_iota(jnp.int32, (8, LANES), 0)
    spot = jnp.where(rows == 3, jnp.sum(weights_of(mask_ref, counts_ref)), 0.0)
    for k, product in enumerate((pred * spatial, pred * pred, spatial * spatial)):
        wide_ref[8 * k : 8 * k + 8, :] = exact(onehot, product, ((1,), (0,)))
        spot = jnp.where(rows == k, exact(ones, product, ((1,), (1,))), spot)
    spot_ref[...] = spot


def pred_sums(n_parts, *args):
    parts, (by_cell, inv, spatial, ids, mask, counts) = args[:n_parts], args[n_parts:]
    width, genes = spatial.shape
    return pl.pallas_call(
        functools.partial(sums_kernel, n_parts),
        out_shape=(
            jax.ShapeDtypeStruct((width, genes), F32),
            jax.ShapeDtypeStruct((24, genes), F32),
            jax.ShapeDtypeStruct((8, width), F32),
            jax.ShapeDtypeStruct(by_cell.shape, F32),
        ),
        name="sums",
        compiler_params=room(12),
        cost_estimate=cost(10 * width * genes * 48, 4 * width * genes * 6),
    )(*parts, by_cell, inv, spatial, ids, mask, counts)


def dpred_kernel(spots, share_blk, share_gene, *refs):
    wides, spot, refs = refs[:2], refs[2][...] + refs[3][...], refs[4:]
    pred_ref, spatial_ref, ids_ref, mask_ref, counts_ref, inv_ref, d_ref, tot_ref = refs
    weights = weights_of(mask_ref, counts_ref)
    genes = pred_ref.shape[1]
    a, b, c = (wides[0][8 * k : 8 * k + 8, :] + wides[1][8 * k : 8 * k + 8, :] for k in range(3))
    e, f, h, wsum = (spot[k : k + 1, :] for k in range(4))
    wsum = jnp.max(wsum)
    gain = weights / wsum
    inv_g = lax.rsqrt(b * c + 1e-06)
    inv_s = lax.rsqrt(f * h + 1e-06)
    grad_a = -gain * inv_g
    grad_b = gain * a * c * inv_g * inv_g * inv_g
    onehot = (lax.broadcasted_iota(jnp.int32, (8, LANES), 0) == ids_ref[...]).astype(F32)
    wide = functools.partial(jnp.concatenate, axis=1)
    by_spatial = exact(onehot, grad_a, ((0,), (0,))) - wide([column_of(inv_s / spots)] * (genes // LANES))
    by_pred = exact(onehot, grad_b, ((0,), (0,))) + wide(
        [column_of(e * h * inv_s * inv_s * inv_s / spots)] * (genes // LANES)
    )
    pred = pred_ref[...]
    dpred = by_spatial * spatial_ref[...] + by_pred * pred
    inv = inv_ref[...]
    d_ref[:LANES, :] = dpred * wide([column_of(inv)] * (genes // LANES))
    own = exact(jnp.ones((8, genes), F32), pred * dpred, ((1,), (1,))) * inv
    d_ref[LANES:, :] = wide([own] * (genes // LANES))
    rows = lax.broadcasted_iota(jnp.int32, (8, LANES), 0)
    tot = jnp.where(rows == 0, jnp.sum(weights * a * inv_g) * share_blk, 0.0)
    tot = jnp.where(rows == 1, jnp.sum(e * inv_s) * share_gene, tot)
    tot = jnp.where(rows == 2, jnp.sum(f) * share_gene, tot)
    tot_ref[...] = jnp.where(rows == 3, wsum, tot)


def dpred_scaled(spots, share_blk, share_gene, *args):
    spatial = args[5]
    width, genes = spatial.shape
    return pl.pallas_call(
        functools.partial(dpred_kernel, spots, share_blk, share_gene),
        out_shape=(
            jax.ShapeDtypeStruct((width + 8, genes), F32),
            jax.ShapeDtypeStruct((8, width), F32),
        ),
        name="dpred",
        compiler_params=room(12),
        cost_estimate=cost(10 * width * genes * 48, 4 * width * genes * 6),
    )(*args)


def dmap_kernel(rows, step, n, *refs):
    xs, ds, outs = refs[:4], refs[4 : 4 + n], refs[4 + n :]
    parts = [split(d[:LANES, :]) for d in ds]
    d = tuple(jnp.concatenate([part[i] for part in parts], axis=0) for i in range(2))
    own = jnp.concatenate([d[LANES : LANES + 1, :LANES] for d in ds], axis=1)
    for k, (x, first) in enumerate(rows):
        here = at_rows(first, step)
        value = three((xs[2 * x][here, :], xs[2 * x + 1][here, :]), d, ((1,), (1,))) - own
        for i, out in enumerate(outs):
            out[at_rows(k, step), :] = value[:, i * LANES : (i + 1) * LANES]


def dmap_blocks(rows, step, ds, xs):
    genes = ds[0].shape[1]
    width = ds[0].shape[0] - 8
    return pl.pallas_call(
        functools.partial(dmap_kernel, rows, step, len(ds)),
        in_specs=[VMEM] * (4 + len(ds)),
        out_specs=(VMEM,) * len(ds),
        out_shape=(jax.ShapeDtypeStruct((len(rows) * step, width), F32),) * len(ds),
        name="dmap",
        compiler_params=room(16),
        cost_estimate=cost(0, 0),
    )(*xs, *ds)


def egrad_kernel(scale, ks, step, wheres, n_add, at_ref, *refs):
    n = len(wheres)
    counts = [2 if isinstance(where, tuple) else 1 for where in wheres]
    ls, ds, adds, o_ref = refs[: sum(counts)], refs[sum(counts) : sum(counts) + n], refs[sum(counts) + n : -1], refs[-1]
    parts = [split(d[:LANES, :]) for d in ds]
    d = tuple(jnp.concatenate([part[i] for part in parts], axis=0) for i in range(2))
    for j, k in enumerate(ks):
        es, at = [], 0
        for where, number in zip(wheres, counts, strict=True):
            if number == 2:
                mine, others = (ls[at + i][at_rows(where[i], step), :] for i in range(2))
                l = jnp.where(at_ref[0] == k, mine, others)
            else:
                l = ls[at][at_rows(where + k, step), :]
            at += number
            es.append(jnp.exp(l))
        value = three(split(jnp.concatenate(es, axis=1)), d, ((1,), (0,))) * scale
        o_ref[at_rows(j, step), :] = value + adds[j][...] if n_add else value


def egrad_part(ks, step, wheres, scale, at, ls, ds, adds=()):
    genes = ds[0].shape[1]
    return pl.pallas_call(
        functools.partial(egrad_kernel, scale, ks, step, wheres, len(adds)),
        in_specs=[SMEM] + [VMEM] * (len(ls) + len(ds) + len(adds)),
        out_specs=VMEM,
        out_shape=jax.ShapeDtypeStruct((len(ks) * step, genes), F32),
        name="egrad",
        compiler_params=room(big(*ls, *ds, *adds) + 24),
        cost_estimate=cost(0, 0),
    )(at, *ls, *ds, *adds)


def ratio_kernel(spots, lo, hi, block, scale, *refs):
    more = lo > 0
    cell_ref, density_ref, inv_ref, a_ref = refs[:4]
    b_ref, given_ref = refs[4:6] if more else (None, None)
    _, o_ref, sum_ref, kl_ref, a, b, sems = refs[-7:]
    inv = inv_ref[...]
    width = a_ref.shape[1]
    n_q, genes = density_ref.shape
    step = block * genes

    def load(k):
        return pltpu.make_async_copy(a_ref.at[at_rows(lo + k, step)], a.at[at_rows(k, step)], sems.at[k])

    def store(k):
        return pltpu.make_async_copy(b.at[at_rows(k, step)], o_ref.at[at_rows(lo + k, step)], sems.at[hi - lo + k])

    for k in range(hi - lo):
        load(k).start()
    density = density_ref[...]
    target = density / jnp.sum(density)
    q = cell_ref[:n_q, :]
    ratios = target / q / spots
    kl_ref[...] = jnp.full(kl_ref.shape, jnp.sum(target * (jnp.log(target) - jnp.log(q))))
    rows = lax.broadcasted_iota(jnp.int32, (16, genes), 0)
    ones = (lax.broadcasted_iota(jnp.int32, (16, LANES), 0) < 3).astype(BF16)
    total = jnp.zeros((8, width), F32)
    for k in range(hi - lo):
        load(k).wait()
        for i in range(block):
            ratio = ratios[(lo + k) * block + i : (lo + k) * block + i + 1, :]
            high = ratio.astype(BF16).astype(F32)
            mid = (ratio - high).astype(BF16).astype(F32)
            terms = jnp.where(rows == 0, high, jnp.where(rows == 1, mid, jnp.where(rows == 2, ratio - high - mid, 0.0)))
            column = lax.dot_general(terms.astype(BF16), ones, (((0,), (0,)), ((), ())), preferred_element_type=F32)
            here = at_rows(k * block + i, genes)
            product = a[here, :] * column
            total = total + jnp.sum(product.reshape(genes // 8, 8, width), axis=0)
            b[here, :] = -product * inv
        store(k).start()
    total = jnp.sum(total, axis=0, keepdims=True) * (inv * inv * (1.0 / scale))
    sum_ref[...] = jnp.broadcast_to(total, sum_ref.shape) + (given_ref[...] if more else 0.0)
    for k in range(hi - lo):
        store(k).wait()


def ratio_part(spots, lo, hi, block, by_cell, density, inv, a, b=None, given=None):
    cells, width = a.shape
    genes = density.shape[1]
    size = (hi - lo) * block * genes
    more = () if b is None else (b, given)
    return pl.pallas_call(
        functools.partial(ratio_kernel, spots, lo, hi, block, float(cells)),
        in_specs=[VMEM, VMEM, VMEM, HBM] + [HBM, VMEM][: len(more)],
        out_specs=(HBM, HBM, VMEM, VMEM),
        out_shape=(
            pltpu.HBM((cells, width), F32),
            pltpu.HBM((cells, width), F32),
            jax.ShapeDtypeStruct((8, width), F32),
            jax.ShapeDtypeStruct((8, width), F32),
        ),
        scratch_shapes=[pltpu.VMEM((size, width), F32)] * 2 + [pltpu.SemaphoreType.DMA((2 * (hi - lo),))],
        input_output_aliases={3: 0, 4: 1} if more else {3: 0},
        name="ratio",
        compiler_params=room(2 * (size * width * 4 // 2**20 + 1) + 6),
        cost_estimate=cost(0, 0),
    )(by_cell, density, inv, a, *more)


def join_kernel(a_ref, b_ref, o_ref):
    half = a_ref.shape[0]
    o_ref[:half, :] = a_ref[...]
    o_ref[half:, :] = b_ref[...]


def join(a, b):
    return pl.pallas_call(
        join_kernel,
        in_specs=[VMEM, VMEM],
        out_specs=VMEM,
        out_shape=jax.ShapeDtypeStruct((2 * a.shape[0], a.shape[1]), F32),
        name="join",
        compiler_params=room(8),
        cost_estimate=cost(0, 0),
    )(a, b)


def add_kernel(first, a_ref, b_ref, o_ref):
    o_ref[...] = a_ref[pl.ds(first, o_ref.shape[0]), :] + b_ref[...]


def add(first, a, b):
    return pl.pallas_call(
        functools.partial(add_kernel, first),
        in_specs=[VMEM, VMEM],
        out_specs=VMEM,
        out_shape=jax.ShapeDtypeStruct(b.shape, F32),
        name="add",
        compiler_params=room(8),
        cost_estimate=cost(0, 0),
    )(a, b)


def add_all_kernel(*refs):
    total = refs[0][...]
    for ref in refs[1:-1]:
        total = total + ref[...]
    refs[-1][...] = total


def add_all(*arrays):
    return pl.pallas_call(
        add_all_kernel,
        in_specs=[VMEM] * len(arrays),
        out_specs=VMEM,
        out_shape=jax.ShapeDtypeStruct(arrays[0].shape, F32),
        name="add_all",
        compiler_params=room(8),
        cost_estimate=cost(0, 0),
    )(*arrays)


def next_kernel(first, at_ref, s_ref, y_ref, b_ref, t_ref, o_ref):
    total = s_ref[...] + y_ref[...]
    t_ref[...] = total
    o_ref[...] = jnp.where(at_ref[0] == 1, b_ref[pl.ds(first, o_ref.shape[0]), :], total)


def next_piece(first, end, s, y, b):
    return pl.pallas_call(
        functools.partial(next_kernel, first),
        in_specs=[SMEM, VMEM, VMEM, VMEM],
        out_specs=(VMEM, VMEM),
        out_shape=(jax.ShapeDtypeStruct(s.shape, F32), jax.ShapeDtypeStruct(s.shape, F32)),
        name="next",
        compiler_params=room(8),
        cost_estimate=cost(0, 0),
    )(end, s, y, b)


def final_kernel(place, n, end_ref, at_ref, *refs):
    rxs, ss, (sum_ref, a_ref, g_ref, _, o_ref, a, b, sems) = refs[:n], refs[n : 2 * n], refs[2 * n :]
    step = a.shape[0] // n
    here = at_rows(at_ref[place], step, n)
    loads = [
        pltpu.make_async_copy(a_ref.at[here], a, sems.at[0]),
        pltpu.make_async_copy(g_ref.at[here], b, sems.at[1]),
    ]
    for load in loads:
        load.start()
    for load in loads:
        load.wait()
    stores = []
    for k in range(n):
        there, rows = at_rows(at_ref[place] + k, step), at_rows(k, step)
        whole = jnp.where(end_ref[0] == 1, rxs[k][...], ss[k][...])
        b[rows, :] = a[rows, :] * (whole + sum_ref[0:1, :]) + b[rows, :]
        stores.append(pltpu.make_async_copy(b.at[rows], o_ref.at[there], sems.at[2 + k]))
        stores[-1].start()
    for store in stores:
        store.wait()


def final_pieces(place, end, at, rxs, ss, ratio_sum, a, grad):
    step, width = ss[0].shape
    n = len(ss)
    return pl.pallas_call(
        functools.partial(final_kernel, place, n),
        in_specs=[SMEM, SMEM] + [VMEM] * (2 * n + 1) + [HBM, HBM],
        out_specs=(HBM, HBM),
        out_shape=(pltpu.HBM(a.shape, F32), pltpu.HBM(grad.shape, F32)),
        scratch_shapes=[pltpu.VMEM((n * step, width), F32)] * 2 + [pltpu.SemaphoreType.DMA((2 + n,))],
        input_output_aliases={3 + 2 * n: 0, 4 + 2 * n: 1},
        name="final",
        compiler_params=room(8),
        cost_estimate=cost(0, 0),
    )(end, at, *rxs, *ss, ratio_sum, a, grad)


def shards(logits, expression, spatial, density, gene_mask, gene_counts, slide_ids):
    n_blk = lax.axis_size("blk")
    n_gene = lax.axis_size("gene")
    me = lax.axis_index("blk")
    plane = lax.axis_index("gene")
    cells, width = logits.shape
    rows, genes = expression.shape
    half = rows // 2
    spots = width * n_blk
    order = Order()

    def swap(x, m):
        return lax.ppermute(x, "blk", [(i, i ^ m) for i in range(n_blk)])

    def across(x, m):
        return lax.ppermute(x, "gene", [(i, i ^ m) for i in range(n_gene)])

    def cut(l, r, first, size):
        return lax.dynamic_slice_in_dim(l, (me ^ r) * rows + first, size, 0)

    far = sorted(range(2, n_blk, 2), key=lambda m: (m.bit_count(), m))
    side = plane % 2
    at = jnp.stack([side, 1 - side, *[(me ^ r) * 2 + k for r in range(n_blk) for k in range(2)]]
        + [(me ^ r) * 2 + side for r in range(n_blk)]).astype(jnp.int32)

    def whole(r):
        return (2 + 2 * r, 3 + 2 * r)

    def mine(r):
        return (2 + 2 * n_blk + r,)

    sent, passed, held = {}, {}, {}

    other = swap(expression, 1)
    constants = (slide_ids[None, :], gene_mask, gene_counts[None, :])
    n_q = cells // genes

    def add_pred(jobs, n_acc, ls, given=(), tail=()):
        n, g = len(ls), len(given)

        def run(*a):
            return pred_sums_of(jobs, n_acc, half, at, a[:n], a[n + g : n + g + 4], a[n : n + g], a[n + g + 4 :])

        return order(run, (*ls, *given), (*own_x, *other_x, *tail))

    def cuts(*layout):
        return order(lambda l: cut_blocks(layout, half, at, l), (logits,))

    if n_blk == 8 and n_gene == 4:
        near3, near5 = cuts(mine(3), mine(5))
        sent[3], sent[5] = swap(near3, 2), swap(near5, 4)
        own_x = order(lambda x: parts_of(x, half), (expression,))
        both, near2, near4, stay = cuts(mine(6) + mine(7), whole(2), whole(4), whole(0) + whole(1))
        passed[3] = across(order(join, (sent[3], sent[5])), 1)
        sent[6], sent[2], sent[4] = swap(order.here(both), 6), swap(order.here(near2), 2), swap(order.here(near4), 4)
        inv, by_cell, scale = order(functools.partial(softmax_sums, spots, genes), (logits,))
        other_x = order(lambda x: parts_of(x, half), (other,))
        by_cell = order(functools.partial(add, 0), (by_cell, swap(by_cell, 1)))
        (acc0,) = add_pred(((0, 0, 0, 0, 0, 0, 2), (0, 0, 0, 2, 1, 0, 2)), 1, (stay,))
        acc2, acc4 = add_pred(((0, 0, 0, 0, 1, [0], 1), (1, 0, 1, 0, 1, [0], 1)), 2, (sent[3], sent[5]))
        passed[6] = across(order.here(sent[6]), 1)
        (acc6,) = add_pred(((0, 0, 0, 0, 0, [0], 1), (0, 0, 0, 1, 1, [0], 1)), 1, (sent[6],))
        acc2, acc4 = add_pred(
            ((0, 1, 0, 0, 1, [1], 1), (1, 2, 0, 1, 1, [1], 1)), 2, (passed[3],), (acc2, acc4)
        )
        (acc2,) = add_pred(((0, 1, 0, 0, 0, 0, 2),), 1, (sent[2],), (acc2,), (by_cell,))
        moved = {2: swap(acc2, 2)}
        (acc4,) = add_pred(((0, 1, 0, 0, 0, 0, 2),), 1, (sent[4],), (acc4,), (by_cell,))
        moved[4] = swap(acc4, 4)
        (acc6,) = add_pred(((0, 1, 0, 0, 0, [1], 1), (0, 0, 0, 1, 1, [1], 1)), 1, (passed[6],), (acc6,), (by_cell,))
        moved[6] = swap(acc6, 6)
        held = {
            2: ((sent[2],), 0),
            3: ((sent[3], passed[3]), (0, 0)),
            4: ((sent[4],), 0),
            5: ((sent[5], passed[3]), (0, 1)),
            6: ((sent[6], passed[6]), (0, 0)),
            7: ((sent[6], passed[6]), (1, 1)),
        }
    else:
        inv, by_cell, scale = order(functools.partial(softmax_sums, spots, genes), (logits,))
        by_cell = order(functools.partial(add, 0), (by_cell, swap(by_cell, 1)))
        own_x = order(lambda x: parts_of(x, half), (expression,))
        other_x = order(lambda x: parts_of(x, half), (other,))
        (stay,) = cuts(whole(0) + whole(1))
        (acc0,) = add_pred(((0, 0, 0, 0, 0, 0, 2), (0, 0, 0, 2, 1, 0, 2)), 1, (stay,))
        moved = {}
        for m in far:
            blocks = cuts(whole(m), whole(m + 1))
            for r in (m, m + 1):
                sent[r] = swap(blocks[r - m], m)
                held[r] = ((sent[r],), 0)
            (acc,) = add_pred(((0, 0, 0, 0, 0, 0, 2), (0, 0, 1, 0, 1, 0, 2)), 1, (sent[m], sent[m + 1]), (), (by_cell,))
            moved[m] = swap(acc, m)
    held[0], held[1] = ((stay,), 0), ((stay,), 2)

    parts = [acc0] + [moved[m] for m in far]
    pred, wide, spot, by_cell = order(
        functools.partial(pred_sums, len(parts)), parts, (by_cell, inv, spatial, *constants)
    )
    density = density.reshape(n_q, genes)
    blocks = n_q // 2
    state = {"scale": scale}

    def kl_part(lo, hi):
        more = (state["grad"], state["ratio_sum"]) if lo else ()
        state["scale"], state["grad"], state["ratio_sum"], state["kl"] = order(
            functools.partial(ratio_part, spots, lo, hi, 2), (by_cell,), (density, inv, state["scale"], *more)
        )

    spot_moved = across(spot, 1)
    m = 1
    while 2 * m < n_blk:
        wide = order(functools.partial(add, 0), (wide, swap(wide, m)))
        m *= 2
        if m == 2:
            spot = order(add_all, (spot, spot_moved))
            spot_moved = across(spot, 2)
    wide_moved = swap(wide, m)
    grad, tot = order(
        functools.partial(dpred_scaled, spots, 1.0 / n_blk, 1.0 / n_gene),
        (wide, wide_moved, spot, spot_moved),
        (pred, spatial, *constants, inv),
    )
    grads = {0: grad}
    for m in far:
        grads[m] = swap(grad, m)
    back = {}

    def dmap(ms, rows, wait=()):
        outs = order(
            lambda *a: dmap_blocks(rows, half, a[: len(ms)], a[len(ms) :]),
            [grads[m] for m in ms],
            (*own_x, *other_x),
            wait,
        )
        for m, d in zip(ms, outs, strict=True):
            d = swap(d, m) if m else d
            for k, (odd, first) in enumerate(rows):
                back[m + odd, first] = (d, k * half)

    if n_blk == 8:
        places = [(0, 0), (0, 1), (1, 0), (1, 1), (2, 0), (4, 0), (2, 1), (4, 1)]
        places += [(r, k) for r in (3, 5, 6, 7) for k in range(2)]
    else:
        places = [(r, k) for m in [0, *far] for r in (m, m + 1) for k in range(2)]
    count, lag = len(places), 3
    part, total_of, mid, got = {}, {}, {}, {}
    end = jnp.reshape((plane == 0) | (plane == n_gene - 1), (1,)).astype(jnp.int32)

    def send(t):
        if t >= count + lag:
            return
        if t < count:
            block, first = back[places[t]]
        if t < lag:
            buffer = block if block.shape[0] == half else order(lambda b: b[first : first + half], (block,))
        elif t < count:
            total_of[t - lag], buffer = order(
                lambda s, y, b: next_piece(first, end, s, y, b), (part[t - lag], mid[t - lag], block)
            )
        else:
            buffer = total_of[t - lag] = order(functools.partial(add, 0), (part[t - lag], mid[t - lag]))
        got[t] = lax.ppermute(buffer, "gene", PAIR)

    def finish(*ts):
        r, k = places[ts[0]]
        n = len(ts)
        state["scale"], state["grad"] = order(
            lambda *a: final_pieces(2 + 2 * r + k, end, at, a[:n], a[n : 2 * n], *a[2 * n :]),
            (*[got[t + lag] for t in ts], *[total_of[t] for t in ts]),
            (state["ratio_sum"], state["scale"], state["grad"]),
        )

    def expr_part(odd, ks, adds=()):
        ms = [0, *far]
        ls = [l for m in ms for l in held[m + odd][0]]
        wheres = [held[m + odd][1] for m in ms]
        n, m = len(ls), len(adds)
        return order(
            lambda d, *a: egrad_part(ks, half, wheres, float(cells), at, a[m : m + n], (d, *a[m + n :]), a[:m]),
            (grads[0], *adds),
            (*ls, *[grads[m] for m in far]),
        )

    all_rows = ((0, 0), (0, 1), (1, 0), (1, 1))

    def extra(t):
        if t == 0:
            dmap((0,), ((1, 0),))
            dmap((0,), ((1, 1),))
            if n_blk == 8:
                dmap((2, 4), ((0, 0),))
            else:
                for m in far:
                    dmap((m,), all_rows)
        if n_blk == 8:
            if t == 2:
                dmap((2, 4), ((0, 1), (1, 0), (1, 1)), (back[2, 0][0], back[4, 0][0]))
            if t == 6:
                dmap((6,), all_rows, (back[3, 0][0], back[5, 0][0]))
        if 0 <= t < 4:
            kl_part(blocks * t // 4, blocks * (t + 1) // 4)
        for step, (move, m) in enumerate(stages):
            if t == first_stage + 2 * step + 2:
                state["tot"] = order(functools.partial(add, 0), (state.get("tot", tot), state["moving"]))
        for step, (move, m) in enumerate(stages):
            if t == first_stage + 2 * step:
                state["moving"] = move(order.here(state.get("tot", tot)), m)
        if t in (15, 16):
            state["swapped", t] = swap(expr_part(1, (t - 15,)), 1)
        if t == 18:
            state["expr"] = expr_part(0, (0, 1), (state["swapped", 15], state["swapped", 16]))

    stages, m = [(across, 1), (across, 2)], 1
    while m < n_blk:
        stages.append((swap, m))
        m *= 2
    first_stage = 16 - 2 * len(stages)

    def joins(t):
        return t + 1 < count and places[t][0] == places[t + 1][0] and places[t][1] == 0

    ready = []
    dmap((0,), ((0, 0),))
    send(0)
    dmap((0,), ((0, 1),))
    for t in range(count + lag):
        send(t + 1)
        extra(t)
        done = t - lag
        if done > 0:
            ready.append(done - 1)
        while ready and (len(ready) > 1 or places[ready[0]][1] == 0 and not joins(ready[0])):
            n = 2 if joins(ready[0]) else 1
            finish(*ready[:n])
            del ready[:n]
        if t < count:
            block, first = back[places[t]]
            part[t] = order(functools.partial(add, first), (block, got[t]))
            mid[t] = lax.ppermute(part[t], "gene", MIDDLE)
    for t in (*ready, count - 1):
        finish(t)

    sums = state["tot"]
    loss = -sums[0, 0] / tot[3, 0] - sums[1, 0] / spots + state["kl"][0, 0]
    rms_map = jnp.sqrt(by_cell[n_q, 0] / (cells * spots))
    rms_pred = jnp.sqrt(sums[2, 0] / (spots * GENES))
    return (loss, state["grad"], state["expr"], rms_map, rms_pred)


def solution(mesh):
    placed = (
        P(None, "blk"),
        P("blk", "gene"),
        P("blk", "gene"),
        P(),
        P(None, "gene"),
        P("gene"),
        P("blk"),
    )
    return jax.shard_map(
        shards,
        mesh=mesh,
        in_specs=placed,
        out_specs=(P(), P(None, "blk"), P("blk", "gene"), P(), P()),
        check_vma=False,
    )
```

```python
import functools

import jax
import jax.numpy as jnp
from jax import lax
from jax.experimental import pallas as pl
from jax.experimental.pallas import tpu as pltpu
from jax.sharding import PartitionSpec as P

GENES = 2048
SLIDES = 4
LANES = 128
F32 = jnp.float32
BF16 = jnp.bfloat16
PAIR = [(0, 1), (1, 0), (2, 3), (3, 2)]
MIDDLE = [(1, 2), (2, 1)]


def room(mib):
    return pltpu.CompilerParams(vmem_limit_bytes=mib * 1024 * 1024)


class Order:
    def __init__(self):
        self.last = None

    def __call__(self, step, fresh, const=(), wait=()):
        gate = [*wait] if self.last is None else [self.last, *wait]
        if gate:
            fresh = lax.optimization_barrier((*fresh, *gate))[: len(fresh)]
        out = step(*fresh, *const)
        self.last = out[0] if isinstance(out, (tuple, list)) else out
        return out

    def here(self, x):
        return lax.optimization_barrier((x, self.last))[0]


def split(x):
    high = x.astype(BF16)
    return high, (x - high.astype(F32)).astype(BF16)


def three(a, b, dims):
    def dot(u, v):
        return lax.dot_general(u, v, (dims, ((), ())), preferred_element_type=F32)

    return dot(a[0], b[0]) + (dot(a[0], b[1]) + dot(a[1], b[0]))


def exact(a, b, dims):
    return lax.dot_general(a, b, (dims, ((), ())), precision=lax.Precision.HIGHEST, preferred_element_type=F32)


def cost(flops, size):
    del flops, size
    return pl.CostEstimate(flops=1, bytes_accessed=1, transcendentals=0)


def big(*arrays):
    return sum(x.size for x in arrays) * 4 // 2**20 + 1


VMEM = pl.BlockSpec(memory_space=pltpu.VMEM)
SMEM = pl.BlockSpec(memory_space=pltpu.SMEM)
HBM = pl.BlockSpec(memory_space=pltpu.HBM)


def at_rows(i, step, count=1):
    start = i * step
    return pl.ds(start if isinstance(i, int) else pl.multiple_of(start, 16), step * count)


def cut_kernel(layout, step, at_ref, l_ref, *refs):
    outs, sems = refs[:-1], refs[-1]
    copies = []
    for out, places in zip(outs, layout, strict=True):
        for k, place in enumerate(places):
            copies.append(
                pltpu.make_async_copy(
                    l_ref.at[at_rows(at_ref[place], step)], out.at[at_rows(k, step)], sems.at[len(copies)]
                )
            )
    for copy in copies:
        copy.start()
    for copy in copies:
        copy.wait()


def cut_blocks(layout, step, at, logits):
    width = logits.shape[1]
    count = sum(len(places) for places in layout)
    return pl.pallas_call(
        functools.partial(cut_kernel, layout, step),
        in_specs=[SMEM, VMEM],
        out_specs=(HBM,) * len(layout),
        out_shape=tuple(jax.ShapeDtypeStruct((len(places) * step, width), F32) for places in layout),
        scratch_shapes=[pltpu.SemaphoreType.DMA((count,))],
        name="cut",
        compiler_params=room(big(logits) + 2),
        cost_estimate=cost(0, 8 * count * step * width),
    )(at, logits)


def by_cell_rows(ref, count, step):
    genes = ref.shape[1]
    return jnp.concatenate([ref[:count, :], ref[count : 2 * count, : step - genes]], axis=1)


def softmax_kernel(spots, scale, step, l_ref, inv_ref, cell_ref, o_ref, buffer, sem):
    cells, width = l_ref.shape
    genes = cell_ref.shape[1]
    count = cells // step

    def column(k, total):
        e = jnp.exp(l_ref[at_rows(k, step), :])
        return total + jnp.sum(e.reshape(step // 8, 8, width), axis=0)

    total = lax.fori_loop(0, count, column, jnp.zeros((8, width), F32))
    inv = 1.0 / jnp.sum(total, axis=0, keepdims=True)
    inv_ref[...] = inv
    ones = jnp.ones((16, width), BF16)

    def row(k, square):
        e = jnp.exp(l_ref[at_rows(k, step), :])
        share = e * inv
        buffer[at_rows(k, step), :] = e * scale
        pltpu.make_async_copy(buffer.at[at_rows(k, step)], o_ref.at[at_rows(k, step)], sem).start()
        high, low = split(share)
        sums = [lax.dot_general(ones, x, (((1,), (1,)), ((), ())), preferred_element_type=F32) for x in (high, low)]
        sums = (sums[0] + sums[1])[0:1, :] * (1.0 / spots)
        cell_ref[pl.ds(k, 1), :] = sums[:, :genes]
        cell_ref[pl.ds(count + k, 1), : step - genes] = sums[:, genes:]
        return square + jnp.sum((share * share).reshape(step // 8, 8, width), axis=0)

    square = lax.fori_loop(0, count, row, jnp.zeros((8, width), F32))
    cell_ref[count:, step - genes :] = jnp.full((count, 2 * genes - step), jnp.sum(square), F32)
    pltpu.make_async_copy(buffer, o_ref, sem).wait()


def softmax_sums(spots, genes, step, logits):
    cells, width = logits.shape
    return pl.pallas_call(
        functools.partial(softmax_kernel, spots, float(cells), step),
        in_specs=[VMEM],
        out_specs=(VMEM, VMEM, HBM),
        out_shape=(
            jax.ShapeDtypeStruct((1, width), F32),
            jax.ShapeDtypeStruct((2 * cells // step, genes), F32),
            pltpu.HBM((cells, width), F32),
        ),
        scratch_shapes=[pltpu.VMEM((cells, width), F32), pltpu.SemaphoreType.DMA],
        name="softmax",
        compiler_params=room(2 * big(logits) + 4),
        cost_estimate=cost(0, 0),
    )(logits)


def parts_kernel(step, x_ref, high_ref, low_ref, buffer, sems):
    count = x_ref.shape[0] // step

    def copy(k):
        return pltpu.make_async_copy(x_ref.at[at_rows(k, step)], buffer.at[at_rows(k, step)], sems.at[k])

    for k in range(count):
        copy(k).start()
    for k in range(count):
        copy(k).wait()
        high_ref[at_rows(k, step), :], low_ref[at_rows(k, step), :] = split(buffer[at_rows(k, step), :])


def parts_of(x, step):
    return pl.pallas_call(
        functools.partial(parts_kernel, step),
        in_specs=[HBM],
        out_specs=(VMEM, VMEM),
        out_shape=(pltpu.VMEM(x.shape, BF16), pltpu.VMEM(x.shape, BF16)),
        scratch_shapes=[pltpu.VMEM(x.shape, F32), pltpu.SemaphoreType.DMA((x.shape[0] // step,))],
        name="parts",
        compiler_params=room(12),
        cost_estimate=cost(4 * x.size, 8 * x.size),
    )(x)


def pred_kernel(jobs, n_acc, step, tail, at_ref, *refs):
    n_l = 1 + max(job[2] for job in jobs)
    n_given = max(job[1] for job in jobs)
    ls, xs, given, outs = refs[:n_l], refs[n_l : n_l + 4], refs[n_l + 4 :][:n_given], refs[-n_acc:]
    place = lambda at: at_ref[at[0]] if isinstance(at, list) else at
    for k in range(n_acc):
        acc = None
        for _, g, l, l_at, x, x_at, count in [job for job in jobs if job[0] == k]:
            if g:
                acc = given[g - 1][...]
            for c in range(count):
                e = split(jnp.exp(ls[l][at_rows(place(l_at) + c, step), :]))
                rows = at_rows(place(x_at) + c, step)
                term = three(e, (xs[2 * x][rows, :], xs[2 * x + 1][rows, :]), ((0,), (0,)))
                acc = term if acc is None else acc + term
        outs[k][: acc.shape[0], :] = acc
        if tail:
            outs[k][acc.shape[0] :, :] = refs[-n_acc - 1][...]


def pred_sums_of(jobs, n_acc, step, at, ls, xs, given, tail=()):
    width, genes = ls[0].shape[1], xs[0].shape[1]
    steps = sum(job[-1] for job in jobs)
    return pl.pallas_call(
        functools.partial(pred_kernel, jobs, n_acc, step, len(tail)),
        in_specs=[SMEM] + [VMEM] * (len(ls) + len(xs) + len(given) + len(tail)),
        out_specs=(VMEM,) * n_acc,
        out_shape=(jax.ShapeDtypeStruct((width + sum(x.shape[0] for x in tail), genes), F32),) * n_acc,
        name="pred",
        compiler_params=room(16),
        cost_estimate=cost(6 * steps * step * width * genes, 4 * steps * step * (width + genes)),
    )(at, *ls, *xs, *given, *tail)


def weights_of(mask_ref, counts_ref):
    weights = (mask_ref[...] * counts_ref[...]).astype(F32)
    return jnp.concatenate([weights, jnp.zeros((8 - SLIDES, weights.shape[1]), F32)], axis=0)


def column_of(row):
    return jnp.transpose(jnp.broadcast_to(row, (LANES, row.shape[1])))


def sums_kernel(n_parts, *refs):
    parts, (cells_ref, inv_ref, spatial_ref, ids_ref, mask_ref, counts_ref, pred_ref, wide_ref, spot_ref, q_ref) = (
        refs[:n_parts],
        refs[n_parts:],
    )
    spatial = spatial_ref[...]
    pred, q = parts[0][...], cells_ref[...]
    for part in parts[1:]:
        pred = pred + part[: pred.shape[0], :]
        q = q + part[pred.shape[0] :, :]
    q_ref[...] = q
    genes = pred.shape[1]
    pred = pred * jnp.concatenate([column_of(inv_ref[...])] * (genes // LANES), axis=1)
    pred_ref[...] = pred
    onehot = (lax.broadcasted_iota(jnp.int32, (8, LANES), 0) == ids_ref[...]).astype(F32)
    ones = jnp.ones((8, genes), F32)
    rows = lax.broadcasted_iota(jnp.int32, (8, LANES), 0)
    spot = jnp.where(rows == 3, jnp.sum(weights_of(mask_ref, counts_ref)), 0.0)
    for k, product in enumerate((pred * spatial, pred * pred, spatial * spatial)):
        wide_ref[8 * k : 8 * k + 8, :] = exact(onehot, product, ((1,), (0,)))
        spot = jnp.where(rows == k, exact(ones, product, ((1,), (1,))), spot)
    spot_ref[...] = spot


def pred_sums(n_parts, *args):
    parts, (by_cell, inv, spatial, ids, mask, counts) = args[:n_parts], args[n_parts:]
    width, genes = spatial.shape
    return pl.pallas_call(
        functools.partial(sums_kernel, n_parts),
        out_shape=(
            jax.ShapeDtypeStruct((width, genes), F32),
            jax.ShapeDtypeStruct((24, genes), F32),
            jax.ShapeDtypeStruct((8, width), F32),
            jax.ShapeDtypeStruct(by_cell.shape, F32),
        ),
        name="sums",
        compiler_params=room(12),
        cost_estimate=cost(10 * width * genes * 48, 4 * width * genes * 6),
    )(*parts, by_cell, inv, spatial, ids, mask, counts)


def dpred_kernel(spots, share_gene, *refs):
    wides, spot, refs = refs[:2], refs[2][...] + refs[3][...], refs[4:]
    pred_ref, spatial_ref, ids_ref, mask_ref, counts_ref, inv_ref, d_ref, tot_ref = refs
    weights = weights_of(mask_ref, counts_ref)
    genes = pred_ref.shape[1]
    a, b, c = (wides[0][8 * k : 8 * k + 8, :] + wides[1][8 * k : 8 * k + 8, :] for k in range(3))
    e, f, h, wsum = (spot[k : k + 1, :] for k in range(4))
    wsum = jnp.max(wsum)
    gain = weights / wsum
    inv_g = lax.rsqrt(b * c + 1e-06)
    inv_s = lax.rsqrt(f * h + 1e-06)
    grad_a = -gain * inv_g
    grad_b = gain * a * c * inv_g * inv_g * inv_g
    onehot = (lax.broadcasted_iota(jnp.int32, (8, LANES), 0) == ids_ref[...]).astype(F32)
    wide = functools.partial(jnp.concatenate, axis=1)
    by_spatial = exact(onehot, grad_a, ((0,), (0,))) - wide([column_of(inv_s / spots)] * (genes // LANES))
    by_pred = exact(onehot, grad_b, ((0,), (0,))) + wide(
        [column_of(e * h * inv_s * inv_s * inv_s / spots)] * (genes // LANES)
    )
    pred = pred_ref[...]
    dpred = by_spatial * spatial_ref[...] + by_pred * pred
    inv = inv_ref[...]
    d_ref[:LANES, :] = dpred * wide([column_of(inv)] * (genes // LANES))
    own = exact(jnp.ones((8, genes), F32), pred * dpred, ((1,), (1,))) * inv
    d_ref[LANES:, :] = wide([own] * (genes // LANES))
    rows = lax.broadcasted_iota(jnp.int32, (8, LANES), 0)
    tot = jnp.where(rows == 0, jnp.sum(weights * a * inv_g), 0.0)
    tot = jnp.where(rows == 1, jnp.sum(e * inv_s), tot)
    tot = jnp.where(rows == 2, jnp.sum(f), tot)
    tot_ref[...] = jnp.where(rows == 3, wsum * share_gene, tot)


def dpred_scaled(spots, share_gene, *args):
    spatial = args[5]
    width, genes = spatial.shape
    return pl.pallas_call(
        functools.partial(dpred_kernel, spots, share_gene),
        out_shape=(
            jax.ShapeDtypeStruct((width + 8, genes), F32),
            jax.ShapeDtypeStruct((8, width), F32),
        ),
        name="dpred",
        compiler_params=room(12),
        cost_estimate=cost(10 * width * genes * 48, 4 * width * genes * 6),
    )(*args)


def dmap_kernel(rows, step, n, *refs):
    xs, ds, outs = refs[:4], refs[4 : 4 + n], refs[-n:]
    parts = [split(d[:LANES, :]) for d in ds]
    d = tuple(jnp.concatenate([part[i] for part in parts], axis=0) for i in range(2))
    own = jnp.concatenate([d[LANES : LANES + 1, :LANES] for d in ds], axis=1)
    for k, (x, first) in enumerate(rows):
        here = at_rows(first, step)
        value = three((xs[2 * x][here, :], xs[2 * x + 1][here, :]), d, ((1,), (1,))) - own
        for i, out in enumerate(outs):
            out[at_rows(k, step), :] = value[:, i * LANES : (i + 1) * LANES]
    if len(refs) > 4 + 2 * n:
        for out in outs:
            out[len(rows) * step :, :] = refs[4 + n][...]


def dmap_blocks(rows, step, ds, xs, tail=()):
    genes = ds[0].shape[1]
    width = ds[0].shape[0] - 8
    return pl.pallas_call(
        functools.partial(dmap_kernel, rows, step, len(ds)),
        in_specs=[VMEM] * (4 + len(ds) + len(tail)),
        out_specs=(VMEM,) * len(ds),
        out_shape=(jax.ShapeDtypeStruct((len(rows) * step + 8 * len(tail), width), F32),) * len(ds),
        name="dmap",
        compiler_params=room(16),
        cost_estimate=cost(0, 0),
    )(*xs, *ds, *tail)


def egrad_kernel(scale, ks, step, wheres, n_add, at_ref, *refs):
    n = len(wheres)
    counts = [2 if isinstance(where, tuple) else 1 for where in wheres]
    ls, ds, adds, o_ref = refs[: sum(counts)], refs[sum(counts) : sum(counts) + n], refs[sum(counts) + n : -1], refs[-1]
    parts = [split(d[:LANES, :]) for d in ds]
    d = tuple(jnp.concatenate([part[i] for part in parts], axis=0) for i in range(2))
    for j, k in enumerate(ks):
        es, at = [], 0
        for where, number in zip(wheres, counts, strict=True):
            if number == 2:
                mine, others = (ls[at + i][at_rows(where[i], step), :] for i in range(2))
                l = jnp.where(at_ref[0] == k, mine, others)
            else:
                l = ls[at][at_rows(where + k, step), :]
            at += number
            es.append(jnp.exp(l))
        value = three(split(jnp.concatenate(es, axis=1)), d, ((1,), (0,))) * scale
        o_ref[at_rows(j, step), :] = value + adds[j][...] if n_add else value


def egrad_part(ks, step, wheres, scale, at, ls, ds, adds=()):
    genes = ds[0].shape[1]
    return pl.pallas_call(
        functools.partial(egrad_kernel, scale, ks, step, wheres, len(adds)),
        in_specs=[SMEM] + [VMEM] * (len(ls) + len(ds) + len(adds)),
        out_specs=VMEM,
        out_shape=jax.ShapeDtypeStruct((len(ks) * step, genes), F32),
        name="egrad",
        compiler_params=room(big(*ls, *ds, *adds) + 24),
        cost_estimate=cost(0, 0),
    )(at, *ls, *ds, *adds)


def ratio_kernel(spots, scale, cell_ref, density_ref, inv_ref, a_ref, _, ratio_ref, sum_ref, kl_ref, a, sems):
    inv = inv_ref[...]
    count, step = density_ref.shape

    def load(k):
        return pltpu.make_async_copy(a_ref.at[at_rows(k, step)], a.at[at_rows(k, step)], sems.at[k])

    for k in range(count):
        load(k).start()
    density = density_ref[...]
    target = density / jnp.sum(density)
    q = by_cell_rows(cell_ref, count, step)
    ratios = target / q / spots
    ratio_ref[...] = ratios
    kl_ref[...] = jnp.full(kl_ref.shape, jnp.sum(target * (jnp.log(target) - jnp.log(q))))
    rows = lax.broadcasted_iota(jnp.int32, (16, step), 0)
    total = jnp.zeros((1, LANES), F32)
    for k in range(count):
        load(k).wait()
        high, low = split(ratios[k : k + 1, :])
        lhs = jnp.where(rows == 0, high.astype(F32), jnp.where(rows == 1, low.astype(F32), 0.0)).astype(BF16)
        for part in split(a[at_rows(k, step), :]):
            sums = lax.dot_general(lhs, part, (((1,), (0,)), ((), ())), preferred_element_type=F32)
            total = total + (sums[0:1, :] + sums[1:2, :])
    sum_ref[...] = jnp.broadcast_to(total * (inv * inv * (1.0 / scale)), sum_ref.shape)


def ratio_part(spots, by_cell, density, inv, a):
    cells, width = a.shape
    return pl.pallas_call(
        functools.partial(ratio_kernel, spots, float(cells)),
        in_specs=[VMEM, VMEM, VMEM, HBM],
        out_specs=(HBM, VMEM, VMEM, VMEM),
        out_shape=(
            pltpu.HBM((cells, width), F32),
            jax.ShapeDtypeStruct(density.shape, F32),
            jax.ShapeDtypeStruct((8, width), F32),
            jax.ShapeDtypeStruct((8, width), F32),
        ),
        scratch_shapes=[pltpu.VMEM((cells, width), F32), pltpu.SemaphoreType.DMA((density.shape[0],))],
        input_output_aliases={3: 0},
        name="ratio",
        compiler_params=room(big(a) + 8),
        cost_estimate=cost(0, 0),
    )(by_cell, density, inv, a)


def join_kernel(a_ref, b_ref, o_ref):
    half = a_ref.shape[0]
    o_ref[:half, :] = a_ref[...]
    o_ref[half:, :] = b_ref[...]


def join(a, b):
    return pl.pallas_call(
        join_kernel,
        in_specs=[VMEM, VMEM],
        out_specs=VMEM,
        out_shape=jax.ShapeDtypeStruct((2 * a.shape[0], a.shape[1]), F32),
        name="join",
        compiler_params=room(8),
        cost_estimate=cost(0, 0),
    )(a, b)


def add_kernel(first, a_ref, b_ref, o_ref):
    o_ref[...] = a_ref[pl.ds(first, o_ref.shape[0]), :] + b_ref[: o_ref.shape[0], :]


def add(first, rows, a, b):
    return pl.pallas_call(
        functools.partial(add_kernel, first),
        in_specs=[VMEM, VMEM],
        out_specs=VMEM,
        out_shape=jax.ShapeDtypeStruct((rows, b.shape[1]), F32),
        name="add",
        compiler_params=room(8),
        cost_estimate=cost(0, 0),
    )(a, b)


def plus(a, b):
    return add(0, a.shape[0], a, b)


def add_all_kernel(*refs):
    total = refs[0][...]
    for ref in refs[1:-1]:
        total = total + ref[...]
    refs[-1][...] = total


def add_all(*arrays):
    return pl.pallas_call(
        add_all_kernel,
        in_specs=[VMEM] * len(arrays),
        out_specs=VMEM,
        out_shape=jax.ShapeDtypeStruct(arrays[0].shape, F32),
        name="add_all",
        compiler_params=room(8),
        cost_estimate=cost(0, 0),
    )(*arrays)


def next_kernel(first, step, end_ref, s_ref, y_ref, b_ref, t_ref, o_ref):
    total = s_ref[...] + y_ref[...]
    t_ref[...] = total
    o_ref[:step, :] = jnp.where(end_ref[0] == 1, b_ref[pl.ds(first, step), :], total[:step, :])
    if total.shape[0] > step:
        o_ref[step:, :] = total[step:, :]


def next_piece(first, step, end, s, y, b):
    return pl.pallas_call(
        functools.partial(next_kernel, first, step),
        in_specs=[SMEM, VMEM, VMEM, VMEM],
        out_specs=(VMEM, VMEM),
        out_shape=(jax.ShapeDtypeStruct(s.shape, F32), jax.ShapeDtypeStruct(s.shape, F32)),
        name="next",
        compiler_params=room(8),
        cost_estimate=cost(0, 0),
    )(end, s, y, b)


def final_kernel(place, n, end_ref, at_ref, *refs):
    rx_ref, s_ref, (ratio_ref, sum_ref, inv_ref, a_ref, _, _, o_ref, a, b, sems) = refs[0], refs[1], refs[2:]
    step = a.shape[0] // n
    here = at_rows(at_ref[place], step, n)
    load = pltpu.make_async_copy(a_ref.at[here], a, sems.at[n])
    load.start()
    rows = lax.broadcasted_iota(jnp.int32, (16, step), 0)
    ones = (lax.broadcasted_iota(jnp.int32, (16, LANES), 0) < 3).astype(BF16)
    stores = []
    for k in range(n):
        at, here = at_ref[place] + k, at_rows(k, step)
        ratio = ratio_ref[pl.ds(at, 1), :]
        high = ratio.astype(BF16).astype(F32)
        mid = (ratio - high).astype(BF16).astype(F32)
        terms = jnp.where(rows == 0, high, jnp.where(rows == 1, mid, jnp.where(rows == 2, ratio - high - mid, 0.0)))
        column = lax.dot_general(terms.astype(BF16), ones, (((0,), (0,)), ((), ())), preferred_element_type=F32)
        whole = jnp.where(end_ref[0] == 1, rx_ref[here, :], s_ref[here, :])
        value = whole + (sum_ref[0:1, :] - column * inv_ref[...])
        if k == 0:
            load.wait()
        b[here, :] = a[here, :] * value
        stores.append(pltpu.make_async_copy(b.at[here], o_ref.at[at_rows(at, step)], sems.at[k]))
        stores[-1].start()
    for store in stores:
        store.wait()


def final_piece(step, n, place, end, at, rx, s, ratio, ratio_sum, inv, a, grad):
    width = s.shape[1]
    return pl.pallas_call(
        functools.partial(final_kernel, place, n),
        in_specs=[SMEM, SMEM] + [VMEM] * 5 + [HBM, HBM],
        out_specs=(HBM, HBM),
        out_shape=(pltpu.HBM(a.shape, F32), pltpu.HBM(grad.shape, F32)),
        scratch_shapes=[pltpu.VMEM((n * step, width), F32)] * 2 + [pltpu.SemaphoreType.DMA((1 + n,))],
        input_output_aliases={7: 0, 8: 1},
        name="final",
        compiler_params=room(10),
        cost_estimate=cost(0, 0),
    )(end, at, rx, s, ratio, ratio_sum, inv, a, grad)


def blank(shape):
    return pl.pallas_call(lambda o_ref: None, out_specs=HBM, out_shape=pltpu.HBM(shape, F32), name="blank")()


def scalars_kernel(n, cells, spots, step, end_ref, *refs):
    sums = [refs[k][-8:, :] for k in range(n)]
    rx_ref, s_ref, q_ref, kl_ref, loss_ref, map_ref, pred_ref = refs[n:]
    while len(sums) > 1:
        sums = [a + b for a, b in zip(sums[::2], sums[1::2], strict=True)]
    by_gene = jnp.where(end_ref[0] == 1, rx_ref[step:, :], s_ref[step:, :])
    cosine, fitted, wsum, scos = by_gene[0:1, :], sums[0][2:3, :], by_gene[3:4, :], sums[0][1:2, :]
    loss = -cosine / wsum - scos / spots + kl_ref[0:1, :]
    rms_map = jnp.sqrt(q_ref[q_ref.shape[0] - 1 :, q_ref.shape[1] - LANES :] / (cells * spots))
    rms_pred = jnp.sqrt(fitted / (spots * GENES))
    for ref, value in zip((loss_ref, map_ref, pred_ref), (loss, rms_map, rms_pred), strict=True):
        ref[0, 0] = jnp.max(value)


def scalar_results(n, cells, spots, step, end, *args):
    return pl.pallas_call(
        functools.partial(scalars_kernel, n, cells, spots, step),
        in_specs=[SMEM] + [VMEM] * len(args),
        out_specs=(SMEM,) * 3,
        out_shape=(jax.ShapeDtypeStruct((1, 1), F32),) * 3,
        name="scalars",
        compiler_params=room(24),
        cost_estimate=cost(0, 0),
    )(end, *args)


def shards(logits, expression, spatial, density, gene_mask, gene_counts, slide_ids):
    n_blk = lax.axis_size("blk")
    n_gene = lax.axis_size("gene")
    me = lax.axis_index("blk")
    plane = lax.axis_index("gene")
    cells, width = logits.shape
    rows, genes = expression.shape
    half = rows // 2
    spots = width * n_blk
    order = Order()

    def swap(x, m):
        return lax.ppermute(x, "blk", [(i, i ^ m) for i in range(n_blk)])

    def across(x, m):
        return lax.ppermute(x, "gene", [(i, i ^ m) for i in range(n_gene)])

    def cut(l, r, first, size):
        return lax.dynamic_slice_in_dim(l, (me ^ r) * rows + first, size, 0)

    far = sorted(range(2, n_blk, 2), key=lambda m: (m.bit_count(), m))
    side = plane % 2
    at = jnp.stack([side, 1 - side, *[(me ^ r) * 2 + k for r in range(n_blk) for k in range(2)]]
        + [(me ^ r) * 2 + side for r in range(n_blk)]).astype(jnp.int32)

    def whole(r):
        return (2 + 2 * r, 3 + 2 * r)

    def mine(r):
        return (2 + 2 * n_blk + r,)

    sent, passed, held = {}, {}, {}

    other = swap(expression, 1)
    constants = (slide_ids[None, :], gene_mask, gene_counts[None, :])
    n_q = cells // genes

    def add_pred(jobs, n_acc, ls, given=(), tail=()):
        n, g = len(ls), len(given)

        def run(*a):
            return pred_sums_of(jobs, n_acc, half, at, a[:n], a[n + g : n + g + 4], a[n : n + g], a[n + g + 4 :])

        return order(run, (*ls, *given), (*own_x, *other_x, *tail))

    def cuts(*layout):
        return order(lambda l: cut_blocks(layout, half, at, l), (logits,))

    if n_blk == 8 and n_gene == 4:
        near3, near5 = order(
            lambda l: [lax.dynamic_slice_in_dim(l, (me ^ r) * rows + side * half, half, 0) for r in (3, 5)], (logits,)
        )
        sent[3], sent[5] = swap(near3, 2), swap(near5, 4)
        own_x = order(lambda x: parts_of(x, half), (expression,))
        both, near2, near4, stay = cuts(mine(6) + mine(7), whole(2), whole(4), whole(0) + whole(1))
        passed[3] = across(order(join, (sent[3], sent[5])), 1)
        sent[6], sent[2], sent[4] = swap(order.here(both), 6), swap(order.here(near2), 2), swap(order.here(near4), 4)
        inv, by_cell, scale = order(functools.partial(softmax_sums, spots, genes, half), (logits,))
        other_x = order(lambda x: parts_of(x, half), (other,))
        (acc0,) = add_pred(((0, 0, 0, 0, 0, 0, 2), (0, 0, 0, 2, 1, 0, 2)), 1, (stay,))
        acc2, acc4 = add_pred(((0, 0, 0, 0, 1, [0], 1), (1, 0, 1, 0, 1, [0], 1)), 2, (sent[3], sent[5]))
        cell_moved = swap(order.here(by_cell), 1)
        passed[6] = across(order.here(sent[6]), 1)
        (acc6,) = add_pred(((0, 0, 0, 0, 0, [0], 1), (0, 0, 0, 1, 1, [0], 1)), 1, (sent[6],))
        acc2, acc4 = add_pred(
            ((0, 1, 0, 0, 1, [1], 1), (1, 2, 0, 1, 1, [1], 1)), 2, (passed[3],), (acc2, acc4)
        )
        by_cell = order(plus, (by_cell, cell_moved))
        (acc2,) = add_pred(((0, 1, 0, 0, 0, 0, 2),), 1, (sent[2],), (acc2,), (by_cell,))
        moved = {2: swap(acc2, 2)}
        (acc4,) = add_pred(((0, 1, 0, 0, 0, 0, 2),), 1, (sent[4],), (acc4,), (by_cell,))
        moved[4] = swap(acc4, 4)
        (acc6,) = add_pred(((0, 1, 0, 0, 0, [1], 1), (0, 0, 0, 1, 1, [1], 1)), 1, (passed[6],), (acc6,), (by_cell,))
        moved[6] = swap(acc6, 6)
        held = {
            2: ((sent[2],), 0),
            3: ((sent[3], passed[3]), (0, 0)),
            4: ((sent[4],), 0),
            5: ((sent[5], passed[3]), (0, 1)),
            6: ((sent[6], passed[6]), (0, 0)),
            7: ((sent[6], passed[6]), (1, 1)),
        }
    else:
        inv, by_cell, scale = order(functools.partial(softmax_sums, spots, genes, half), (logits,))
        by_cell = order(plus, (by_cell, swap(by_cell, 1)))
        own_x = order(lambda x: parts_of(x, half), (expression,))
        other_x = order(lambda x: parts_of(x, half), (other,))
        (stay,) = cuts(whole(0) + whole(1))
        (acc0,) = add_pred(((0, 0, 0, 0, 0, 0, 2), (0, 0, 0, 2, 1, 0, 2)), 1, (stay,))
        moved = {}
        for m in far:
            blocks = cuts(whole(m), whole(m + 1))
            for r in (m, m + 1):
                sent[r] = swap(blocks[r - m], m)
                held[r] = ((sent[r],), 0)
            (acc,) = add_pred(((0, 0, 0, 0, 0, 0, 2), (0, 0, 1, 0, 1, 0, 2)), 1, (sent[m], sent[m + 1]), (), (by_cell,))
            moved[m] = swap(acc, m)
    held[0], held[1] = ((stay,), 0), ((stay,), 2)

    parts = [acc0] + [moved[m] for m in far]
    pred, wide, spot, by_cell = order(
        functools.partial(pred_sums, len(parts)), parts, (by_cell, inv, spatial, *constants)
    )
    density = density.reshape(cells // half, half)
    state = {"scale": scale, "grad": blank((cells, width))}

    spot_moved = across(spot, 1)
    m = 1
    while 2 * m < n_blk:
        wide = order(plus, (wide, swap(wide, m)))
        m *= 2
        if m == 2:
            spot = order(add_all, (spot, spot_moved))
            spot_moved = across(spot, 2)
    wide_moved = swap(wide, m)
    grad, tot = order(
        functools.partial(dpred_scaled, spots, 1.0 / n_gene),
        (wide, wide_moved, spot, spot_moved),
        (pred, spatial, *constants, inv),
    )
    grads, back, tails = {0: grad}, {}, {}
    for m in far:
        grads[m] = swap(grad, m)

    def dmap(ms, steps, wait=(), tail=()):
        outs = order(
            lambda *a: dmap_blocks(steps, half, a[: len(ms)], a[len(ms) : len(ms) + 4], a[len(ms) + 4 :]),
            [grads[m] for m in ms],
            (*own_x, *other_x, *tail),
            wait,
        )
        for m, d in zip(ms, outs, strict=True):
            d = swap(d, m) if m else d
            for k, (odd, first) in enumerate(steps):
                if first == 0:
                    back[m + odd] = (d, k * half)
            if tail:
                tails[m] = d

    own_rows, other_rows = ((0, 0), (0, 1)), ((1, 0), (1, 1))
    places = [0, 1, 2, 4, 3, 5, 6, 7] if n_blk == 8 else [r for m in [0, *far] for r in (m, m + 1)]
    count, lag = len(places), 3
    part, total_of, mid, got = {}, {}, {}, {}
    end = jnp.reshape((plane == 0) | (plane == n_gene - 1), (1,)).astype(jnp.int32)

    def send(t):
        if t >= count + lag:
            return
        if t < count:
            block, first = back[places[t]]
        if t < lag:
            buffer = block if block.shape[0] <= rows + 8 else block[first : first + rows]
        elif t < count:
            total_of[t - lag], buffer = order(
                lambda s, y, b: next_piece(first, rows, end, s, y, b), (part[t - lag], mid[t - lag], block)
            )
        else:
            buffer = total_of[t - lag] = order(plus, (part[t - lag], mid[t - lag]))
        got[t] = lax.ppermute(buffer, "gene", PAIR)

    def finish(t):
        state["scale"], state["grad"] = order(
            functools.partial(final_piece, half, 2, 2 + 2 * places[t], end, at),
            (got[t + lag], total_of[t]),
            (state["ratio"], state["ratio_sum"], inv, state["scale"], state["grad"]),
        )

    def expr_part(odd, ks, adds=()):
        ms = [0, *far]
        ls = [l for m in ms for l in held[m + odd][0]]
        wheres = [held[m + odd][1] for m in ms]
        n, m = len(ls), len(adds)
        return order(
            lambda d, *a: egrad_part(ks, half, wheres, float(cells), at, a[m : m + n], (d, *a[m + n :]), a[:m]),
            (grads[0], *adds),
            (*ls, *[grads[m] for m in far]),
        )

    def extra(t):
        if t == 0:
            tails[0] = order(plus, (tot, tot_moved))
            if n_blk == 8:
                dmap((2, 4), own_rows)
            else:
                for m in far:
                    dmap((m,), own_rows + other_rows, (), (tails[0],))
            state["scale"], state["ratio"], state["ratio_sum"], state["kl"] = order(
                functools.partial(ratio_part, spots), (by_cell,), (density, inv, state["scale"])
            )
        if n_blk == 8:
            if t == 1:
                dmap((2, 4), other_rows, (back[2][0], back[4][0]), (tails[0],))
            if t == 3:
                dmap((6,), own_rows + other_rows, (back[3][0], back[5][0]), (tails[0],))
        if t in (count - 2, count - 1):
            state["swapped", t - count] = swap(expr_part(1, (t - count + 2,)), 1)
        if t == count:
            state["scalars"] = order(
                functools.partial(scalar_results, n_blk // 2, cells, spots, rows, end),
                (*[tails[m] for m in range(0, n_blk, 2)], got[lag], total_of[0], by_cell),
                (state["kl"],),
            )
        if t == count + 1:
            state["expr"] = expr_part(0, (0, 1), (state["swapped", -2], state["swapped", -1]))

    dmap((0,), own_rows, (), (tot,))
    send(0)
    dmap((0,), other_rows)
    tot_moved = swap(order.here(tot), 1)
    for t in range(count + lag):
        send(t + 1)
        extra(t)
        if t > lag:
            finish(t - lag - 1)
        if t < count:
            block, first = back[places[t]]
            size = block.shape[0] if t == 0 else rows
            part[t] = order(functools.partial(add, first, size), (block, got[t]))
            mid[t] = lax.ppermute(part[t], "gene", MIDDLE)
    finish(count - 1)
    loss, rms_map, rms_pred = (x[0, 0] for x in state["scalars"])
    return (loss, state["grad"], state["expr"], rms_map, rms_pred)


def solution(mesh):
    placed = (
        P(None, "blk"),
        P("blk", "gene"),
        P("blk", "gene"),
        P(),
        P(None, "gene"),
        P("gene"),
        P("blk"),
    )
    return jax.shard_map(
        shards,
        mesh=mesh,
        in_specs=placed,
        out_specs=(P(), P(None, "blk"), P("blk", "gene"), P(), P()),
        check_vma=False,
    )
```

```python
import functools

import jax
import jax.numpy as jnp
from jax import lax
from jax.experimental import pallas as pl
from jax.experimental.pallas import tpu as pltpu
from jax.sharding import PartitionSpec as P

GENES = 2048
SLIDES = 4
LANES = 128
F32 = jnp.float32
BF16 = jnp.bfloat16
PAIR = [(0, 1), (1, 0), (2, 3), (3, 2)]
MIDDLE = [(1, 2), (2, 1)]


def room(mib):
    return pltpu.CompilerParams(vmem_limit_bytes=mib * 1024 * 1024)


class Order:
    def __init__(self):
        self.last = None

    def __call__(self, step, fresh, const=(), wait=()):
        gate = [*wait] if self.last is None else [self.last, *wait]
        if gate:
            fresh = lax.optimization_barrier((*fresh, *gate))[: len(fresh)]
        out = step(*fresh, *const)
        self.last = out[0] if isinstance(out, (tuple, list)) else out
        return out

    def here(self, x):
        return lax.optimization_barrier((x, self.last))[0]


def split(x):
    high = x.astype(BF16)
    return high, (x - high.astype(F32)).astype(BF16)


def three(a, b, dims):
    def dot(u, v):
        return lax.dot_general(u, v, (dims, ((), ())), preferred_element_type=F32)

    return dot(a[0], b[0]) + (dot(a[0], b[1]) + dot(a[1], b[0]))


def exact(a, b, dims):
    return lax.dot_general(a, b, (dims, ((), ())), precision=lax.Precision.HIGHEST, preferred_element_type=F32)


def cost(flops, size):
    del flops, size
    return pl.CostEstimate(flops=1, bytes_accessed=1, transcendentals=0)


def big(*arrays):
    return sum(x.size for x in arrays) * 4 // 2**20 + 1


VMEM = pl.BlockSpec(memory_space=pltpu.VMEM)
SMEM = pl.BlockSpec(memory_space=pltpu.SMEM)
HBM = pl.BlockSpec(memory_space=pltpu.HBM)


def at_rows(i, step, count=1):
    start = i * step
    return pl.ds(start if isinstance(i, int) else pl.multiple_of(start, 16), step * count)


def cut_kernel(layout, step, at_ref, l_ref, *refs):
    outs, sems = refs[:-1], refs[-1]
    copies = []
    for out, places in zip(outs, layout, strict=True):
        for k, place in enumerate(places):
            copies.append(
                pltpu.make_async_copy(
                    l_ref.at[at_rows(at_ref[place], step)], out.at[at_rows(k, step)], sems.at[len(copies)]
                )
            )
    for copy in copies:
        copy.start()
    for copy in copies:
        copy.wait()


def cut_blocks(layout, step, at, logits):
    width = logits.shape[1]
    count = sum(len(places) for places in layout)
    return pl.pallas_call(
        functools.partial(cut_kernel, layout, step),
        in_specs=[SMEM, VMEM],
        out_specs=(HBM,) * len(layout),
        out_shape=tuple(jax.ShapeDtypeStruct((len(places) * step, width), F32) for places in layout),
        scratch_shapes=[pltpu.SemaphoreType.DMA((count,))],
        name="cut",
        compiler_params=room(big(logits) + 2),
        cost_estimate=cost(0, 8 * count * step * width),
    )(at, logits)


def by_cell_rows(ref, count, step):
    genes = ref.shape[1]
    return jnp.concatenate([ref[:count, :], ref[count : 2 * count, : step - genes]], axis=1)


def softmax_kernel(spots, scale, step, l_ref, inv_ref, cell_ref, o_ref, buffer, sem):
    cells, width = l_ref.shape
    genes = cell_ref.shape[1]
    count = cells // step

    def column(k, total):
        e = jnp.exp(l_ref[at_rows(k, step), :])
        return total + jnp.sum(e.reshape(step // 8, 8, width), axis=0)

    total = lax.fori_loop(0, count, column, jnp.zeros((8, width), F32))
    inv = 1.0 / jnp.sum(total, axis=0, keepdims=True)
    inv_ref[...] = inv
    ones = jnp.ones((16, width), BF16)

    def row(k, square):
        e = jnp.exp(l_ref[at_rows(k, step), :])
        share = e * inv
        buffer[at_rows(k, step), :] = e * scale
        pltpu.make_async_copy(buffer.at[at_rows(k, step)], o_ref.at[at_rows(k, step)], sem).start()
        high, low = split(share)
        sums = [lax.dot_general(ones, x, (((1,), (1,)), ((), ())), preferred_element_type=F32) for x in (high, low)]
        sums = (sums[0] + sums[1])[0:1, :] * (1.0 / spots)
        cell_ref[pl.ds(k, 1), :] = sums[:, :genes]
        cell_ref[pl.ds(count + k, 1), : step - genes] = sums[:, genes:]
        return square + jnp.sum((share * share).reshape(step // 8, 8, width), axis=0)

    square = lax.fori_loop(0, count, row, jnp.zeros((8, width), F32))
    cell_ref[count:, step - genes :] = jnp.full((count, 2 * genes - step), jnp.sum(square), F32)
    pltpu.make_async_copy(buffer, o_ref, sem).wait()


def softmax_sums(spots, genes, step, logits):
    cells, width = logits.shape
    return pl.pallas_call(
        functools.partial(softmax_kernel, spots, float(cells), step),
        in_specs=[VMEM],
        out_specs=(VMEM, VMEM, HBM),
        out_shape=(
            jax.ShapeDtypeStruct((1, width), F32),
            jax.ShapeDtypeStruct((2 * cells // step, genes), F32),
            pltpu.HBM((cells, width), F32),
        ),
        scratch_shapes=[pltpu.VMEM((cells, width), F32), pltpu.SemaphoreType.DMA],
        name="softmax",
        compiler_params=room(2 * big(logits) + 4),
        cost_estimate=cost(0, 0),
    )(logits)


def parts_kernel(step, x_ref, high_ref, low_ref, buffer, sems):
    count = x_ref.shape[0] // step

    def copy(k):
        return pltpu.make_async_copy(x_ref.at[at_rows(k, step)], buffer.at[at_rows(k, step)], sems.at[k])

    for k in range(count):
        copy(k).start()
    for k in range(count):
        copy(k).wait()
        high_ref[at_rows(k, step), :], low_ref[at_rows(k, step), :] = split(buffer[at_rows(k, step), :])


def parts_of(x, step):
    return pl.pallas_call(
        functools.partial(parts_kernel, step),
        in_specs=[HBM],
        out_specs=(VMEM, VMEM),
        out_shape=(pltpu.VMEM(x.shape, BF16), pltpu.VMEM(x.shape, BF16)),
        scratch_shapes=[pltpu.VMEM(x.shape, F32), pltpu.SemaphoreType.DMA((x.shape[0] // step,))],
        name="parts",
        compiler_params=room(12),
        cost_estimate=cost(4 * x.size, 8 * x.size),
    )(x)


def pred_kernel(jobs, n_acc, step, tail, at_ref, *refs):
    n_l = 1 + max(job[2] for job in jobs)
    n_given = max(job[1] for job in jobs)
    ls, xs, given, outs = refs[:n_l], refs[n_l : n_l + 4], refs[n_l + 4 :][:n_given], refs[-n_acc:]
    place = lambda at: at_ref[at[0]] if isinstance(at, list) else at
    for k in range(n_acc):
        acc = None
        for _, g, l, l_at, x, x_at, count in [job for job in jobs if job[0] == k]:
            if g:
                acc = given[g - 1][...]
            for c in range(count):
                e = split(jnp.exp(ls[l][at_rows(place(l_at) + c, step), :]))
                rows = at_rows(place(x_at) + c, step)
                term = three(e, (xs[2 * x][rows, :], xs[2 * x + 1][rows, :]), ((0,), (0,)))
                acc = term if acc is None else acc + term
        outs[k][: acc.shape[0], :] = acc
        if tail:
            outs[k][acc.shape[0] :, :] = refs[-n_acc - 1][...]


def pred_sums_of(jobs, n_acc, step, at, ls, xs, given, tail=()):
    width, genes = ls[0].shape[1], xs[0].shape[1]
    steps = sum(job[-1] for job in jobs)
    return pl.pallas_call(
        functools.partial(pred_kernel, jobs, n_acc, step, len(tail)),
        in_specs=[SMEM] + [VMEM] * (len(ls) + len(xs) + len(given) + len(tail)),
        out_specs=(VMEM,) * n_acc,
        out_shape=(jax.ShapeDtypeStruct((width + sum(x.shape[0] for x in tail), genes), F32),) * n_acc,
        name="pred",
        compiler_params=room(16),
        cost_estimate=cost(6 * steps * step * width * genes, 4 * steps * step * (width + genes)),
    )(at, *ls, *xs, *given, *tail)


def weights_of(mask_ref, counts_ref):
    weights = (mask_ref[...] * counts_ref[...]).astype(F32)
    return jnp.concatenate([weights, jnp.zeros((8 - SLIDES, weights.shape[1]), F32)], axis=0)


def column_of(row):
    return jnp.transpose(jnp.broadcast_to(row, (LANES, row.shape[1])))


def sums_kernel(n_parts, *refs):
    parts, (cells_ref, inv_ref, spatial_ref, ids_ref, mask_ref, counts_ref, pred_ref, wide_ref, spot_ref, q_ref) = (
        refs[:n_parts],
        refs[n_parts:],
    )
    spatial = spatial_ref[...]
    pred, q = parts[0][...], cells_ref[...]
    for part in parts[1:]:
        pred = pred + part[: pred.shape[0], :]
        q = q + part[pred.shape[0] :, :]
    q_ref[...] = q
    genes = pred.shape[1]
    pred = pred * jnp.concatenate([column_of(inv_ref[...])] * (genes // LANES), axis=1)
    pred_ref[...] = pred
    onehot = (lax.broadcasted_iota(jnp.int32, (8, LANES), 0) == ids_ref[...]).astype(F32)
    ones = jnp.ones((8, genes), F32)
    rows = lax.broadcasted_iota(jnp.int32, (8, LANES), 0)
    spot = jnp.where(rows == 3, jnp.sum(weights_of(mask_ref, counts_ref)), 0.0)
    for k, product in enumerate((pred * spatial, pred * pred, spatial * spatial)):
        wide_ref[8 * k : 8 * k + 8, :] = exact(onehot, product, ((1,), (0,)))
        spot = jnp.where(rows == k, exact(ones, product, ((1,), (1,))), spot)
    spot_ref[...] = spot


def pred_sums(n_parts, *args):
    parts, (by_cell, inv, spatial, ids, mask, counts) = args[:n_parts], args[n_parts:]
    width, genes = spatial.shape
    return pl.pallas_call(
        functools.partial(sums_kernel, n_parts),
        out_shape=(
            jax.ShapeDtypeStruct((width, genes), F32),
            jax.ShapeDtypeStruct((24, genes), F32),
            jax.ShapeDtypeStruct((8, width), F32),
            jax.ShapeDtypeStruct(by_cell.shape, F32),
        ),
        name="sums",
        compiler_params=room(12),
        cost_estimate=cost(10 * width * genes * 48, 4 * width * genes * 6),
    )(*parts, by_cell, inv, spatial, ids, mask, counts)


def dpred_kernel(spots, share_gene, *refs):
    wides, spot, refs = refs[:2], refs[2][...] + refs[3][...], refs[4:]
    pred_ref, spatial_ref, ids_ref, mask_ref, counts_ref, inv_ref, d_ref, tot_ref = refs
    weights = weights_of(mask_ref, counts_ref)
    genes = pred_ref.shape[1]
    a, b, c = (wides[0][8 * k : 8 * k + 8, :] + wides[1][8 * k : 8 * k + 8, :] for k in range(3))
    e, f, h, wsum = (spot[k : k + 1, :] for k in range(4))
    wsum = jnp.max(wsum)
    gain = weights / wsum
    inv_g = lax.rsqrt(b * c + 1e-06)
    inv_s = lax.rsqrt(f * h + 1e-06)
    grad_a = -gain * inv_g
    grad_b = gain * a * c * inv_g * inv_g * inv_g
    onehot = (lax.broadcasted_iota(jnp.int32, (8, LANES), 0) == ids_ref[...]).astype(F32)
    wide = functools.partial(jnp.concatenate, axis=1)
    by_spatial = exact(onehot, grad_a, ((0,), (0,))) - wide([column_of(inv_s / spots)] * (genes // LANES))
    by_pred = exact(onehot, grad_b, ((0,), (0,))) + wide(
        [column_of(e * h * inv_s * inv_s * inv_s / spots)] * (genes // LANES)
    )
    pred = pred_ref[...]
    dpred = by_spatial * spatial_ref[...] + by_pred * pred
    inv = inv_ref[...]
    d_ref[:LANES, :] = dpred * wide([column_of(inv)] * (genes // LANES))
    own = exact(jnp.ones((8, genes), F32), pred * dpred, ((1,), (1,))) * inv
    d_ref[LANES:, :] = wide([own] * (genes // LANES))
    rows = lax.broadcasted_iota(jnp.int32, (8, LANES), 0)
    tot = jnp.where(rows == 0, jnp.sum(weights * a * inv_g), 0.0)
    tot = jnp.where(rows == 1, jnp.sum(e * inv_s), tot)
    tot = jnp.where(rows == 2, jnp.sum(f), tot)
    tot_ref[...] = jnp.where(rows == 3, wsum * share_gene, tot)


def dpred_scaled(spots, share_gene, *args):
    spatial = args[5]
    width, genes = spatial.shape
    return pl.pallas_call(
        functools.partial(dpred_kernel, spots, share_gene),
        out_shape=(
            jax.ShapeDtypeStruct((width + 8, genes), F32),
            jax.ShapeDtypeStruct((8, width), F32),
        ),
        name="dpred",
        compiler_params=room(12),
        cost_estimate=cost(10 * width * genes * 48, 4 * width * genes * 6),
    )(*args)


def dmap_kernel(ranges, n, *refs):
    xs, ds, outs = refs[:4], refs[4 : 4 + n], refs[-n:]
    parts = [split(d[:LANES, :]) for d in ds]
    d = tuple(jnp.concatenate([part[i] for part in parts], axis=0) for i in range(2))
    own = jnp.concatenate([d[LANES : LANES + 1, :LANES] for d in ds], axis=1)
    at = 0
    for x, first, count in ranges:
        here = pl.ds(first, count)
        value = three((xs[2 * x][here, :], xs[2 * x + 1][here, :]), d, ((1,), (1,))) - own
        for i, out in enumerate(outs):
            out[at : at + count, :] = value[:, i * LANES : (i + 1) * LANES]
        at += count
    if len(refs) > 4 + 2 * n:
        for out in outs:
            out[at:, :] = refs[4 + n][...]


def dmap_blocks(ranges, ds, xs, tail=()):
    width = ds[0].shape[0] - 8
    rows = sum(count for _, _, count in ranges) + 8 * len(tail)
    return pl.pallas_call(
        functools.partial(dmap_kernel, ranges, len(ds)),
        in_specs=[VMEM] * (4 + len(ds) + len(tail)),
        out_specs=(VMEM,) * len(ds),
        out_shape=(jax.ShapeDtypeStruct((rows, width), F32),) * len(ds),
        name="dmap",
        compiler_params=room(16),
        cost_estimate=cost(0, 0),
    )(*xs, *ds, *tail)


def egrad_kernel(scale, ks, step, wheres, n_add, at_ref, *refs):
    n = len(wheres)
    counts = [2 if isinstance(where, tuple) else 1 for where in wheres]
    ls, ds, adds, o_ref = refs[: sum(counts)], refs[sum(counts) : sum(counts) + n], refs[sum(counts) + n : -1], refs[-1]
    parts = [split(d[:LANES, :]) for d in ds]
    d = tuple(jnp.concatenate([part[i] for part in parts], axis=0) for i in range(2))
    for j, k in enumerate(ks):
        es, at = [], 0
        for where, number in zip(wheres, counts, strict=True):
            if number == 2:
                mine, others = (ls[at + i][at_rows(where[i], step), :] for i in range(2))
                l = jnp.where(at_ref[0] == k, mine, others)
            else:
                l = ls[at][at_rows(where + k, step), :]
            at += number
            es.append(jnp.exp(l))
        value = three(split(jnp.concatenate(es, axis=1)), d, ((1,), (0,))) * scale
        o_ref[at_rows(j, step), :] = value + adds[j][...] if n_add else value


def egrad_part(ks, step, wheres, scale, at, ls, ds, adds=()):
    genes = ds[0].shape[1]
    return pl.pallas_call(
        functools.partial(egrad_kernel, scale, ks, step, wheres, len(adds)),
        in_specs=[SMEM] + [VMEM] * (len(ls) + len(ds) + len(adds)),
        out_specs=VMEM,
        out_shape=jax.ShapeDtypeStruct((len(ks) * step, genes), F32),
        name="egrad",
        compiler_params=room(big(*ls, *ds, *adds) + 24),
        cost_estimate=cost(0, 0),
    )(at, *ls, *ds, *adds)


def ratio_kernel(spots, scale, cell_ref, density_ref, inv_ref, a_ref, _, ratio_ref, sum_ref, kl_ref, a, sems):
    inv = inv_ref[...]
    count, step = density_ref.shape

    def load(k):
        return pltpu.make_async_copy(a_ref.at[at_rows(k, step)], a.at[at_rows(k, step)], sems.at[k])

    for k in range(count):
        load(k).start()
    density = density_ref[...]
    target = density / jnp.sum(density)
    q = by_cell_rows(cell_ref, count, step)
    ratios = target / q / spots
    ratio_ref[...] = ratios
    kl_ref[...] = jnp.full(kl_ref.shape, jnp.sum(target * (jnp.log(target) - jnp.log(q))))
    rows = lax.broadcasted_iota(jnp.int32, (16, step), 0)
    total = jnp.zeros((1, LANES), F32)
    for k in range(count):
        load(k).wait()
        high, low = split(ratios[k : k + 1, :])
        lhs = jnp.where(rows == 0, high.astype(F32), jnp.where(rows == 1, low.astype(F32), 0.0)).astype(BF16)
        for part in split(a[at_rows(k, step), :]):
            sums = lax.dot_general(lhs, part, (((1,), (0,)), ((), ())), preferred_element_type=F32)
            total = total + (sums[0:1, :] + sums[1:2, :])
    sum_ref[...] = jnp.broadcast_to(total * (inv * inv * (1.0 / scale)), sum_ref.shape)


def ratio_part(spots, by_cell, density, inv, a):
    cells, width = a.shape
    return pl.pallas_call(
        functools.partial(ratio_kernel, spots, float(cells)),
        in_specs=[VMEM, VMEM, VMEM, HBM],
        out_specs=(HBM, VMEM, VMEM, VMEM),
        out_shape=(
            pltpu.HBM((cells, width), F32),
            jax.ShapeDtypeStruct(density.shape, F32),
            jax.ShapeDtypeStruct((8, width), F32),
            jax.ShapeDtypeStruct((8, width), F32),
        ),
        scratch_shapes=[pltpu.VMEM((cells, width), F32), pltpu.SemaphoreType.DMA((density.shape[0],))],
        input_output_aliases={3: 0},
        name="ratio",
        compiler_params=room(big(a) + 8),
        cost_estimate=cost(0, 0),
    )(by_cell, density, inv, a)


def join_kernel(a_ref, b_ref, o_ref):
    half = a_ref.shape[0]
    o_ref[:half, :] = a_ref[...]
    o_ref[half:, :] = b_ref[...]


def join(a, b):
    return pl.pallas_call(
        join_kernel,
        in_specs=[VMEM, VMEM],
        out_specs=VMEM,
        out_shape=jax.ShapeDtypeStruct((2 * a.shape[0], a.shape[1]), F32),
        name="join",
        compiler_params=room(8),
        cost_estimate=cost(0, 0),
    )(a, b)


def add_kernel(a_ref, b_ref, o_ref):
    o_ref[...] = a_ref[...] + b_ref[: o_ref.shape[0], :]


def plus(a, b):
    return pl.pallas_call(
        add_kernel,
        in_specs=[VMEM, VMEM],
        out_specs=VMEM,
        out_shape=jax.ShapeDtypeStruct(a.shape, F32),
        name="add",
        compiler_params=room(8),
        cost_estimate=cost(0, 0),
    )(a, b)


def add_all_kernel(*refs):
    total = refs[0][...]
    for ref in refs[1:-1]:
        total = total + ref[...]
    refs[-1][...] = total


def add_all(*arrays):
    return pl.pallas_call(
        add_all_kernel,
        in_specs=[VMEM] * len(arrays),
        out_specs=VMEM,
        out_shape=jax.ShapeDtypeStruct(arrays[0].shape, F32),
        name="add_all",
        compiler_params=room(8),
        cost_estimate=cost(0, 0),
    )(*arrays)


def next_kernel(cuts, end_ref, s_ref, y_ref, *refs):
    blocks, (t_ref, o_ref, c_ref) = refs[:-3], refs[-3:]
    total = s_ref[...] + y_ref[...]
    t_ref[...] = total
    at = 0
    for block, (first, count) in zip(blocks, cuts, strict=True):
        c_ref[at : at + count, :] = block[first : first + count, :]
        at += count
    own = c_ref[...]
    both = min(at, total.shape[0])
    o_ref[:both, :] = jnp.where(end_ref[0] == 1, own[:both, :], total[:both, :])
    if o_ref.shape[0] > both:
        o_ref[both:, :] = (own if at > both else total)[both:, :]


def next_piece(cuts, end, s, y, *blocks):
    size, width = sum(count for _, count in cuts), s.shape[1]
    return pl.pallas_call(
        functools.partial(next_kernel, cuts),
        in_specs=[SMEM] + [VMEM] * (2 + len(blocks)),
        out_specs=(VMEM, VMEM, VMEM),
        out_shape=(
            jax.ShapeDtypeStruct(s.shape, F32),
            jax.ShapeDtypeStruct((max(size, s.shape[0]), width), F32),
            jax.ShapeDtypeStruct((size, width), F32),
        ),
        name="next",
        compiler_params=room(10),
        cost_estimate=cost(0, 0),
    )(end, s, y, *blocks)


def final_kernel(place, cuts, step, end_ref, at_ref, *refs):
    n, m = len(cuts), 1 + max(k for half in cuts for k, _, _ in half)
    rxs, ss = refs[:m], refs[m : 2 * m]
    ratio_ref, sum_ref, inv_ref, a_ref, _, _, o_ref, a, b, sems = refs[2 * m :]
    load = pltpu.make_async_copy(a_ref.at[at_rows(at_ref[place], step, n)], a, sems.at[n])
    load.start()
    rows = lax.broadcasted_iota(jnp.int32, (16, step), 0)
    ones = (lax.broadcasted_iota(jnp.int32, (16, LANES), 0) < 3).astype(BF16)
    stores = []
    for k in range(n):
        at, here = at_ref[place] + k, at_rows(k, step)
        ratio = ratio_ref[pl.ds(at, 1), :]
        high = ratio.astype(BF16).astype(F32)
        mid = (ratio - high).astype(BF16).astype(F32)
        terms = jnp.where(rows == 0, high, jnp.where(rows == 1, mid, jnp.where(rows == 2, ratio - high - mid, 0.0)))
        column = lax.dot_general(terms.astype(BF16), ones, (((0,), (0,)), ((), ())), preferred_element_type=F32)
        whole = jnp.concatenate(
            [
                jnp.where(end_ref[0] == 1, rxs[i][first : first + count, :], ss[i][first : first + count, :])
                for i, first, count in cuts[k]
            ],
            axis=0,
        )
        value = whole + (sum_ref[0:1, :] - column * inv_ref[...])
        if k == 0:
            load.wait()
        b[here, :] = a[here, :] * value
        stores.append(pltpu.make_async_copy(b.at[here], o_ref.at[at_rows(at, step)], sems.at[k]))
        stores[-1].start()
    for store in stores:
        store.wait()


def final_block(step, cuts, place, end, at, rxs, ss, ratio, ratio_sum, inv, a, grad):
    width = a.shape[1]
    n, m = len(cuts), len(ss)
    return pl.pallas_call(
        functools.partial(final_kernel, place, cuts, step),
        in_specs=[SMEM, SMEM] + [VMEM] * (2 * m + 3) + [HBM, HBM],
        out_specs=(HBM, HBM),
        out_shape=(pltpu.HBM(a.shape, F32), pltpu.HBM(grad.shape, F32)),
        scratch_shapes=[pltpu.VMEM((n * step, width), F32)] * 2 + [pltpu.SemaphoreType.DMA((1 + n,))],
        input_output_aliases={5 + 2 * m: 0, 6 + 2 * m: 1},
        name="final",
        compiler_params=room(12),
        cost_estimate=cost(0, 0),
    )(end, at, *rxs, *ss, ratio, ratio_sum, inv, a, grad)


def blank(shape):
    return pl.pallas_call(lambda o_ref: None, out_specs=HBM, out_shape=pltpu.HBM(shape, F32), name="blank")()


def scalars_kernel(n, cells, spots, step, end_ref, *refs):
    sums = [refs[k][-8:, :] for k in range(n)]
    rx_ref, s_ref, q_ref, kl_ref, loss_ref, map_ref, pred_ref = refs[n:]
    while len(sums) > 1:
        sums = [a + b for a, b in zip(sums[::2], sums[1::2], strict=True)]
    by_gene = jnp.where(end_ref[0] == 1, rx_ref[step : step + 8, :], s_ref[step : step + 8, :])
    cosine, fitted, wsum, scos = by_gene[0:1, :], sums[0][2:3, :], by_gene[3:4, :], sums[0][1:2, :]
    loss = -cosine / wsum - scos / spots + kl_ref[0:1, :]
    rms_map = jnp.sqrt(q_ref[q_ref.shape[0] - 1 :, q_ref.shape[1] - LANES :] / (cells * spots))
    rms_pred = jnp.sqrt(fitted / (spots * GENES))
    for ref, value in zip((loss_ref, map_ref, pred_ref), (loss, rms_map, rms_pred), strict=True):
        ref[0, 0] = jnp.max(value)


def scalar_results(n, cells, spots, step, end, *args):
    return pl.pallas_call(
        functools.partial(scalars_kernel, n, cells, spots, step),
        in_specs=[SMEM] + [VMEM] * len(args),
        out_specs=(SMEM,) * 3,
        out_shape=(jax.ShapeDtypeStruct((1, 1), F32),) * 3,
        name="scalars",
        compiler_params=room(24),
        cost_estimate=cost(0, 0),
    )(end, *args)


def shards(logits, expression, spatial, density, gene_mask, gene_counts, slide_ids):
    n_blk = lax.axis_size("blk")
    n_gene = lax.axis_size("gene")
    me = lax.axis_index("blk")
    plane = lax.axis_index("gene")
    cells, width = logits.shape
    rows, genes = expression.shape
    half = rows // 2
    spots = width * n_blk
    order = Order()

    def swap(x, m):
        return lax.ppermute(x, "blk", [(i, i ^ m) for i in range(n_blk)])

    def across(x, m):
        return lax.ppermute(x, "gene", [(i, i ^ m) for i in range(n_gene)])

    def cut(l, r, first, size):
        return lax.dynamic_slice_in_dim(l, (me ^ r) * rows + first, size, 0)

    far = sorted(range(2, n_blk, 2), key=lambda m: (m.bit_count(), m))
    side = plane % 2
    at = jnp.stack([side, 1 - side, *[(me ^ r) * 2 + k for r in range(n_blk) for k in range(2)]]
        + [(me ^ r) * 2 + side for r in range(n_blk)]).astype(jnp.int32)

    def whole(r):
        return (2 + 2 * r, 3 + 2 * r)

    def mine(r):
        return (2 + 2 * n_blk + r,)

    sent, passed, held = {}, {}, {}

    other = swap(expression, 1)
    constants = (slide_ids[None, :], gene_mask, gene_counts[None, :])
    n_q = cells // genes

    def add_pred(jobs, n_acc, ls, given=(), tail=()):
        n, g = len(ls), len(given)

        def run(*a):
            return pred_sums_of(jobs, n_acc, half, at, a[:n], a[n + g : n + g + 4], a[n : n + g], a[n + g + 4 :])

        return order(run, (*ls, *given), (*own_x, *other_x, *tail))

    def cuts(*layout):
        return order(lambda l: cut_blocks(layout, half, at, l), (logits,))

    if n_blk == 8 and n_gene == 4:
        near3, near5 = order(
            lambda l: [lax.dynamic_slice_in_dim(l, (me ^ r) * rows + side * half, half, 0) for r in (3, 5)], (logits,)
        )
        sent[3], sent[5] = swap(near3, 2), swap(near5, 4)
        own_x = order(lambda x: parts_of(x, half), (expression,))
        both, near2, near4, stay = cuts(mine(6) + mine(7), whole(2), whole(4), whole(0) + whole(1))
        passed[3] = across(order(join, (sent[3], sent[5])), 1)
        sent[6], sent[2], sent[4] = swap(order.here(both), 6), swap(order.here(near2), 2), swap(order.here(near4), 4)
        inv, by_cell, scale = order(functools.partial(softmax_sums, spots, genes, half), (logits,))
        other_x = order(lambda x: parts_of(x, half), (other,))
        (acc0,) = add_pred(((0, 0, 0, 0, 0, 0, 2), (0, 0, 0, 2, 1, 0, 2)), 1, (stay,))
        acc2, acc4 = add_pred(((0, 0, 0, 0, 1, [0], 1), (1, 0, 1, 0, 1, [0], 1)), 2, (sent[3], sent[5]))
        cell_moved = swap(order.here(by_cell), 1)
        passed[6] = across(order.here(sent[6]), 1)
        (acc6,) = add_pred(((0, 0, 0, 0, 0, [0], 1), (0, 0, 0, 1, 1, [0], 1)), 1, (sent[6],))
        acc2, acc4 = add_pred(
            ((0, 1, 0, 0, 1, [1], 1), (1, 2, 0, 1, 1, [1], 1)), 2, (passed[3],), (acc2, acc4)
        )
        by_cell = order(plus, (by_cell, cell_moved))
        (acc2,) = add_pred(((0, 1, 0, 0, 0, 0, 2),), 1, (sent[2],), (acc2,), (by_cell,))
        moved = {2: swap(acc2, 2)}
        (acc4,) = add_pred(((0, 1, 0, 0, 0, 0, 2),), 1, (sent[4],), (acc4,), (by_cell,))
        moved[4] = swap(acc4, 4)
        (acc6,) = add_pred(((0, 1, 0, 0, 0, [1], 1), (0, 0, 0, 1, 1, [1], 1)), 1, (passed[6],), (acc6,), (by_cell,))
        moved[6] = swap(acc6, 6)
        held = {
            2: ((sent[2],), 0),
            3: ((sent[3], passed[3]), (0, 0)),
            4: ((sent[4],), 0),
            5: ((sent[5], passed[3]), (0, 1)),
            6: ((sent[6], passed[6]), (0, 0)),
            7: ((sent[6], passed[6]), (1, 1)),
        }
    else:
        inv, by_cell, scale = order(functools.partial(softmax_sums, spots, genes, half), (logits,))
        by_cell = order(plus, (by_cell, swap(by_cell, 1)))
        own_x = order(lambda x: parts_of(x, half), (expression,))
        other_x = order(lambda x: parts_of(x, half), (other,))
        (stay,) = cuts(whole(0) + whole(1))
        (acc0,) = add_pred(((0, 0, 0, 0, 0, 0, 2), (0, 0, 0, 2, 1, 0, 2)), 1, (stay,))
        moved = {}
        for m in far:
            blocks = cuts(whole(m), whole(m + 1))
            for r in (m, m + 1):
                sent[r] = swap(blocks[r - m], m)
                held[r] = ((sent[r],), 0)
            (acc,) = add_pred(((0, 0, 0, 0, 0, 0, 2), (0, 0, 1, 0, 1, 0, 2)), 1, (sent[m], sent[m + 1]), (), (by_cell,))
            moved[m] = swap(acc, m)
    held[0], held[1] = ((stay,), 0), ((stay,), 2)

    parts = [acc0] + [moved[m] for m in far]
    pred, wide, spot, by_cell = order(
        functools.partial(pred_sums, len(parts)), parts, (by_cell, inv, spatial, *constants)
    )
    density = density.reshape(cells // half, half)
    state = {"scale": scale, "grad": blank((cells, width))}

    spot_moved = across(spot, 1)
    m = 1
    while 2 * m < n_blk:
        wide = order(plus, (wide, swap(wide, m)))
        m *= 2
        if m == 2:
            spot = order(add_all, (spot, spot_moved))
            spot_moved = across(spot, 2)
    wide_moved = swap(wide, m)
    grad, tot = order(
        functools.partial(dpred_scaled, spots, 1.0 / n_gene),
        (wide, wide_moved, spot, spot_moved),
        (pred, spatial, *constants, inv),
    )
    grads, back, tails = {0: grad}, {}, {}

    def dmap(ms, ranges, wait=(), tail=()):
        outs = order(
            lambda *a: dmap_blocks(ranges, a[: len(ms)], a[len(ms) : len(ms) + 4], a[len(ms) + 4 :]),
            [grads[m] for m in ms],
            (*own_x, *other_x, *tail),
            wait,
        )
        if tail and ms != (0,):
            tails.update({m: swap(d, m) for m, d in zip(ms, outs, strict=True)})
            return [tails[m] for m in ms]
        return [swap(d, m) if m else d for m, d in zip(ms, outs, strict=True)]

    def block_rows(odd):
        return ((odd, 0, half), (odd, half, half))

    blocks = [0, 1, 2, 4, 3, 5, 6, 7] if n_blk == 8 else [r for m in [0, *far] for r in (m, m + 1)]
    long = 3 * half // 2
    sizes = [long, long, half] + [long] * ((cells - 2 * rows) // long)
    starts = [sum(sizes[:t]) for t in range(len(sizes))]
    count, lag = len(sizes), 3
    assert starts[3] == 2 * rows and sum(sizes) == cells

    def overlap(first, size, cuts_at, cuts_size):
        found = []
        for k, (a, n) in enumerate(zip(cuts_at, cuts_size, strict=True)):
            low, high = max(first, a), min(first + size, a + n)
            if low < high:
                found.append((k, low - a, high - low))
        return found

    block_starts, block_sizes = [rows * k for k in range(len(blocks))], [rows] * len(blocks)
    part, total_of, mid, got, own = {}, {}, {}, {}, {}
    end = jnp.reshape((plane == 0) | (plane == n_gene - 1), (1,)).astype(jnp.int32)

    def send(t):
        if t >= count + lag:
            return
        if t < lag:
            ranges = overlap(starts[t], sizes[t], (0, rows), (rows, rows))
            own[t] = buffer = dmap((0,), tuple(ranges), (), (tot,) if t == 0 else ())[0]
        elif t < count:
            found = overlap(starts[t], sizes[t], block_starts, block_sizes)
            cuts = tuple((back[blocks[k]][1] + first, n) for k, first, n in found)
            total_of[t - lag], buffer, own[t] = order(
                lambda s, y, *b: next_piece(cuts, end, s, y, *b),
                (part[t - lag], mid[t - lag], *[back[blocks[k]][0] for k, _, _ in found]),
            )
        else:
            buffer = total_of[t - lag] = order(plus, (part[t - lag], mid[t - lag]))
        got[t] = lax.ppermute(buffer, "gene", PAIR)

    def finish(k):
        halves = [overlap(block_starts[k] + half * h, half, starts, sizes) for h in range(2)]
        ts = sorted({t for found in halves for t, _, _ in found})
        cuts = tuple(tuple((ts.index(t), first, n) for t, first, n in found) for found in halves)
        m = len(ts)
        state["scale"], state["grad"] = order(
            lambda *a: final_block(half, cuts, 2 + 2 * blocks[k], end, at, a[:m], a[m : 2 * m], *a[2 * m :]),
            (*[got[t + lag] for t in ts], *[total_of[t] for t in ts]),
            (state["ratio"], state["ratio_sum"], inv, state["scale"], state["grad"]),
        )

    last_piece = [max(t for t, _, _ in overlap(a, rows, starts, sizes)) for a in block_starts]

    def expr_part(odd, ks, adds=()):
        ms = [0, *far]
        ls = [l for m in ms for l in held[m + odd][0]]
        wheres = [held[m + odd][1] for m in ms]
        n, m = len(ls), len(adds)
        return order(
            lambda d, *a: egrad_part(ks, half, wheres, float(cells), at, a[m : m + n], (d, *a[m + n :]), a[:m]),
            (grads[0], *adds),
            (*ls, *[grads[m] for m in far]),
        )

    def first_dmap():
        if n_blk == 8:
            for r, d in zip((2, 4), dmap((2, 4), block_rows(0)), strict=True):
                back[r] = (d, 0)
        else:
            tails[0] = order(plus, (tot, tot_moved))
            for m in far:
                (d,) = dmap((m,), block_rows(0) + block_rows(1), (), (tails[0],))
                back[m], back[m + 1] = (d, 0), (d, rows)

    def second_dmap():
        if n_blk == 8:
            tails[0] = order(plus, (tot, tot_moved))
            for r, d in zip((3, 5), dmap((2, 4), block_rows(1), (back[2][0], back[4][0]), (tails[0],)), strict=True):
                back[r] = (d, 0)

    def third_dmap():
        if n_blk == 8:
            back[6] = (dmap((6,), block_rows(0), (back[3][0], back[5][0]))[0], 0)

    def fourth_dmap():
        if n_blk == 8:
            back[7] = (dmap((6,), block_rows(1), (), (tails[0],))[0], 0)

    def kl():
        state["scale"], state["ratio"], state["ratio_sum"], state["kl"] = order(
            functools.partial(ratio_part, spots), (by_cell,), (density, inv, state["scale"])
        )

    def egrad(k):
        state["swapped", k] = swap(expr_part(1, (k,)), 1)

    def scalars():
        state["scalars"] = order(
            functools.partial(scalar_results, n_blk // 2, cells, spots, long, end),
            (*[tails[m] for m in range(0, n_blk, 2)], got[lag], total_of[0], by_cell),
            (state["kl"],),
        )

    def expr():
        state["expr"] = expr_part(0, (0, 1), (state["swapped", 0], state["swapped", 1]))

    late = count - 11
    plan = {
        (0, "between"): [first_dmap],
        (1, "after"): [kl],
        (2, "between"): [second_dmap],
        (4, "between"): [third_dmap],
        (5, "between"): [fourth_dmap],
        (late + 7, "between"): [functools.partial(egrad, 0)],
        (late + 8, "between"): [functools.partial(egrad, 1)],
        (late + 11, "between"): [scalars],
        (late + 12, "between"): [expr],
    }
    for k in range(len(blocks)):
        t = last_piece[k] + lag + 1
        if t < count + lag:
            plan.setdefault((t, "after"), []).append(functools.partial(finish, k))

    def extra(t, place):
        for step in plan.get((t, place), ()):
            step()

    send(0)
    for m in far:
        grads[m] = swap(order.here(grad), m)
    tot_moved = swap(order.here(tot), 1)
    for t in range(count + lag):
        extra(t, "before")
        send(t + 1)
        extra(t, "between")
        if t < count:
            part[t] = order(plus, (own[t], got[t]))
            mid[t] = lax.ppermute(part[t], "gene", MIDDLE)
        extra(t, "after")
    for k in range(len(blocks)):
        if last_piece[k] + lag + 1 >= count + lag:
            finish(k)
    loss, rms_map, rms_pred = (x[0, 0] for x in state["scalars"])
    return (loss, state["grad"], state["expr"], rms_map, rms_pred)


def solution(mesh):
    placed = (
        P(None, "blk"),
        P("blk", "gene"),
        P("blk", "gene"),
        P(),
        P(None, "gene"),
        P("gene"),
        P("blk"),
    )
    return jax.shard_map(
        shards,
        mesh=mesh,
        in_specs=placed,
        out_specs=(P(), P(None, "blk"), P("blk", "gene"), P(), P()),
        check_vma=False,
    )
```

```python
import functools

import jax
import jax.numpy as jnp
from jax import lax
from jax.experimental import pallas as pl
from jax.experimental.pallas import tpu as pltpu
from jax.sharding import PartitionSpec as P

GENES = 2048
SLIDES = 4
LANES = 128
F32 = jnp.float32
BF16 = jnp.bfloat16
PAIR = [(0, 1), (1, 0), (2, 3), (3, 2)]
MIDDLE = [(1, 2), (2, 1)]


def room(mib):
    return pltpu.CompilerParams(vmem_limit_bytes=mib * 1024 * 1024)


class Order:
    def __init__(self):
        self.last = None

    def __call__(self, step, fresh, const=(), wait=()):
        gate = [*wait] if self.last is None else [self.last, *wait]
        if gate:
            fresh = lax.optimization_barrier((*fresh, *gate))[: len(fresh)]
        out = step(*fresh, *const)
        self.last = out[0] if isinstance(out, (tuple, list)) else out
        return out

    def here(self, x):
        return lax.optimization_barrier((x, self.last))[0]


def split(x):
    high = x.astype(BF16)
    return high, (x - high.astype(F32)).astype(BF16)


def three(a, b, dims):
    def dot(u, v):
        return lax.dot_general(u, v, (dims, ((), ())), preferred_element_type=F32)

    return dot(a[0], b[0]) + (dot(a[0], b[1]) + dot(a[1], b[0]))


def exact(a, b, dims):
    return lax.dot_general(a, b, (dims, ((), ())), precision=lax.Precision.HIGHEST, preferred_element_type=F32)


def cost(flops, size):
    del flops, size
    return pl.CostEstimate(flops=1, bytes_accessed=1, transcendentals=0)


def big(*arrays):
    return sum(x.size for x in arrays) * 4 // 2**20 + 1


VMEM = pl.BlockSpec(memory_space=pltpu.VMEM)
SMEM = pl.BlockSpec(memory_space=pltpu.SMEM)
HBM = pl.BlockSpec(memory_space=pltpu.HBM)


def at_rows(i, step, count=1):
    start = i * step
    return pl.ds(start if isinstance(i, int) else pl.multiple_of(start, 16), step * count)


def cut_kernel(layout, step, at_ref, l_ref, *refs):
    outs, sems = refs[:-1], refs[-1]
    copies = []
    for out, places in zip(outs, layout, strict=True):
        for k, place in enumerate(places):
            copies.append(
                pltpu.make_async_copy(
                    l_ref.at[at_rows(at_ref[place], step)], out.at[at_rows(k, step)], sems.at[len(copies)]
                )
            )
    for copy in copies:
        copy.start()
    for copy in copies:
        copy.wait()


def cut_blocks(layout, step, at, logits):
    width = logits.shape[1]
    count = sum(len(places) for places in layout)
    return pl.pallas_call(
        functools.partial(cut_kernel, layout, step),
        in_specs=[SMEM, VMEM],
        out_specs=(HBM,) * len(layout),
        out_shape=tuple(jax.ShapeDtypeStruct((len(places) * step, width), F32) for places in layout),
        scratch_shapes=[pltpu.SemaphoreType.DMA((count,))],
        name="cut",
        compiler_params=room(big(logits) + 2),
        cost_estimate=cost(0, 8 * count * step * width),
    )(at, logits)


def by_cell_rows(ref, count, step):
    genes = ref.shape[1]
    return jnp.concatenate([ref[:count, :], ref[count : 2 * count, : step - genes]], axis=1)


def softmax_kernel(spots, scale, step, l_ref, inv_ref, cell_ref, o_ref, buffer, sem):
    cells, width = l_ref.shape
    genes = cell_ref.shape[1]
    count = cells // step

    def column(k, total):
        e = jnp.exp(l_ref[at_rows(k, step), :])
        return total + jnp.sum(e.reshape(step // 8, 8, width), axis=0)

    total = lax.fori_loop(0, count, column, jnp.zeros((8, width), F32))
    inv = 1.0 / jnp.sum(total, axis=0, keepdims=True)
    inv_ref[...] = inv
    ones = jnp.ones((16, width), BF16)

    def row(k, square):
        e = jnp.exp(l_ref[at_rows(k, step), :])
        share = e * inv
        buffer[at_rows(k, step), :] = e * scale
        pltpu.make_async_copy(buffer.at[at_rows(k, step)], o_ref.at[at_rows(k, step)], sem).start()
        high, low = split(share)
        sums = [lax.dot_general(ones, x, (((1,), (1,)), ((), ())), preferred_element_type=F32) for x in (high, low)]
        sums = (sums[0] + sums[1])[0:1, :] * (1.0 / spots)
        cell_ref[pl.ds(k, 1), :] = sums[:, :genes]
        cell_ref[pl.ds(count + k, 1), : step - genes] = sums[:, genes:]
        return square + jnp.sum((share * share).reshape(step // 8, 8, width), axis=0)

    square = lax.fori_loop(0, count, row, jnp.zeros((8, width), F32))
    cell_ref[count:, step - genes :] = jnp.full((count, 2 * genes - step), jnp.sum(square), F32)
    pltpu.make_async_copy(buffer, o_ref, sem).wait()


def softmax_sums(spots, genes, step, logits):
    cells, width = logits.shape
    return pl.pallas_call(
        functools.partial(softmax_kernel, spots, float(cells), step),
        in_specs=[VMEM],
        out_specs=(VMEM, VMEM, HBM),
        out_shape=(
            jax.ShapeDtypeStruct((1, width), F32),
            jax.ShapeDtypeStruct((2 * cells // step, genes), F32),
            pltpu.HBM((cells, width), F32),
        ),
        scratch_shapes=[pltpu.VMEM((cells, width), F32), pltpu.SemaphoreType.DMA],
        name="softmax",
        compiler_params=room(2 * big(logits) + 4),
        cost_estimate=cost(0, 0),
    )(logits)


def parts_kernel(step, x_ref, high_ref, low_ref, buffer, sems):
    count = x_ref.shape[0] // step

    def copy(k):
        return pltpu.make_async_copy(x_ref.at[at_rows(k, step)], buffer.at[at_rows(k, step)], sems.at[k])

    for k in range(count):
        copy(k).start()
    for k in range(count):
        copy(k).wait()
        high_ref[at_rows(k, step), :], low_ref[at_rows(k, step), :] = split(buffer[at_rows(k, step), :])


def parts_of(x, step):
    return pl.pallas_call(
        functools.partial(parts_kernel, step),
        in_specs=[HBM],
        out_specs=(VMEM, VMEM),
        out_shape=(pltpu.VMEM(x.shape, BF16), pltpu.VMEM(x.shape, BF16)),
        scratch_shapes=[pltpu.VMEM(x.shape, F32), pltpu.SemaphoreType.DMA((x.shape[0] // step,))],
        name="parts",
        compiler_params=room(12),
        cost_estimate=cost(4 * x.size, 8 * x.size),
    )(x)


def pred_kernel(jobs, n_acc, step, tail, at_ref, *refs):
    n_l = 1 + max(job[2] for job in jobs)
    n_given = max(job[1] for job in jobs)
    ls, xs, given, outs = refs[:n_l], refs[n_l : n_l + 4], refs[n_l + 4 :][:n_given], refs[-n_acc:]
    place = lambda at: at_ref[at[0]] if isinstance(at, list) else at
    for k in range(n_acc):
        acc = None
        for _, g, l, l_at, x, x_at, count in [job for job in jobs if job[0] == k]:
            if g:
                acc = given[g - 1][...]
            for c in range(count):
                e = split(jnp.exp(ls[l][at_rows(place(l_at) + c, step), :]))
                rows = at_rows(place(x_at) + c, step)
                term = three(e, (xs[2 * x][rows, :], xs[2 * x + 1][rows, :]), ((0,), (0,)))
                acc = term if acc is None else acc + term
        outs[k][: acc.shape[0], :] = acc
        if tail:
            outs[k][acc.shape[0] :, :] = refs[-n_acc - 1][...]


def pred_sums_of(jobs, n_acc, step, at, ls, xs, given, tail=()):
    width, genes = ls[0].shape[1], xs[0].shape[1]
    steps = sum(job[-1] for job in jobs)
    return pl.pallas_call(
        functools.partial(pred_kernel, jobs, n_acc, step, len(tail)),
        in_specs=[SMEM] + [VMEM] * (len(ls) + len(xs) + len(given) + len(tail)),
        out_specs=(VMEM,) * n_acc,
        out_shape=(jax.ShapeDtypeStruct((width + sum(x.shape[0] for x in tail), genes), F32),) * n_acc,
        name="pred",
        compiler_params=room(16),
        cost_estimate=cost(6 * steps * step * width * genes, 4 * steps * step * (width + genes)),
    )(at, *ls, *xs, *given, *tail)


def weights_of(mask_ref, counts_ref):
    weights = (mask_ref[...] * counts_ref[...]).astype(F32)
    return jnp.concatenate([weights, jnp.zeros((8 - SLIDES, weights.shape[1]), F32)], axis=0)


def column_of(row):
    return jnp.transpose(jnp.broadcast_to(row, (LANES, row.shape[1])))


def sums_kernel(n_parts, *refs):
    parts, (cells_ref, inv_ref, spatial_ref, ids_ref, mask_ref, counts_ref, pred_ref, wide_ref, spot_ref, q_ref) = (
        refs[:n_parts],
        refs[n_parts:],
    )
    spatial = spatial_ref[...]
    pred, q = parts[0][...], cells_ref[...]
    for part in parts[1:]:
        pred = pred + part[: pred.shape[0], :]
        q = q + part[pred.shape[0] :, :]
    q_ref[...] = q
    genes = pred.shape[1]
    pred = pred * jnp.concatenate([column_of(inv_ref[...])] * (genes // LANES), axis=1)
    pred_ref[...] = pred
    onehot = (lax.broadcasted_iota(jnp.int32, (8, LANES), 0) == ids_ref[...]).astype(F32)
    ones = jnp.ones((8, genes), F32)
    rows = lax.broadcasted_iota(jnp.int32, (8, LANES), 0)
    spot = jnp.where(rows == 3, jnp.sum(weights_of(mask_ref, counts_ref)), 0.0)
    for k, product in enumerate((pred * spatial, pred * pred, spatial * spatial)):
        wide_ref[8 * k : 8 * k + 8, :] = exact(onehot, product, ((1,), (0,)))
        spot = jnp.where(rows == k, exact(ones, product, ((1,), (1,))), spot)
    spot_ref[...] = spot


def pred_sums(n_parts, *args):
    parts, (by_cell, inv, spatial, ids, mask, counts) = args[:n_parts], args[n_parts:]
    width, genes = spatial.shape
    return pl.pallas_call(
        functools.partial(sums_kernel, n_parts),
        out_shape=(
            jax.ShapeDtypeStruct((width, genes), F32),
            jax.ShapeDtypeStruct((24, genes), F32),
            jax.ShapeDtypeStruct((8, width), F32),
            jax.ShapeDtypeStruct(by_cell.shape, F32),
        ),
        name="sums",
        compiler_params=room(12),
        cost_estimate=cost(10 * width * genes * 48, 4 * width * genes * 6),
    )(*parts, by_cell, inv, spatial, ids, mask, counts)


def dpred_kernel(spots, share_gene, *refs):
    wides, spot, refs = refs[:2], refs[2][...] + refs[3][...], refs[4:]
    pred_ref, spatial_ref, ids_ref, mask_ref, counts_ref, inv_ref, d_ref, tot_ref = refs
    weights = weights_of(mask_ref, counts_ref)
    genes = pred_ref.shape[1]
    a, b, c = (wides[0][8 * k : 8 * k + 8, :] + wides[1][8 * k : 8 * k + 8, :] for k in range(3))
    e, f, h, wsum = (spot[k : k + 1, :] for k in range(4))
    wsum = jnp.max(wsum)
    gain = weights / wsum
    inv_g = lax.rsqrt(b * c + 1e-06)
    inv_s = lax.rsqrt(f * h + 1e-06)
    grad_a = -gain * inv_g
    grad_b = gain * a * c * inv_g * inv_g * inv_g
    onehot = (lax.broadcasted_iota(jnp.int32, (8, LANES), 0) == ids_ref[...]).astype(F32)
    wide = functools.partial(jnp.concatenate, axis=1)
    by_spatial = exact(onehot, grad_a, ((0,), (0,))) - wide([column_of(inv_s / spots)] * (genes // LANES))
    by_pred = exact(onehot, grad_b, ((0,), (0,))) + wide(
        [column_of(e * h * inv_s * inv_s * inv_s / spots)] * (genes // LANES)
    )
    pred = pred_ref[...]
    dpred = by_spatial * spatial_ref[...] + by_pred * pred
    inv = inv_ref[...]
    d_ref[:LANES, :] = dpred * wide([column_of(inv)] * (genes // LANES))
    own = exact(jnp.ones((8, genes), F32), pred * dpred, ((1,), (1,))) * inv
    d_ref[LANES:, :] = wide([own] * (genes // LANES))
    rows = lax.broadcasted_iota(jnp.int32, (8, LANES), 0)
    tot = jnp.where(rows == 0, jnp.sum(weights * a * inv_g), 0.0)
    tot = jnp.where(rows == 1, jnp.sum(e * inv_s), tot)
    tot = jnp.where(rows == 2, jnp.sum(f), tot)
    tot_ref[...] = jnp.where(rows == 3, wsum * share_gene, tot)


def dpred_scaled(spots, share_gene, *args):
    spatial = args[5]
    width, genes = spatial.shape
    return pl.pallas_call(
        functools.partial(dpred_kernel, spots, share_gene),
        out_shape=(
            jax.ShapeDtypeStruct((width + 8, genes), F32),
            jax.ShapeDtypeStruct((8, width), F32),
        ),
        name="dpred",
        compiler_params=room(12),
        cost_estimate=cost(10 * width * genes * 48, 4 * width * genes * 6),
    )(*args)


def dmap_kernel(ranges, n, *refs):
    xs, ds, outs = refs[:4], refs[4 : 4 + n], refs[-n:]
    parts = [split(d[:LANES, :]) for d in ds]
    d = tuple(jnp.concatenate([part[i] for part in parts], axis=0) for i in range(2))
    own = jnp.concatenate([d[LANES : LANES + 1, :LANES] for d in ds], axis=1)
    at = 0
    for x, first, count in ranges:
        here = pl.ds(first, count)
        value = three((xs[2 * x][here, :], xs[2 * x + 1][here, :]), d, ((1,), (1,))) - own
        for i, out in enumerate(outs):
            out[at : at + count, :] = value[:, i * LANES : (i + 1) * LANES]
        at += count
    if len(refs) > 4 + 2 * n:
        for out in outs:
            out[at:, :] = refs[4 + n][...]


def dmap_blocks(ranges, ds, xs, tail=()):
    width = ds[0].shape[0] - 8
    rows = sum(count for _, _, count in ranges) + 8 * len(tail)
    return pl.pallas_call(
        functools.partial(dmap_kernel, ranges, len(ds)),
        in_specs=[VMEM] * (4 + len(ds) + len(tail)),
        out_specs=(VMEM,) * len(ds),
        out_shape=(jax.ShapeDtypeStruct((rows, width), F32),) * len(ds),
        name="dmap",
        compiler_params=room(16),
        cost_estimate=cost(0, 0),
    )(*xs, *ds, *tail)


def egrad_kernel(scale, ks, step, wheres, n_add, at_ref, *refs):
    n = len(wheres)
    counts = [2 if isinstance(where, tuple) else 1 for where in wheres]
    ls, ds, adds, o_ref = refs[: sum(counts)], refs[sum(counts) : sum(counts) + n], refs[sum(counts) + n : -1], refs[-1]
    parts = [split(d[:LANES, :]) for d in ds]
    d = tuple(jnp.concatenate([part[i] for part in parts], axis=0) for i in range(2))
    for j, k in enumerate(ks):
        es, at = [], 0
        for where, number in zip(wheres, counts, strict=True):
            if number == 2:
                mine, others = (ls[at + i][at_rows(where[i], step), :] for i in range(2))
                l = jnp.where(at_ref[0] == k, mine, others)
            else:
                l = ls[at][at_rows(where + k, step), :]
            at += number
            es.append(jnp.exp(l))
        value = three(split(jnp.concatenate(es, axis=1)), d, ((1,), (0,))) * scale
        o_ref[at_rows(j, step), :] = value + adds[j][...] if n_add else value


def egrad_part(ks, step, wheres, scale, at, ls, ds, adds=()):
    genes = ds[0].shape[1]
    return pl.pallas_call(
        functools.partial(egrad_kernel, scale, ks, step, wheres, len(adds)),
        in_specs=[SMEM] + [VMEM] * (len(ls) + len(ds) + len(adds)),
        out_specs=VMEM,
        out_shape=jax.ShapeDtypeStruct((len(ks) * step, genes), F32),
        name="egrad",
        compiler_params=room(big(*ls, *ds, *adds) + 24),
        cost_estimate=cost(0, 0),
    )(at, *ls, *ds, *adds)


def ratio_kernel(spots, scale, cell_ref, density_ref, inv_ref, a_ref, _, ratio_ref, sum_ref, kl_ref, a, sems):
    inv = inv_ref[...]
    count, step = density_ref.shape

    def load(k):
        return pltpu.make_async_copy(a_ref.at[at_rows(k, step)], a.at[at_rows(k, step)], sems.at[k])

    for k in range(count):
        load(k).start()
    density = density_ref[...]
    target = density / jnp.sum(density)
    q = by_cell_rows(cell_ref, count, step)
    ratios = target / q / spots
    ratio_ref[...] = ratios
    kl_ref[...] = jnp.full(kl_ref.shape, jnp.sum(target * (jnp.log(target) - jnp.log(q))))
    rows = lax.broadcasted_iota(jnp.int32, (16, step), 0)
    total = jnp.zeros((1, LANES), F32)
    for k in range(count):
        load(k).wait()
        high, low = split(ratios[k : k + 1, :])
        lhs = jnp.where(rows == 0, high.astype(F32), jnp.where(rows == 1, low.astype(F32), 0.0)).astype(BF16)
        for part in split(a[at_rows(k, step), :]):
            sums = lax.dot_general(lhs, part, (((1,), (0,)), ((), ())), preferred_element_type=F32)
            total = total + (sums[0:1, :] + sums[1:2, :])
    sum_ref[...] = jnp.broadcast_to(total * (inv * inv * (1.0 / scale)), sum_ref.shape)


def ratio_part(spots, by_cell, density, inv, a):
    cells, width = a.shape
    return pl.pallas_call(
        functools.partial(ratio_kernel, spots, float(cells)),
        in_specs=[VMEM, VMEM, VMEM, HBM],
        out_specs=(HBM, VMEM, VMEM, VMEM),
        out_shape=(
            pltpu.HBM((cells, width), F32),
            jax.ShapeDtypeStruct(density.shape, F32),
            jax.ShapeDtypeStruct((8, width), F32),
            jax.ShapeDtypeStruct((8, width), F32),
        ),
        scratch_shapes=[pltpu.VMEM((cells, width), F32), pltpu.SemaphoreType.DMA((density.shape[0],))],
        input_output_aliases={3: 0},
        name="ratio",
        compiler_params=room(big(a) + 8),
        cost_estimate=cost(0, 0),
    )(by_cell, density, inv, a)


def join_kernel(a_ref, b_ref, o_ref):
    half = a_ref.shape[0]
    o_ref[:half, :] = a_ref[...]
    o_ref[half:, :] = b_ref[...]


def join(a, b):
    return pl.pallas_call(
        join_kernel,
        in_specs=[VMEM, VMEM],
        out_specs=VMEM,
        out_shape=jax.ShapeDtypeStruct((2 * a.shape[0], a.shape[1]), F32),
        name="join",
        compiler_params=room(8),
        cost_estimate=cost(0, 0),
    )(a, b)


def add_kernel(a_ref, b_ref, o_ref):
    o_ref[...] = a_ref[...] + b_ref[: o_ref.shape[0], :]


def plus(a, b):
    return pl.pallas_call(
        add_kernel,
        in_specs=[VMEM, VMEM],
        out_specs=VMEM,
        out_shape=jax.ShapeDtypeStruct(a.shape, F32),
        name="add",
        compiler_params=room(8),
        cost_estimate=cost(0, 0),
    )(a, b)


def add_all_kernel(*refs):
    total = refs[0][...]
    for ref in refs[1:-1]:
        total = total + ref[...]
    refs[-1][...] = total


def add_all(*arrays):
    return pl.pallas_call(
        add_all_kernel,
        in_specs=[VMEM] * len(arrays),
        out_specs=VMEM,
        out_shape=jax.ShapeDtypeStruct(arrays[0].shape, F32),
        name="add_all",
        compiler_params=room(8),
        cost_estimate=cost(0, 0),
    )(*arrays)


def next_kernel(cuts, end_ref, s_ref, y_ref, *refs):
    blocks, (t_ref, o_ref, c_ref) = refs[:-3], refs[-3:]
    total = s_ref[...] + y_ref[...]
    t_ref[...] = total
    at = 0
    for block, (first, count) in zip(blocks, cuts, strict=True):
        c_ref[at : at + count, :] = block[first : first + count, :]
        at += count
    own = c_ref[...]
    both = min(at, total.shape[0])
    o_ref[:both, :] = jnp.where(end_ref[0] == 1, own[:both, :], total[:both, :])
    if o_ref.shape[0] > both:
        o_ref[both:, :] = (own if at > both else total)[both:, :]


def next_piece(cuts, end, s, y, *blocks):
    size, width = sum(count for _, count in cuts), s.shape[1]
    return pl.pallas_call(
        functools.partial(next_kernel, cuts),
        in_specs=[SMEM] + [VMEM] * (2 + len(blocks)),
        out_specs=(VMEM, VMEM, VMEM),
        out_shape=(
            jax.ShapeDtypeStruct(s.shape, F32),
            jax.ShapeDtypeStruct((max(size, s.shape[0]), width), F32),
            jax.ShapeDtypeStruct((size, width), F32),
        ),
        name="next",
        compiler_params=room(10),
        cost_estimate=cost(0, 0),
    )(end, s, y, *blocks)


def final_kernel(place, cuts, step, end_ref, at_ref, *refs):
    n, m = len(cuts), 1 + max(k for half in cuts for k, _, _ in half)
    rxs, ss = refs[:m], refs[m : 2 * m]
    ratio_ref, sum_ref, inv_ref, a_ref, _, _, o_ref, a, b, sems = refs[2 * m :]
    load = pltpu.make_async_copy(a_ref.at[at_rows(at_ref[place], step, n)], a, sems.at[n])
    load.start()
    rows = lax.broadcasted_iota(jnp.int32, (16, step), 0)
    ones = (lax.broadcasted_iota(jnp.int32, (16, LANES), 0) < 3).astype(BF16)
    stores = []
    for k in range(n):
        at, here = at_ref[place] + k, at_rows(k, step)
        ratio = ratio_ref[pl.ds(at, 1), :]
        high = ratio.astype(BF16).astype(F32)
        mid = (ratio - high).astype(BF16).astype(F32)
        terms = jnp.where(rows == 0, high, jnp.where(rows == 1, mid, jnp.where(rows == 2, ratio - high - mid, 0.0)))
        column = lax.dot_general(terms.astype(BF16), ones, (((0,), (0,)), ((), ())), preferred_element_type=F32)
        whole = jnp.concatenate(
            [
                jnp.where(end_ref[0] == 1, rxs[i][first : first + count, :], ss[i][first : first + count, :])
                for i, first, count in cuts[k]
            ],
            axis=0,
        )
        value = whole + (sum_ref[0:1, :] - column * inv_ref[...])
        if k == 0:
            load.wait()
        b[here, :] = a[here, :] * value
        stores.append(pltpu.make_async_copy(b.at[here], o_ref.at[at_rows(at, step)], sems.at[k]))
        stores[-1].start()
    for store in stores:
        store.wait()


def final_block(step, cuts, place, end, at, rxs, ss, ratio, ratio_sum, inv, a, grad):
    width = a.shape[1]
    n, m = len(cuts), len(ss)
    return pl.pallas_call(
        functools.partial(final_kernel, place, cuts, step),
        in_specs=[SMEM, SMEM] + [VMEM] * (2 * m + 3) + [HBM, HBM],
        out_specs=(HBM, HBM),
        out_shape=(pltpu.HBM(a.shape, F32), pltpu.HBM(grad.shape, F32)),
        scratch_shapes=[pltpu.VMEM((n * step, width), F32)] * 2 + [pltpu.SemaphoreType.DMA((1 + n,))],
        input_output_aliases={5 + 2 * m: 0, 6 + 2 * m: 1},
        name="final",
        compiler_params=room(12),
        cost_estimate=cost(0, 0),
    )(end, at, *rxs, *ss, ratio, ratio_sum, inv, a, grad)


def blank(shape):
    return pl.pallas_call(lambda o_ref: None, out_specs=HBM, out_shape=pltpu.HBM(shape, F32), name="blank")()


def scalars_kernel(n, cells, spots, step, end_ref, *refs):
    sums = [refs[k][-8:, :] for k in range(n)]
    rx_ref, s_ref, q_ref, kl_ref, loss_ref, map_ref, pred_ref = refs[n:]
    while len(sums) > 1:
        sums = [a + b for a, b in zip(sums[::2], sums[1::2], strict=True)]
    by_gene = jnp.where(end_ref[0] == 1, rx_ref[step : step + 8, :], s_ref[step : step + 8, :])
    cosine, fitted, wsum, scos = by_gene[0:1, :], sums[0][2:3, :], by_gene[3:4, :], sums[0][1:2, :]
    loss = -cosine / wsum - scos / spots + kl_ref[0:1, :]
    rms_map = jnp.sqrt(q_ref[q_ref.shape[0] - 1 :, q_ref.shape[1] - LANES :] / (cells * spots))
    rms_pred = jnp.sqrt(fitted / (spots * GENES))
    for ref, value in zip((loss_ref, map_ref, pred_ref), (loss, rms_map, rms_pred), strict=True):
        ref[0, 0] = jnp.max(value)


def scalar_results(n, cells, spots, step, end, *args):
    return pl.pallas_call(
        functools.partial(scalars_kernel, n, cells, spots, step),
        in_specs=[SMEM] + [VMEM] * len(args),
        out_specs=(SMEM,) * 3,
        out_shape=(jax.ShapeDtypeStruct((1, 1), F32),) * 3,
        name="scalars",
        compiler_params=room(24),
        cost_estimate=cost(0, 0),
    )(end, *args)


def shards(logits, expression, spatial, density, gene_mask, gene_counts, slide_ids):
    n_blk = lax.axis_size("blk")
    n_gene = lax.axis_size("gene")
    me = lax.axis_index("blk")
    plane = lax.axis_index("gene")
    cells, width = logits.shape
    rows, genes = expression.shape
    half = rows // 2
    spots = width * n_blk
    order = Order()

    def swap(x, m):
        return lax.ppermute(x, "blk", [(i, i ^ m) for i in range(n_blk)])

    def across(x, m):
        return lax.ppermute(x, "gene", [(i, i ^ m) for i in range(n_gene)])

    def cut(l, r, first, size):
        return lax.dynamic_slice_in_dim(l, (me ^ r) * rows + first, size, 0)

    far = sorted(range(2, n_blk, 2), key=lambda m: (m.bit_count(), m))
    side = plane % 2
    at = jnp.stack([side, 1 - side, *[(me ^ r) * 2 + k for r in range(n_blk) for k in range(2)]]
        + [(me ^ r) * 2 + side for r in range(n_blk)]).astype(jnp.int32)

    def whole(r):
        return (2 + 2 * r, 3 + 2 * r)

    def mine(r):
        return (2 + 2 * n_blk + r,)

    sent, passed, held = {}, {}, {}

    other = swap(expression, 1)
    constants = (slide_ids[None, :], gene_mask, gene_counts[None, :])
    n_q = cells // genes

    def add_pred(jobs, n_acc, ls, given=(), tail=()):
        n, g = len(ls), len(given)

        def run(*a):
            return pred_sums_of(jobs, n_acc, half, at, a[:n], a[n + g : n + g + 4], a[n : n + g], a[n + g + 4 :])

        return order(run, (*ls, *given), (*own_x, *other_x, *tail))

    def cuts(*layout):
        return order(lambda l: cut_blocks(layout, half, at, l), (logits,))

    if n_blk == 8 and n_gene == 4:
        near3, near5 = order(
            lambda l: [lax.dynamic_slice_in_dim(l, (me ^ r) * rows + side * half, half, 0) for r in (3, 5)], (logits,)
        )
        sent[3], sent[5] = swap(near3, 2), swap(near5, 4)
        own_x = order(lambda x: parts_of(x, half), (expression,))
        both, near2, near4, stay = cuts(mine(6) + mine(7), whole(2), whole(4), whole(0) + whole(1))
        passed[3] = across(order(join, (sent[3], sent[5])), 1)
        sent[6], sent[2], sent[4] = swap(order.here(both), 6), swap(order.here(near2), 2), swap(order.here(near4), 4)
        inv, by_cell, scale = order(functools.partial(softmax_sums, spots, genes, half), (logits,))
        other_x = order(lambda x: parts_of(x, half), (other,))
        (acc0,) = add_pred(((0, 0, 0, 0, 0, 0, 2), (0, 0, 0, 2, 1, 0, 2)), 1, (stay,))
        acc2, acc4 = add_pred(((0, 0, 0, 0, 1, [0], 1), (1, 0, 1, 0, 1, [0], 1)), 2, (sent[3], sent[5]))
        cell_moved = swap(order.here(by_cell), 1)
        passed[6] = across(order.here(sent[6]), 1)
        (acc6,) = add_pred(((0, 0, 0, 0, 0, [0], 1), (0, 0, 0, 1, 1, [0], 1)), 1, (sent[6],))
        acc2, acc4 = add_pred(
            ((0, 1, 0, 0, 1, [1], 1), (1, 2, 0, 1, 1, [1], 1)), 2, (passed[3],), (acc2, acc4)
        )
        by_cell = order(plus, (by_cell, cell_moved))
        (acc2,) = add_pred(((0, 1, 0, 0, 0, 0, 2),), 1, (sent[2],), (acc2,), (by_cell,))
        moved = {2: swap(acc2, 2)}
        (acc4,) = add_pred(((0, 1, 0, 0, 0, 0, 2),), 1, (sent[4],), (acc4,), (by_cell,))
        moved[4] = swap(acc4, 4)
        (acc6,) = add_pred(((0, 1, 0, 0, 0, [1], 1), (0, 0, 0, 1, 1, [1], 1)), 1, (passed[6],), (acc6,), (by_cell,))
        moved[6] = swap(acc6, 6)
        held = {
            2: ((sent[2],), 0),
            3: ((sent[3], passed[3]), (0, 0)),
            4: ((sent[4],), 0),
            5: ((sent[5], passed[3]), (0, 1)),
            6: ((sent[6], passed[6]), (0, 0)),
            7: ((sent[6], passed[6]), (1, 1)),
        }
    else:
        inv, by_cell, scale = order(functools.partial(softmax_sums, spots, genes, half), (logits,))
        by_cell = order(plus, (by_cell, swap(by_cell, 1)))
        own_x = order(lambda x: parts_of(x, half), (expression,))
        other_x = order(lambda x: parts_of(x, half), (other,))
        (stay,) = cuts(whole(0) + whole(1))
        (acc0,) = add_pred(((0, 0, 0, 0, 0, 0, 2), (0, 0, 0, 2, 1, 0, 2)), 1, (stay,))
        moved = {}
        for m in far:
            blocks = cuts(whole(m), whole(m + 1))
            for r in (m, m + 1):
                sent[r] = swap(blocks[r - m], m)
                held[r] = ((sent[r],), 0)
            (acc,) = add_pred(((0, 0, 0, 0, 0, 0, 2), (0, 0, 1, 0, 1, 0, 2)), 1, (sent[m], sent[m + 1]), (), (by_cell,))
            moved[m] = swap(acc, m)
    held[0], held[1] = ((stay,), 0), ((stay,), 2)

    parts = [acc0] + [moved[m] for m in far]
    pred, wide, spot, by_cell = order(
        functools.partial(pred_sums, len(parts)), parts, (by_cell, inv, spatial, *constants)
    )
    density = density.reshape(cells // half, half)
    state = {"scale": scale, "grad": blank((cells, width))}

    spot_moved = across(spot, 1)
    m = 1
    while 2 * m < n_blk:
        wide = order(plus, (wide, swap(wide, m)))
        m *= 2
        if m == 2:
            spot = order(add_all, (spot, spot_moved))
            spot_moved = across(spot, 2)
    wide_moved = swap(wide, m)
    grad, tot = order(
        functools.partial(dpred_scaled, spots, 1.0 / n_gene),
        (wide, wide_moved, spot, spot_moved),
        (pred, spatial, *constants, inv),
    )
    grads, back, tails = {0: grad}, {}, {}

    def dmap(ms, ranges, wait=(), tail=()):
        outs = order(
            lambda *a: dmap_blocks(ranges, a[: len(ms)], a[len(ms) : len(ms) + 4], a[len(ms) + 4 :]),
            [grads[m] for m in ms],
            (*own_x, *other_x, *tail),
            wait,
        )
        if tail and ms != (0,):
            tails.update({m: swap(d, m) for m, d in zip(ms, outs, strict=True)})
            return [tails[m] for m in ms]
        return [swap(d, m) if m else d for m, d in zip(ms, outs, strict=True)]

    def block_rows(odd):
        return ((odd, 0, half), (odd, half, half))

    blocks = [0, 1, 2, 4, 3, 5, 6, 7] if n_blk == 8 else [r for m in [0, *far] for r in (m, m + 1)]
    long = 848
    short = 2 * rows // 3 // 16 * 16
    sizes = [2 * rows - 2 * short, short, short] + [long] * ((cells - 2 * rows) // long)
    sizes += [n for n in [cells - sum(sizes)] if n]
    starts = [sum(sizes[:t]) for t in range(len(sizes))]
    count, lag = len(sizes), 3
    assert starts[3] == 2 * rows and sum(sizes) == cells

    def overlap(first, size, cuts_at, cuts_size):
        found = []
        for k, (a, n) in enumerate(zip(cuts_at, cuts_size, strict=True)):
            low, high = max(first, a), min(first + size, a + n)
            if low < high:
                found.append((k, low - a, high - low))
        return found

    block_starts, block_sizes = [rows * k for k in range(len(blocks))], [rows] * len(blocks)
    part, total_of, mid, got, own = {}, {}, {}, {}, {}
    end = jnp.reshape((plane == 0) | (plane == n_gene - 1), (1,)).astype(jnp.int32)

    def send(t):
        if t >= count + lag:
            return
        if t < lag:
            ranges = overlap(starts[t], sizes[t], (0, rows), (rows, rows))
            own[t] = buffer = dmap((0,), tuple(ranges), (), (tot,) if t == 0 else ())[0]
        elif t < count:
            found = overlap(starts[t], sizes[t], block_starts, block_sizes)
            cuts = tuple((back[blocks[k]][1] + first, n) for k, first, n in found)
            total_of[t - lag], buffer, own[t] = order(
                lambda s, y, *b: next_piece(cuts, end, s, y, *b),
                (part[t - lag], mid[t - lag], *[back[blocks[k]][0] for k, _, _ in found]),
            )
        else:
            buffer = total_of[t - lag] = order(plus, (part[t - lag], mid[t - lag]))
        got[t] = lax.ppermute(buffer, "gene", PAIR)

    def finish(k):
        halves = [overlap(block_starts[k] + half * h, half, starts, sizes) for h in range(2)]
        ts = sorted({t for found in halves for t, _, _ in found})
        cuts = tuple(tuple((ts.index(t), first, n) for t, first, n in found) for found in halves)
        m = len(ts)
        state["scale"], state["grad"] = order(
            lambda *a: final_block(half, cuts, 2 + 2 * blocks[k], end, at, a[:m], a[m : 2 * m], *a[2 * m :]),
            (*[got[t + lag] for t in ts], *[total_of[t] for t in ts]),
            (state["ratio"], state["ratio_sum"], inv, state["scale"], state["grad"]),
        )

    last_piece = [max(t for t, _, _ in overlap(a, rows, starts, sizes)) for a in block_starts]

    def expr_part(odd, ks, adds=()):
        ms = [0, *far]
        ls = [l for m in ms for l in held[m + odd][0]]
        wheres = [held[m + odd][1] for m in ms]
        n, m = len(ls), len(adds)
        return order(
            lambda d, *a: egrad_part(ks, half, wheres, float(cells), at, a[m : m + n], (d, *a[m + n :]), a[:m]),
            (grads[0], *adds),
            (*ls, *[grads[m] for m in far]),
        )

    def first_dmap():
        if n_blk == 8:
            for r, d in zip((2, 4), dmap((2, 4), block_rows(0)), strict=True):
                back[r] = (d, 0)
        else:
            tails[0] = order(plus, (tot, tot_moved))
            for m in far:
                (d,) = dmap((m,), block_rows(0) + block_rows(1), (), (tails[0],))
                back[m], back[m + 1] = (d, 0), (d, rows)

    def second_dmap():
        if n_blk == 8:
            tails[0] = order(plus, (tot, tot_moved))
            for r, d in zip((3, 5), dmap((2, 4), block_rows(1), (back[2][0], back[4][0]), (tails[0],)), strict=True):
                back[r] = (d, 0)

    def third_dmap():
        if n_blk == 8:
            back[6] = (dmap((6,), block_rows(0), (back[3][0], back[5][0]))[0], 0)

    def fourth_dmap():
        if n_blk == 8:
            back[7] = (dmap((6,), block_rows(1), (), (tails[0],))[0], 0)

    def kl():
        state["scale"], state["ratio"], state["ratio_sum"], state["kl"] = order(
            functools.partial(ratio_part, spots), (by_cell,), (density, inv, state["scale"])
        )

    def egrad(k):
        state["swapped", k] = swap(expr_part(1, (k,)), 1)

    def scalars():
        state["scalars"] = order(
            functools.partial(scalar_results, n_blk // 2, cells, spots, sizes[0], end),
            (*[tails[m] for m in range(0, n_blk, 2)], got[lag], total_of[0], by_cell),
            (state["kl"],),
        )

    def expr():
        state["expr"] = expr_part(0, (0, 1), (state["swapped", 0], state["swapped", 1]))

    plan = {
        (0, "between"): [first_dmap],
        (1, "after"): [kl],
        (2, "between"): [second_dmap],
        (5, "between"): [third_dmap],
        (7, "between"): [fourth_dmap, functools.partial(egrad, 0)],
        (8, "between"): [functools.partial(egrad, 1)],
        (count, "between"): [scalars],
        (count + 1, "between"): [expr],
    }
    for k in range(len(blocks)):
        t = last_piece[k] + lag + 1
        if t < count + lag:
            plan.setdefault((t, "between"), []).append(functools.partial(finish, k))

    def extra(t, place):
        for step in plan.get((t, place), ()):
            step()

    send(0)
    for m in far:
        grads[m] = swap(order.here(grad), m)
    tot_moved = swap(order.here(tot), 1)
    for t in range(count + lag):
        extra(t, "before")
        send(t + 1)
        extra(t, "between")
        if t < count:
            part[t] = order(plus, (own[t], got[t]))
            mid[t] = lax.ppermute(part[t], "gene", MIDDLE)
        extra(t, "after")
    for k in range(len(blocks)):
        if last_piece[k] + lag + 1 >= count + lag:
            finish(k)
    loss, rms_map, rms_pred = (x[0, 0] for x in state["scalars"])
    return (loss, state["grad"], state["expr"], rms_map, rms_pred)


def solution(mesh):
    placed = (
        P(None, "blk"),
        P("blk", "gene"),
        P("blk", "gene"),
        P(),
        P(None, "gene"),
        P("gene"),
        P("blk"),
    )
    return jax.shard_map(
        shards,
        mesh=mesh,
        in_specs=placed,
        out_specs=(P(), P(None, "blk"), P("blk", "gene"), P(), P()),
        check_vma=False,
    )
```

```python
import functools

import jax
import jax.numpy as jnp
from jax import lax
from jax.experimental import pallas as pl
from jax.experimental.pallas import tpu as pltpu
from jax.sharding import PartitionSpec as P

GENES = 2048
SLIDES = 4
LANES = 128
F32 = jnp.float32
BF16 = jnp.bfloat16
PAIR = [(0, 1), (1, 0), (2, 3), (3, 2)]
MIDDLE = [(1, 2), (2, 1)]


def room(mib):
    return pltpu.CompilerParams(vmem_limit_bytes=mib * 1024 * 1024)


class Order:
    def __init__(self):
        self.last = None

    def __call__(self, step, fresh, const=(), wait=()):
        gate = [*wait] if self.last is None else [self.last, *wait]
        if gate:
            fresh = lax.optimization_barrier((*fresh, *gate))[: len(fresh)]
        out = step(*fresh, *const)
        self.last = out[0] if isinstance(out, (tuple, list)) else out
        return out

    def here(self, x):
        return lax.optimization_barrier((x, self.last))[0]


def split(x):
    high = x.astype(BF16)
    return high, (x - high.astype(F32)).astype(BF16)


def three(a, b, dims):
    def dot(u, v):
        return lax.dot_general(u, v, (dims, ((), ())), preferred_element_type=F32)

    return dot(a[0], b[0]) + (dot(a[0], b[1]) + dot(a[1], b[0]))


def exact(a, b, dims):
    return lax.dot_general(a, b, (dims, ((), ())), precision=lax.Precision.HIGHEST, preferred_element_type=F32)


def cost(flops, size):
    del flops, size
    return pl.CostEstimate(flops=1, bytes_accessed=1, transcendentals=0)


def big(*arrays):
    return sum(x.size for x in arrays) * 4 // 2**20 + 1


VMEM = pl.BlockSpec(memory_space=pltpu.VMEM)
SMEM = pl.BlockSpec(memory_space=pltpu.SMEM)
HBM = pl.BlockSpec(memory_space=pltpu.HBM)


def at_rows(i, step, count=1):
    start = i * step
    return pl.ds(start if isinstance(i, int) else pl.multiple_of(start, 16), step * count)


def cut_kernel(layout, step, at_ref, l_ref, *refs):
    outs, sems = refs[:-1], refs[-1]
    copies = []
    for out, places in zip(outs, layout, strict=True):
        for k, place in enumerate(places):
            copies.append(
                pltpu.make_async_copy(
                    l_ref.at[at_rows(at_ref[place], step)], out.at[at_rows(k, step)], sems.at[len(copies)]
                )
            )
    for copy in copies:
        copy.start()
    for copy in copies:
        copy.wait()


def cut_blocks(layout, step, at, logits):
    width = logits.shape[1]
    count = sum(len(places) for places in layout)
    return pl.pallas_call(
        functools.partial(cut_kernel, layout, step),
        in_specs=[SMEM, VMEM],
        out_specs=(HBM,) * len(layout),
        out_shape=tuple(jax.ShapeDtypeStruct((len(places) * step, width), F32) for places in layout),
        scratch_shapes=[pltpu.SemaphoreType.DMA((count,))],
        name="cut",
        compiler_params=room(big(logits) + 2),
        cost_estimate=cost(0, 8 * count * step * width),
    )(at, logits)


def by_cell_rows(ref, count, step):
    genes = ref.shape[1]
    rest = [ref[count : count + count // 2, at : at + step - genes] for at in (0, genes // 2)]
    return jnp.concatenate([ref[:count, :], jnp.concatenate(rest, axis=0)], axis=1)


def softmax_kernel(spots, scale, step, l_ref, inv_ref, cell_ref, o_ref, buffer, sem):
    cells, width = l_ref.shape
    genes = cell_ref.shape[1]
    count = cells // step

    def column(k, total):
        e = jnp.exp(l_ref[at_rows(k, step), :])
        return total + jnp.sum(e.reshape(step // 8, 8, width), axis=0)

    total = lax.fori_loop(0, count, column, jnp.zeros((8, width), F32))
    inv = 1.0 / jnp.sum(total, axis=0, keepdims=True)
    inv_ref[...] = inv
    ones = jnp.ones((16, width), BF16)

    def row(at, k, square):
        e = jnp.exp(l_ref[at_rows(k, step), :])
        share = e * inv
        buffer[at_rows(k, step), :] = e * scale
        pltpu.make_async_copy(buffer.at[at_rows(k, step)], o_ref.at[at_rows(k, step)], sem).start()
        high, low = split(share)
        sums = [lax.dot_general(ones, x, (((1,), (1,)), ((), ())), preferred_element_type=F32) for x in (high, low)]
        sums = (sums[0] + sums[1])[0:1, :] * (1.0 / spots)
        cell_ref[pl.ds(k, 1), :] = sums[:, :genes]
        cell_ref[pl.ds(count + k - at * (count // 2), 1), at * (genes // 2) : at * (genes // 2) + step - genes] = sums[:, genes:]
        return square + jnp.sum((share * share).reshape(step // 8, 8, width), axis=0)

    square = lax.fori_loop(0, count // 2, functools.partial(row, 0), jnp.zeros((8, width), F32))
    square = lax.fori_loop(count // 2, count, functools.partial(row, 1), square)
    for at in (0, genes // 2):
        left = genes // 2 - (step - genes)
        cell_ref[count:, at + step - genes : at + genes // 2] = jnp.full((count // 2, left), jnp.sum(square), F32)
    pltpu.make_async_copy(buffer, o_ref, sem).wait()


def softmax_sums(spots, genes, step, logits):
    cells, width = logits.shape
    return pl.pallas_call(
        functools.partial(softmax_kernel, spots, float(cells), step),
        in_specs=[VMEM],
        out_specs=(VMEM, VMEM, HBM),
        out_shape=(
            jax.ShapeDtypeStruct((1, width), F32),
            jax.ShapeDtypeStruct((3 * cells // (2 * step), genes), F32),
            pltpu.HBM((cells, width), F32),
        ),
        scratch_shapes=[pltpu.VMEM((cells, width), F32), pltpu.SemaphoreType.DMA],
        name="softmax",
        compiler_params=room(2 * big(logits) + 4),
        cost_estimate=cost(0, 0),
    )(logits)


def parts_kernel(step, x_ref, high_ref, low_ref, buffer, sems):
    count = x_ref.shape[0] // step

    def copy(k):
        return pltpu.make_async_copy(x_ref.at[at_rows(k, step)], buffer.at[at_rows(k, step)], sems.at[k])

    for k in range(count):
        copy(k).start()
    for k in range(count):
        copy(k).wait()
        high_ref[at_rows(k, step), :], low_ref[at_rows(k, step), :] = split(buffer[at_rows(k, step), :])


def parts_of(x, step):
    return pl.pallas_call(
        functools.partial(parts_kernel, step),
        in_specs=[HBM],
        out_specs=(VMEM, VMEM),
        out_shape=(pltpu.VMEM(x.shape, BF16), pltpu.VMEM(x.shape, BF16)),
        scratch_shapes=[pltpu.VMEM(x.shape, F32), pltpu.SemaphoreType.DMA((x.shape[0] // step,))],
        name="parts",
        compiler_params=room(12),
        cost_estimate=cost(4 * x.size, 8 * x.size),
    )(x)


def pred_kernel(jobs, n_acc, step, tail, at_ref, *refs):
    n_l = 1 + max(job[2] for job in jobs)
    n_given = max(job[1] for job in jobs)
    ls, xs, given, outs = refs[:n_l], refs[n_l : n_l + 4], refs[n_l + 4 :][:n_given], refs[-n_acc:]
    place = lambda at: at_ref[at[0]] if isinstance(at, list) else at
    for k in range(n_acc):
        acc = None
        for _, g, l, l_at, x, x_at, count in [job for job in jobs if job[0] == k]:
            if g:
                acc = given[g - 1][...]
            for c in range(count):
                e = split(jnp.exp(ls[l][at_rows(place(l_at) + c, step), :]))
                rows = at_rows(place(x_at) + c, step)
                term = three(e, (xs[2 * x][rows, :], xs[2 * x + 1][rows, :]), ((0,), (0,)))
                acc = term if acc is None else acc + term
        outs[k][: acc.shape[0], :] = acc
        if tail:
            outs[k][acc.shape[0] :, :] = refs[-n_acc - 1][...]


def pred_sums_of(jobs, n_acc, step, at, ls, xs, given, tail=()):
    width, genes = ls[0].shape[1], xs[0].shape[1]
    steps = sum(job[-1] for job in jobs)
    return pl.pallas_call(
        functools.partial(pred_kernel, jobs, n_acc, step, len(tail)),
        in_specs=[SMEM] + [VMEM] * (len(ls) + len(xs) + len(given) + len(tail)),
        out_specs=(VMEM,) * n_acc,
        out_shape=(jax.ShapeDtypeStruct((width + sum(x.shape[0] for x in tail), genes), F32),) * n_acc,
        name="pred",
        compiler_params=room(16),
        cost_estimate=cost(6 * steps * step * width * genes, 4 * steps * step * (width + genes)),
    )(at, *ls, *xs, *given, *tail)


def weights_of(mask_ref, counts_ref):
    weights = (mask_ref[...] * counts_ref[...]).astype(F32)
    return jnp.concatenate([weights, jnp.zeros((8 - SLIDES, weights.shape[1]), F32)], axis=0)


def column_of(row):
    return jnp.transpose(jnp.broadcast_to(row, (LANES, row.shape[1])))


def sums_kernel(n_parts, *refs):
    parts, (cells_ref, inv_ref, spatial_ref, ids_ref, mask_ref, counts_ref, pred_ref, wide_ref, spot_ref, q_ref) = (
        refs[:n_parts],
        refs[n_parts:],
    )
    spatial = spatial_ref[...]
    pred, q = parts[0][...], cells_ref[...]
    for part in parts[1:]:
        pred = pred + part[: pred.shape[0], :]
        q = q + part[pred.shape[0] :, :]
    q_ref[...] = q
    genes = pred.shape[1]
    pred = pred * jnp.concatenate([column_of(inv_ref[...])] * (genes // LANES), axis=1)
    pred_ref[...] = pred
    onehot = (lax.broadcasted_iota(jnp.int32, (8, LANES), 0) == ids_ref[...]).astype(F32)
    ones = jnp.ones((8, genes), F32)
    rows = lax.broadcasted_iota(jnp.int32, (8, LANES), 0)
    spot = jnp.where(rows == 3, jnp.sum(weights_of(mask_ref, counts_ref)), 0.0)
    for k, product in enumerate((pred * spatial, pred * pred, spatial * spatial)):
        wide_ref[8 * k : 8 * k + 8, :] = exact(onehot, product, ((1,), (0,)))
        spot = jnp.where(rows == k, exact(ones, product, ((1,), (1,))), spot)
    spot_ref[...] = spot


def pred_sums(n_parts, *args):
    parts, (by_cell, inv, spatial, ids, mask, counts) = args[:n_parts], args[n_parts:]
    width, genes = spatial.shape
    return pl.pallas_call(
        functools.partial(sums_kernel, n_parts),
        out_shape=(
            jax.ShapeDtypeStruct((width, genes), F32),
            jax.ShapeDtypeStruct((24, genes), F32),
            jax.ShapeDtypeStruct((8, width), F32),
            jax.ShapeDtypeStruct(by_cell.shape, F32),
        ),
        name="sums",
        compiler_params=room(12),
        cost_estimate=cost(10 * width * genes * 48, 4 * width * genes * 6),
    )(*parts, by_cell, inv, spatial, ids, mask, counts)


def dpred_kernel(spots, share_gene, *refs):
    wides, spot, refs = refs[:2], refs[2][...] + refs[3][...], refs[4:]
    pred_ref, spatial_ref, ids_ref, mask_ref, counts_ref, inv_ref, d_ref, tot_ref = refs
    weights = weights_of(mask_ref, counts_ref)
    genes = pred_ref.shape[1]
    a, b, c = (wides[0][8 * k : 8 * k + 8, :] + wides[1][8 * k : 8 * k + 8, :] for k in range(3))
    e, f, h, wsum = (spot[k : k + 1, :] for k in range(4))
    wsum = jnp.max(wsum)
    gain = weights / wsum
    inv_g = lax.rsqrt(b * c + 1e-06)
    inv_s = lax.rsqrt(f * h + 1e-06)
    grad_a = -gain * inv_g
    grad_b = gain * a * c * inv_g * inv_g * inv_g
    onehot = (lax.broadcasted_iota(jnp.int32, (8, LANES), 0) == ids_ref[...]).astype(F32)
    wide = functools.partial(jnp.concatenate, axis=1)
    by_spatial = exact(onehot, grad_a, ((0,), (0,))) - wide([column_of(inv_s / spots)] * (genes // LANES))
    by_pred = exact(onehot, grad_b, ((0,), (0,))) + wide(
        [column_of(e * h * inv_s * inv_s * inv_s / spots)] * (genes // LANES)
    )
    pred = pred_ref[...]
    dpred = by_spatial * spatial_ref[...] + by_pred * pred
    inv = inv_ref[...]
    d_ref[:LANES, :] = dpred * wide([column_of(inv)] * (genes // LANES))
    own = exact(jnp.ones((8, genes), F32), pred * dpred, ((1,), (1,))) * inv
    d_ref[LANES:, :] = wide([own] * (genes // LANES))
    rows = lax.broadcasted_iota(jnp.int32, (8, LANES), 0)
    tot = jnp.where(rows == 0, jnp.sum(weights * a * inv_g), 0.0)
    tot = jnp.where(rows == 1, jnp.sum(e * inv_s), tot)
    tot = jnp.where(rows == 2, jnp.sum(f), tot)
    tot_ref[...] = jnp.where(rows == 3, wsum * share_gene, tot)


def dpred_scaled(spots, share_gene, *args):
    spatial = args[5]
    width, genes = spatial.shape
    return pl.pallas_call(
        functools.partial(dpred_kernel, spots, share_gene),
        out_shape=(
            jax.ShapeDtypeStruct((width + 8, genes), F32),
            jax.ShapeDtypeStruct((8, width), F32),
        ),
        name="dpred",
        compiler_params=room(12),
        cost_estimate=cost(10 * width * genes * 48, 4 * width * genes * 6),
    )(*args)


def dmap_kernel(ranges, n, *refs):
    xs, ds, outs = refs[:4], refs[4 : 4 + n], refs[-n:]
    parts = [split(d[:LANES, :]) for d in ds]
    d = tuple(jnp.concatenate([part[i] for part in parts], axis=0) for i in range(2))
    own = jnp.concatenate([d[LANES : LANES + 1, :LANES] for d in ds], axis=1)
    at = 0
    for x, first, count in ranges:
        here = pl.ds(first, count)
        value = three((xs[2 * x][here, :], xs[2 * x + 1][here, :]), d, ((1,), (1,))) - own
        for i, out in enumerate(outs):
            out[at : at + count, :] = value[:, i * LANES : (i + 1) * LANES]
        at += count
    if len(refs) > 4 + 2 * n:
        for out in outs:
            out[at:, :] = refs[4 + n][...]


def dmap_blocks(ranges, ds, xs, tail=()):
    width = ds[0].shape[0] - 8
    rows = sum(count for _, _, count in ranges) + 8 * len(tail)
    return pl.pallas_call(
        functools.partial(dmap_kernel, ranges, len(ds)),
        in_specs=[VMEM] * (4 + len(ds) + len(tail)),
        out_specs=(VMEM,) * len(ds),
        out_shape=(jax.ShapeDtypeStruct((rows, width), F32),) * len(ds),
        name="dmap",
        compiler_params=room(16),
        cost_estimate=cost(0, 0),
    )(*xs, *ds, *tail)


def egrad_kernel(scale, ks, step, wheres, n_add, at_ref, *refs):
    n = len(wheres)
    counts = [2 if isinstance(where, tuple) else 1 for where in wheres]
    ls, ds, adds, o_ref = refs[: sum(counts)], refs[sum(counts) : sum(counts) + n], refs[sum(counts) + n : -1], refs[-1]
    parts = [split(d[:LANES, :]) for d in ds]
    d = tuple(jnp.concatenate([part[i] for part in parts], axis=0) for i in range(2))
    for j, k in enumerate(ks):
        es, at = [], 0
        for where, number in zip(wheres, counts, strict=True):
            if number == 2:
                mine, others = (ls[at + i][at_rows(where[i], step), :] for i in range(2))
                l = jnp.where(at_ref[0] == k, mine, others)
            else:
                l = ls[at][at_rows(where + k, step), :]
            at += number
            es.append(jnp.exp(l))
        value = three(split(jnp.concatenate(es, axis=1)), d, ((1,), (0,))) * scale
        o_ref[at_rows(j, step), :] = value + adds[j][...] if n_add else value


def egrad_part(ks, step, wheres, scale, at, ls, ds, adds=()):
    genes = ds[0].shape[1]
    return pl.pallas_call(
        functools.partial(egrad_kernel, scale, ks, step, wheres, len(adds)),
        in_specs=[SMEM] + [VMEM] * (len(ls) + len(ds) + len(adds)),
        out_specs=VMEM,
        out_shape=jax.ShapeDtypeStruct((len(ks) * step, genes), F32),
        name="egrad",
        compiler_params=room(big(*ls, *ds, *adds) + 24),
        cost_estimate=cost(0, 0),
    )(at, *ls, *ds, *adds)


def ratio_kernel(spots, scale, cell_ref, density_ref, inv_ref, a_ref, _, ratio_ref, sum_ref, kl_ref, a, sems):
    inv = inv_ref[...]
    count, step = density_ref.shape

    def load(k):
        return pltpu.make_async_copy(a_ref.at[at_rows(k, step)], a.at[at_rows(k, step)], sems.at[k])

    for k in range(count):
        load(k).start()
    density = density_ref[...]
    target = density / jnp.sum(density)
    q = by_cell_rows(cell_ref, count, step)
    ratios = target / q / spots
    ratio_ref[...] = ratios
    kl_ref[...] = jnp.full(kl_ref.shape, jnp.sum(target * (jnp.log(target) - jnp.log(q))))
    rows = lax.broadcasted_iota(jnp.int32, (16, step), 0)
    total = jnp.zeros((1, LANES), F32)
    for k in range(count):
        load(k).wait()
        high, low = split(ratios[k : k + 1, :])
        lhs = jnp.where(rows == 0, high.astype(F32), jnp.where(rows == 1, low.astype(F32), 0.0)).astype(BF16)
        for part in split(a[at_rows(k, step), :]):
            sums = lax.dot_general(lhs, part, (((1,), (0,)), ((), ())), preferred_element_type=F32)
            total = total + (sums[0:1, :] + sums[1:2, :])
    sum_ref[...] = jnp.broadcast_to(total * (inv * inv * (1.0 / scale)), sum_ref.shape)


def ratio_part(spots, by_cell, density, inv, a):
    cells, width = a.shape
    return pl.pallas_call(
        functools.partial(ratio_kernel, spots, float(cells)),
        in_specs=[VMEM, VMEM, VMEM, HBM],
        out_specs=(HBM, VMEM, VMEM, VMEM),
        out_shape=(
            pltpu.HBM((cells, width), F32),
            jax.ShapeDtypeStruct(density.shape, F32),
            jax.ShapeDtypeStruct((8, width), F32),
            jax.ShapeDtypeStruct((8, width), F32),
        ),
        scratch_shapes=[pltpu.VMEM((cells, width), F32), pltpu.SemaphoreType.DMA((density.shape[0],))],
        input_output_aliases={3: 0},
        name="ratio",
        compiler_params=room(big(a) + 8),
        cost_estimate=cost(0, 0),
    )(by_cell, density, inv, a)


def join_kernel(a_ref, b_ref, o_ref):
    half = a_ref.shape[0]
    o_ref[:half, :] = a_ref[...]
    o_ref[half:, :] = b_ref[...]


def join(a, b):
    return pl.pallas_call(
        join_kernel,
        in_specs=[VMEM, VMEM],
        out_specs=VMEM,
        out_shape=jax.ShapeDtypeStruct((2 * a.shape[0], a.shape[1]), F32),
        name="join",
        compiler_params=room(8),
        cost_estimate=cost(0, 0),
    )(a, b)


def add_kernel(a_ref, b_ref, o_ref):
    o_ref[...] = a_ref[...] + b_ref[: o_ref.shape[0], :]


def plus(a, b):
    return pl.pallas_call(
        add_kernel,
        in_specs=[VMEM, VMEM],
        out_specs=VMEM,
        out_shape=jax.ShapeDtypeStruct(a.shape, F32),
        name="add",
        compiler_params=room(8),
        cost_estimate=cost(0, 0),
    )(a, b)


def add_all_kernel(*refs):
    total = refs[0][...]
    for ref in refs[1:-1]:
        total = total + ref[...]
    refs[-1][...] = total


def add_all(*arrays):
    return pl.pallas_call(
        add_all_kernel,
        in_specs=[VMEM] * len(arrays),
        out_specs=VMEM,
        out_shape=jax.ShapeDtypeStruct(arrays[0].shape, F32),
        name="add_all",
        compiler_params=room(8),
        cost_estimate=cost(0, 0),
    )(*arrays)


def next_kernel(cuts, end_ref, s_ref, y_ref, *refs):
    blocks, (t_ref, o_ref, c_ref) = refs[:-3], refs[-3:]
    total = s_ref[...] + y_ref[...]
    t_ref[...] = total
    at = 0
    for block, (first, count) in zip(blocks, cuts, strict=True):
        c_ref[at : at + count, :] = block[first : first + count, :]
        at += count
    own = c_ref[...]
    both = min(at, total.shape[0])
    o_ref[:both, :] = jnp.where(end_ref[0] == 1, own[:both, :], total[:both, :])
    if o_ref.shape[0] > both:
        o_ref[both:, :] = (own if at > both else total)[both:, :]


def next_piece(cuts, end, s, y, *blocks):
    size, width = sum(count for _, count in cuts), s.shape[1]
    return pl.pallas_call(
        functools.partial(next_kernel, cuts),
        in_specs=[SMEM] + [VMEM] * (2 + len(blocks)),
        out_specs=(VMEM, VMEM, VMEM),
        out_shape=(
            jax.ShapeDtypeStruct(s.shape, F32),
            jax.ShapeDtypeStruct((max(size, s.shape[0]), width), F32),
            jax.ShapeDtypeStruct((size, width), F32),
        ),
        name="next",
        compiler_params=room(10),
        cost_estimate=cost(0, 0),
    )(end, s, y, *blocks)


def final_kernel(place, cuts, step, end_ref, at_ref, *refs):
    n, m = len(cuts), 1 + max(k for half in cuts for k, _, _ in half)
    rxs, ss = refs[:m], refs[m : 2 * m]
    ratio_ref, sum_ref, inv_ref, a_ref, _, _, o_ref, a, b, sems = refs[2 * m :]
    load = pltpu.make_async_copy(a_ref.at[at_rows(at_ref[place], step, n)], a, sems.at[n])
    load.start()
    rows = lax.broadcasted_iota(jnp.int32, (16, step), 0)
    ones = (lax.broadcasted_iota(jnp.int32, (16, LANES), 0) < 3).astype(BF16)
    stores = []
    for k in range(n):
        at, here = at_ref[place] + k, at_rows(k, step)
        ratio = ratio_ref[pl.ds(at, 1), :]
        high = ratio.astype(BF16).astype(F32)
        mid = (ratio - high).astype(BF16).astype(F32)
        terms = jnp.where(rows == 0, high, jnp.where(rows == 1, mid, jnp.where(rows == 2, ratio - high - mid, 0.0)))
        column = lax.dot_general(terms.astype(BF16), ones, (((0,), (0,)), ((), ())), preferred_element_type=F32)
        whole = jnp.concatenate(
            [
                jnp.where(end_ref[0] == 1, rxs[i][first : first + count, :], ss[i][first : first + count, :])
                for i, first, count in cuts[k]
            ],
            axis=0,
        )
        value = whole + (sum_ref[0:1, :] - column * inv_ref[...])
        if k == 0:
            load.wait()
        b[here, :] = a[here, :] * value
        stores.append(pltpu.make_async_copy(b.at[here], o_ref.at[at_rows(at, step)], sems.at[k]))
        stores[-1].start()
    for store in stores:
        store.wait()


def final_block(step, cuts, place, end, at, rxs, ss, ratio, ratio_sum, inv, a, grad):
    width = a.shape[1]
    n, m = len(cuts), len(ss)
    return pl.pallas_call(
        functools.partial(final_kernel, place, cuts, step),
        in_specs=[SMEM, SMEM] + [VMEM] * (2 * m + 3) + [HBM, HBM],
        out_specs=(HBM, HBM),
        out_shape=(pltpu.HBM(a.shape, F32), pltpu.HBM(grad.shape, F32)),
        scratch_shapes=[pltpu.VMEM((n * step, width), F32)] * 2 + [pltpu.SemaphoreType.DMA((1 + n,))],
        input_output_aliases={5 + 2 * m: 0, 6 + 2 * m: 1},
        name="final",
        compiler_params=room(12),
        cost_estimate=cost(0, 0),
    )(end, at, *rxs, *ss, ratio, ratio_sum, inv, a, grad)


def blank(shape):
    return pl.pallas_call(lambda o_ref: None, out_specs=HBM, out_shape=pltpu.HBM(shape, F32), name="blank")()


def scalars_kernel(n, cells, spots, step, end_ref, *refs):
    sums = [refs[k][-8:, :] for k in range(n)]
    rx_ref, s_ref, q_ref, kl_ref, loss_ref, map_ref, pred_ref = refs[n:]
    while len(sums) > 1:
        sums = [a + b for a, b in zip(sums[::2], sums[1::2], strict=True)]
    by_gene = jnp.where(end_ref[0] == 1, rx_ref[step : step + 8, :], s_ref[step : step + 8, :])
    cosine, fitted, wsum, scos = by_gene[0:1, :], sums[0][2:3, :], by_gene[3:4, :], sums[0][1:2, :]
    loss = -cosine / wsum - scos / spots + kl_ref[0:1, :]
    rms_map = jnp.sqrt(q_ref[q_ref.shape[0] - 1 :, q_ref.shape[1] - 8 :] / (cells * spots))
    rms_pred = jnp.sqrt(fitted / (spots * GENES))
    for ref, value in zip((loss_ref, map_ref, pred_ref), (loss, rms_map, rms_pred), strict=True):
        ref[0, 0] = jnp.max(value)


def scalar_results(n, cells, spots, step, end, *args):
    return pl.pallas_call(
        functools.partial(scalars_kernel, n, cells, spots, step),
        in_specs=[SMEM] + [VMEM] * len(args),
        out_specs=(SMEM,) * 3,
        out_shape=(jax.ShapeDtypeStruct((1, 1), F32),) * 3,
        name="scalars",
        compiler_params=room(24),
        cost_estimate=cost(0, 0),
    )(end, *args)


def shards(logits, expression, spatial, density, gene_mask, gene_counts, slide_ids):
    n_blk = lax.axis_size("blk")
    n_gene = lax.axis_size("gene")
    me = lax.axis_index("blk")
    plane = lax.axis_index("gene")
    cells, width = logits.shape
    rows, genes = expression.shape
    half = rows // 2
    spots = width * n_blk
    order = Order()

    def swap(x, m):
        return lax.ppermute(x, "blk", [(i, i ^ m) for i in range(n_blk)])

    def across(x, m):
        return lax.ppermute(x, "gene", [(i, i ^ m) for i in range(n_gene)])

    def cut(l, r, first, size):
        return lax.dynamic_slice_in_dim(l, (me ^ r) * rows + first, size, 0)

    far = sorted(range(2, n_blk, 2), key=lambda m: (m.bit_count(), m))
    side = plane % 2
    at = jnp.stack([side, 1 - side, *[(me ^ r) * 2 + k for r in range(n_blk) for k in range(2)]]
        + [(me ^ r) * 2 + side for r in range(n_blk)]).astype(jnp.int32)

    def whole(r):
        return (2 + 2 * r, 3 + 2 * r)

    def mine(r):
        return (2 + 2 * n_blk + r,)

    sent, passed, held = {}, {}, {}

    other = swap(expression, 1)
    constants = (slide_ids[None, :], gene_mask, gene_counts[None, :])
    n_q = cells // genes

    def add_pred(jobs, n_acc, ls, given=(), tail=()):
        n, g = len(ls), len(given)

        def run(*a):
            return pred_sums_of(jobs, n_acc, half, at, a[:n], a[n + g : n + g + 4], a[n : n + g], a[n + g + 4 :])

        return order(run, (*ls, *given), (*own_x, *other_x, *tail))

    def cuts(*layout):
        return order(lambda l: cut_blocks(layout, half, at, l), (logits,))

    if n_blk == 8 and n_gene == 4:
        near3, near5 = order(
            lambda l: [lax.dynamic_slice_in_dim(l, (me ^ r) * rows + side * half, half, 0) for r in (3, 5)], (logits,)
        )
        sent[3], sent[5] = swap(near3, 2), swap(near5, 4)
        own_x = order(lambda x: parts_of(x, half), (expression,))
        both, near2, near4, stay = cuts(mine(6) + mine(7), whole(2), whole(4), whole(0) + whole(1))
        passed[3] = across(order(join, (sent[3], sent[5])), 1)
        sent[6], sent[2], sent[4] = swap(order.here(both), 6), swap(order.here(near2), 2), swap(order.here(near4), 4)
        inv, by_cell, scale = order(functools.partial(softmax_sums, spots, genes, half), (logits,))
        other_x = order(lambda x: parts_of(x, half), (other,))
        (acc0,) = add_pred(((0, 0, 0, 0, 0, 0, 2), (0, 0, 0, 2, 1, 0, 2)), 1, (stay,))
        acc2, acc4 = add_pred(((0, 0, 0, 0, 1, [0], 1), (1, 0, 1, 0, 1, [0], 1)), 2, (sent[3], sent[5]))
        cell_moved = swap(order.here(by_cell), 1)
        passed[6] = across(order.here(sent[6]), 1)
        (acc6,) = add_pred(((0, 0, 0, 0, 0, [0], 1), (0, 0, 0, 1, 1, [0], 1)), 1, (sent[6],))
        acc2, acc4 = add_pred(
            ((0, 1, 0, 0, 1, [1], 1), (1, 2, 0, 1, 1, [1], 1)), 2, (passed[3],), (acc2, acc4)
        )
        by_cell = order(plus, (by_cell, cell_moved))
        (acc2,) = add_pred(((0, 1, 0, 0, 0, 0, 2),), 1, (sent[2],), (acc2,), (by_cell,))
        moved = {2: swap(acc2, 2)}
        (acc4,) = add_pred(((0, 1, 0, 0, 0, 0, 2),), 1, (sent[4],), (acc4,), (by_cell,))
        moved[4] = swap(acc4, 4)
        (acc6,) = add_pred(((0, 1, 0, 0, 0, [1], 1), (0, 0, 0, 1, 1, [1], 1)), 1, (passed[6],), (acc6,), (by_cell,))
        moved[6] = swap(acc6, 6)
        held = {
            2: ((sent[2],), 0),
            3: ((sent[3], passed[3]), (0, 0)),
            4: ((sent[4],), 0),
            5: ((sent[5], passed[3]), (0, 1)),
            6: ((sent[6], passed[6]), (0, 0)),
            7: ((sent[6], passed[6]), (1, 1)),
        }
    else:
        inv, by_cell, scale = order(functools.partial(softmax_sums, spots, genes, half), (logits,))
        by_cell = order(plus, (by_cell, swap(by_cell, 1)))
        own_x = order(lambda x: parts_of(x, half), (expression,))
        other_x = order(lambda x: parts_of(x, half), (other,))
        (stay,) = cuts(whole(0) + whole(1))
        (acc0,) = add_pred(((0, 0, 0, 0, 0, 0, 2), (0, 0, 0, 2, 1, 0, 2)), 1, (stay,))
        moved = {}
        for m in far:
            blocks = cuts(whole(m), whole(m + 1))
            for r in (m, m + 1):
                sent[r] = swap(blocks[r - m], m)
                held[r] = ((sent[r],), 0)
            (acc,) = add_pred(((0, 0, 0, 0, 0, 0, 2), (0, 0, 1, 0, 1, 0, 2)), 1, (sent[m], sent[m + 1]), (), (by_cell,))
            moved[m] = swap(acc, m)
    held[0], held[1] = ((stay,), 0), ((stay,), 2)

    parts = [acc0] + [moved[m] for m in far]
    pred, wide, spot, by_cell = order(
        functools.partial(pred_sums, len(parts)), parts, (by_cell, inv, spatial, *constants)
    )
    density = density.reshape(cells // half, half)
    state = {"scale": scale, "grad": blank((cells, width))}

    spot_moved = across(spot, 1)
    m = 1
    while 2 * m < n_blk:
        wide = order(plus, (wide, swap(wide, m)))
        m *= 2
        if m == 2:
            spot = order(add_all, (spot, spot_moved))
            spot_moved = across(spot, 2)
    wide_moved = swap(wide, m)
    grad, tot = order(
        functools.partial(dpred_scaled, spots, 1.0 / n_gene),
        (wide, wide_moved, spot, spot_moved),
        (pred, spatial, *constants, inv),
    )
    grads, back, tails = {0: grad}, {}, {}

    def dmap(ms, ranges, wait=(), tail=()):
        outs = order(
            lambda *a: dmap_blocks(ranges, a[: len(ms)], a[len(ms) : len(ms) + 4], a[len(ms) + 4 :]),
            [grads[m] for m in ms],
            (*own_x, *other_x, *tail),
            wait,
        )
        if tail and ms != (0,):
            tails.update({m: swap(d, m) for m, d in zip(ms, outs, strict=True)})
            return [tails[m] for m in ms]
        return [swap(d, m) if m else d for m, d in zip(ms, outs, strict=True)]

    def block_rows(odd):
        return ((odd, 0, half), (odd, half, half))

    blocks = [0, 1, 2, 4, 3, 5, 6, 7] if n_blk == 8 else [r for m in [0, *far] for r in (m, m + 1)]
    long = 848
    short = 2 * rows // 3 // 16 * 16
    sizes = [2 * rows - 2 * short, short, short] + [long] * ((cells - 2 * rows) // long)
    sizes += [n for n in [cells - sum(sizes)] if n]
    starts = [sum(sizes[:t]) for t in range(len(sizes))]
    count, lag = len(sizes), 3
    assert starts[3] == 2 * rows and sum(sizes) == cells

    def overlap(first, size, cuts_at, cuts_size):
        found = []
        for k, (a, n) in enumerate(zip(cuts_at, cuts_size, strict=True)):
            low, high = max(first, a), min(first + size, a + n)
            if low < high:
                found.append((k, low - a, high - low))
        return found

    block_starts, block_sizes = [rows * k for k in range(len(blocks))], [rows] * len(blocks)
    part, total_of, mid, got, own = {}, {}, {}, {}, {}
    end = jnp.reshape((plane == 0) | (plane == n_gene - 1), (1,)).astype(jnp.int32)

    def send(t):
        if t >= count + lag:
            return
        if t < lag:
            ranges = overlap(starts[t], sizes[t], (0, rows), (rows, rows))
            own[t] = buffer = dmap((0,), tuple(ranges), (), (tot,) if t == 0 else ())[0]
        elif t < count:
            found = overlap(starts[t], sizes[t], block_starts, block_sizes)
            cuts = tuple((back[blocks[k]][1] + first, n) for k, first, n in found)
            total_of[t - lag], buffer, own[t] = order(
                lambda s, y, *b: next_piece(cuts, end, s, y, *b),
                (part[t - lag], mid[t - lag], *[back[blocks[k]][0] for k, _, _ in found]),
            )
        else:
            buffer = total_of[t - lag] = order(plus, (part[t - lag], mid[t - lag]))
        got[t] = lax.ppermute(buffer, "gene", PAIR)

    def finish(k):
        halves = [overlap(block_starts[k] + half * h, half, starts, sizes) for h in range(2)]
        ts = sorted({t for found in halves for t, _, _ in found})
        cuts = tuple(tuple((ts.index(t), first, n) for t, first, n in found) for found in halves)
        m = len(ts)
        state["scale"], state["grad"] = order(
            lambda *a: final_block(half, cuts, 2 + 2 * blocks[k], end, at, a[:m], a[m : 2 * m], *a[2 * m :]),
            (*[got[t + lag] for t in ts], *[total_of[t] for t in ts]),
            (state["ratio"], state["ratio_sum"], inv, state["scale"], state["grad"]),
        )

    last_piece = [max(t for t, _, _ in overlap(a, rows, starts, sizes)) for a in block_starts]

    def expr_part(odd, ks, adds=()):
        ms = [0, *far]
        ls = [l for m in ms for l in held[m + odd][0]]
        wheres = [held[m + odd][1] for m in ms]
        n, m = len(ls), len(adds)
        return order(
            lambda d, *a: egrad_part(ks, half, wheres, float(cells), at, a[m : m + n], (d, *a[m + n :]), a[:m]),
            (grads[0], *adds),
            (*ls, *[grads[m] for m in far]),
        )

    def first_dmap():
        if n_blk == 8:
            for r, d in zip((2, 4), dmap((2, 4), block_rows(0)), strict=True):
                back[r] = (d, 0)
        else:
            tails[0] = order(plus, (tot, tot_moved))
            for m in far:
                (d,) = dmap((m,), block_rows(0) + block_rows(1), (), (tails[0],))
                back[m], back[m + 1] = (d, 0), (d, rows)

    def second_dmap():
        if n_blk == 8:
            tails[0] = order(plus, (tot, tot_moved))
            for r, d in zip((3, 5), dmap((2, 4), block_rows(1), (back[2][0], back[4][0]), (tails[0],)), strict=True):
                back[r] = (d, 0)

    def third_dmap():
        if n_blk == 8:
            back[6] = (dmap((6,), block_rows(0), (back[3][0], back[5][0]))[0], 0)

    def fourth_dmap():
        if n_blk == 8:
            back[7] = (dmap((6,), block_rows(1), (), (tails[0],))[0], 0)

    def kl():
        state["scale"], state["ratio"], state["ratio_sum"], state["kl"] = order(
            functools.partial(ratio_part, spots), (by_cell,), (density, inv, state["scale"])
        )

    def egrad(k):
        state["swapped", k] = swap(expr_part(1, (k,)), 1)

    def scalars():
        state["scalars"] = order(
            functools.partial(scalar_results, n_blk // 2, cells, spots, sizes[0], end),
            (*[tails[m] for m in range(0, n_blk, 2)], got[lag], total_of[0], by_cell),
            (state["kl"],),
        )

    def expr():
        state["expr"] = expr_part(0, (0, 1), (state["swapped", 0], state["swapped", 1]))

    plan = {
        (0, "between"): [first_dmap],
        (1, "after"): [kl],
        (2, "between"): [second_dmap],
        (5, "between"): [third_dmap],
        (7, "between"): [fourth_dmap, functools.partial(egrad, 0)],
        (8, "between"): [functools.partial(egrad, 1)],
        (count, "between"): [scalars],
        (count + 1, "between"): [expr],
    }
    for k in range(len(blocks)):
        t = last_piece[k] + lag + 1
        if t < count + lag:
            plan.setdefault((t, "between"), []).append(functools.partial(finish, k))

    def extra(t, place):
        for step in plan.get((t, place), ()):
            step()

    send(0)
    for m in far:
        grads[m] = swap(order.here(grad), m)
    tot_moved = swap(order.here(tot), 1)
    for t in range(count + lag):
        extra(t, "before")
        send(t + 1)
        extra(t, "between")
        if t < count:
            part[t] = order(plus, (own[t], got[t]))
            mid[t] = lax.ppermute(part[t], "gene", MIDDLE)
        extra(t, "after")
    for k in range(len(blocks)):
        if last_piece[k] + lag + 1 >= count + lag:
            finish(k)
    loss, rms_map, rms_pred = (x[0, 0] for x in state["scalars"])
    return (loss, state["grad"], state["expr"], rms_map, rms_pred)


def solution(mesh):
    placed = (
        P(None, "blk"),
        P("blk", "gene"),
        P("blk", "gene"),
        P(),
        P(None, "gene"),
        P("gene"),
        P("blk"),
    )
    return jax.shard_map(
        shards,
        mesh=mesh,
        in_specs=placed,
        out_specs=(P(), P(None, "blk"), P("blk", "gene"), P(), P()),
        check_vma=False,
    )
```

```python
import functools

import jax
import jax.numpy as jnp
from jax import lax
from jax.experimental import pallas as pl
from jax.experimental.pallas import tpu as pltpu
from jax.sharding import PartitionSpec as P

GENES = 2048
SLIDES = 4
LANES = 128
F32 = jnp.float32
BF16 = jnp.bfloat16
PAIR = [(0, 1), (1, 0), (2, 3), (3, 2)]
MIDDLE = [(1, 2), (2, 1)]


def room(mib):
    return pltpu.CompilerParams(vmem_limit_bytes=mib * 1024 * 1024)


class Order:
    def __init__(self):
        self.last = None

    def __call__(self, step, fresh, const=(), wait=()):
        gate = [*wait] if self.last is None else [self.last, *wait]
        if gate:
            fresh = lax.optimization_barrier((*fresh, *gate))[: len(fresh)]
        out = step(*fresh, *const)
        self.last = out[0] if isinstance(out, (tuple, list)) else out
        return out

    def here(self, x):
        return lax.optimization_barrier((x, self.last))[0]


def split(x):
    high = x.astype(BF16)
    return high, (x - high.astype(F32)).astype(BF16)


def three(a, b, dims):
    def dot(u, v):
        return lax.dot_general(u, v, (dims, ((), ())), preferred_element_type=F32)

    return dot(a[0], b[0]) + (dot(a[0], b[1]) + dot(a[1], b[0]))


def exact(a, b, dims):
    return lax.dot_general(a, b, (dims, ((), ())), precision=lax.Precision.HIGHEST, preferred_element_type=F32)


def cost(flops, size):
    del flops, size
    return pl.CostEstimate(flops=1, bytes_accessed=1, transcendentals=0)


def big(*arrays):
    return sum(x.size for x in arrays) * 4 // 2**20 + 1


VMEM = pl.BlockSpec(memory_space=pltpu.VMEM)
SMEM = pl.BlockSpec(memory_space=pltpu.SMEM)
HBM = pl.BlockSpec(memory_space=pltpu.HBM)


def at_rows(i, step, count=1):
    start = i * step
    return pl.ds(start if isinstance(i, int) else pl.multiple_of(start, 16), step * count)


def cut_kernel(layout, step, at_ref, l_ref, *refs):
    outs, sems = refs[:-1], refs[-1]
    copies = []
    for out, places in zip(outs, layout, strict=True):
        for k, place in enumerate(places):
            copies.append(
                pltpu.make_async_copy(
                    l_ref.at[at_rows(at_ref[place], step)], out.at[at_rows(k, step)], sems.at[len(copies)]
                )
            )
    for copy in copies:
        copy.start()
    for copy in copies:
        copy.wait()


def cut_blocks(layout, step, at, logits):
    width = logits.shape[1]
    count = sum(len(places) for places in layout)
    return pl.pallas_call(
        functools.partial(cut_kernel, layout, step),
        in_specs=[SMEM, VMEM],
        out_specs=(HBM,) * len(layout),
        out_shape=tuple(jax.ShapeDtypeStruct((len(places) * step, width), F32) for places in layout),
        scratch_shapes=[pltpu.SemaphoreType.DMA((count,))],
        name="cut",
        compiler_params=room(big(logits) + 2),
        cost_estimate=cost(0, 8 * count * step * width),
    )(at, logits)


def by_cell_rows(ref, count, step):
    genes = ref.shape[1]
    rest = [ref[count : count + count // 2, at : at + step - genes] for at in (0, genes // 2)]
    return jnp.concatenate([ref[:count, :], jnp.concatenate(rest, axis=0)], axis=1)


def softmax_kernel(spots, scale, step, l_ref, inv_ref, cell_ref, o_ref, buffer, sem):
    cells, width = l_ref.shape
    genes = cell_ref.shape[1]
    count = cells // step

    def column(k, total):
        e = jnp.exp(l_ref[at_rows(k, step), :])
        return total + jnp.sum(e.reshape(step // 8, 8, width), axis=0)

    total = lax.fori_loop(0, count, column, jnp.zeros((8, width), F32))
    inv = 1.0 / jnp.sum(total, axis=0, keepdims=True)
    inv_ref[...] = inv
    ones = jnp.ones((16, width), BF16)

    def row(at, k, square):
        e = jnp.exp(l_ref[at_rows(k, step), :])
        share = e * inv
        buffer[at_rows(k, step), :] = e * scale
        pltpu.make_async_copy(buffer.at[at_rows(k, step)], o_ref.at[at_rows(k, step)], sem).start()
        high, low = split(share)
        sums = [lax.dot_general(ones, x, (((1,), (1,)), ((), ())), preferred_element_type=F32) for x in (high, low)]
        sums = (sums[0] + sums[1])[0:1, :] * (1.0 / spots)
        cell_ref[pl.ds(k, 1), :] = sums[:, :genes]
        cell_ref[pl.ds(count + k - at * (count // 2), 1), at * (genes // 2) : at * (genes // 2) + step - genes] = sums[:, genes:]
        return square + jnp.sum((share * share).reshape(step // 8, 8, width), axis=0)

    square = lax.fori_loop(0, count // 2, functools.partial(row, 0), jnp.zeros((8, width), F32))
    square = lax.fori_loop(count // 2, count, functools.partial(row, 1), square)
    for at in (0, genes // 2):
        left = genes // 2 - (step - genes)
        cell_ref[count:, at + step - genes : at + genes // 2] = jnp.full((count // 2, left), jnp.sum(square), F32)
    pltpu.make_async_copy(buffer, o_ref, sem).wait()


def softmax_sums(spots, genes, step, logits):
    cells, width = logits.shape
    return pl.pallas_call(
        functools.partial(softmax_kernel, spots, float(cells), step),
        in_specs=[VMEM],
        out_specs=(VMEM, VMEM, HBM),
        out_shape=(
            jax.ShapeDtypeStruct((1, width), F32),
            jax.ShapeDtypeStruct((3 * cells // (2 * step), genes), F32),
            pltpu.HBM((cells, width), F32),
        ),
        scratch_shapes=[pltpu.VMEM((cells, width), F32), pltpu.SemaphoreType.DMA],
        name="softmax",
        compiler_params=room(2 * big(logits) + 4),
        cost_estimate=cost(0, 0),
    )(logits)


def parts_kernel(step, x_ref, high_ref, low_ref, buffer, sems):
    count = x_ref.shape[0] // step

    def copy(k):
        return pltpu.make_async_copy(x_ref.at[at_rows(k, step)], buffer.at[at_rows(k, step)], sems.at[k])

    for k in range(count):
        copy(k).start()
    for k in range(count):
        copy(k).wait()
        high_ref[at_rows(k, step), :], low_ref[at_rows(k, step), :] = split(buffer[at_rows(k, step), :])


def parts_of(x, step):
    return pl.pallas_call(
        functools.partial(parts_kernel, step),
        in_specs=[HBM],
        out_specs=(VMEM, VMEM),
        out_shape=(pltpu.VMEM(x.shape, BF16), pltpu.VMEM(x.shape, BF16)),
        scratch_shapes=[pltpu.VMEM(x.shape, F32), pltpu.SemaphoreType.DMA((x.shape[0] // step,))],
        name="parts",
        compiler_params=room(12),
        cost_estimate=cost(4 * x.size, 8 * x.size),
    )(x)


def pred_kernel(jobs, n_acc, step, tail, at_ref, *refs):
    n_l = 1 + max(job[2] for job in jobs)
    n_given = max(job[1] for job in jobs)
    ls, xs, given, outs = refs[:n_l], refs[n_l : n_l + 4], refs[n_l + 4 :][:n_given], refs[-n_acc:]
    place = lambda at: at_ref[at[0]] if isinstance(at, list) else at
    for k in range(n_acc):
        acc = None
        for _, g, l, l_at, x, x_at, count in [job for job in jobs if job[0] == k]:
            if g:
                acc = given[g - 1][...]
            for c in range(count):
                e = split(jnp.exp(ls[l][at_rows(place(l_at) + c, step), :]))
                rows = at_rows(place(x_at) + c, step)
                term = three(e, (xs[2 * x][rows, :], xs[2 * x + 1][rows, :]), ((0,), (0,)))
                acc = term if acc is None else acc + term
        outs[k][: acc.shape[0], :] = acc
        if tail:
            outs[k][acc.shape[0] :, :] = refs[-n_acc - 1][...]


def pred_sums_of(jobs, n_acc, step, at, ls, xs, given, tail=()):
    width, genes = ls[0].shape[1], xs[0].shape[1]
    steps = sum(job[-1] for job in jobs)
    return pl.pallas_call(
        functools.partial(pred_kernel, jobs, n_acc, step, len(tail)),
        in_specs=[SMEM] + [VMEM] * (len(ls) + len(xs) + len(given) + len(tail)),
        out_specs=(VMEM,) * n_acc,
        out_shape=(jax.ShapeDtypeStruct((width + sum(x.shape[0] for x in tail), genes), F32),) * n_acc,
        name="pred",
        compiler_params=room(16),
        cost_estimate=cost(6 * steps * step * width * genes, 4 * steps * step * (width + genes)),
    )(at, *ls, *xs, *given, *tail)


def weights_of(mask_ref, counts_ref):
    weights = (mask_ref[...] * counts_ref[...]).astype(F32)
    return jnp.concatenate([weights, jnp.zeros((8 - SLIDES, weights.shape[1]), F32)], axis=0)


def column_of(row):
    return jnp.transpose(jnp.broadcast_to(row, (LANES, row.shape[1])))


def sums_kernel(n_parts, *refs):
    parts, (cells_ref, inv_ref, spatial_ref, ids_ref, mask_ref, counts_ref, pred_ref, wide_ref, spot_ref, q_ref) = (
        refs[:n_parts],
        refs[n_parts:],
    )
    spatial = spatial_ref[...]
    pred, q = parts[0][...], cells_ref[...]
    for part in parts[1:]:
        pred = pred + part[: pred.shape[0], :]
        q = q + part[pred.shape[0] :, :]
    q_ref[...] = q
    genes = pred.shape[1]
    pred = pred * jnp.concatenate([column_of(inv_ref[...])] * (genes // LANES), axis=1)
    pred_ref[...] = pred
    onehot = (lax.broadcasted_iota(jnp.int32, (8, LANES), 0) == ids_ref[...]).astype(F32)
    ones = jnp.ones((8, genes), F32)
    rows = lax.broadcasted_iota(jnp.int32, (8, LANES), 0)
    spot = jnp.where(rows == 3, jnp.sum(weights_of(mask_ref, counts_ref)), 0.0)
    wide_ref[3 * SLIDES :, :] = jnp.zeros((16 - 3 * SLIDES, genes), F32)
    for k, product in enumerate((pred * spatial, pred * pred, spatial * spatial)):
        wide_ref[SLIDES * k : SLIDES * (k + 1), :] = exact(onehot, product, ((1,), (0,)))[:SLIDES, :]
        spot = jnp.where(rows == k, exact(ones, product, ((1,), (1,))), spot)
    spot_ref[...] = spot


def pred_sums(n_parts, *args):
    parts, (by_cell, inv, spatial, ids, mask, counts) = args[:n_parts], args[n_parts:]
    width, genes = spatial.shape
    return pl.pallas_call(
        functools.partial(sums_kernel, n_parts),
        out_shape=(
            jax.ShapeDtypeStruct((width, genes), F32),
            jax.ShapeDtypeStruct((16, genes), F32),
            jax.ShapeDtypeStruct((8, width), F32),
            jax.ShapeDtypeStruct(by_cell.shape, F32),
        ),
        name="sums",
        compiler_params=room(12),
        cost_estimate=cost(10 * width * genes * 48, 4 * width * genes * 6),
    )(*parts, by_cell, inv, spatial, ids, mask, counts)


def dpred_kernel(spots, share_gene, *refs):
    wides, spot, refs = refs[:2], refs[2][...] + refs[3][...], refs[4:]
    pred_ref, spatial_ref, ids_ref, mask_ref, counts_ref, inv_ref, d_ref, tot_ref = refs
    weights = weights_of(mask_ref, counts_ref)
    genes = pred_ref.shape[1]
    sums = wides[0][...] + wides[1][...]
    none = jnp.zeros((8 - SLIDES, genes), F32)
    a, b, c = (jnp.concatenate([sums[SLIDES * k : SLIDES * (k + 1), :], none], axis=0) for k in range(3))
    e, f, h, wsum = (spot[k : k + 1, :] for k in range(4))
    wsum = jnp.max(wsum)
    gain = weights / wsum
    inv_g = lax.rsqrt(b * c + 1e-06)
    inv_s = lax.rsqrt(f * h + 1e-06)
    grad_a = -gain * inv_g
    grad_b = gain * a * c * inv_g * inv_g * inv_g
    onehot = (lax.broadcasted_iota(jnp.int32, (8, LANES), 0) == ids_ref[...]).astype(F32)
    wide = functools.partial(jnp.concatenate, axis=1)
    by_spatial = exact(onehot, grad_a, ((0,), (0,))) - wide([column_of(inv_s / spots)] * (genes // LANES))
    by_pred = exact(onehot, grad_b, ((0,), (0,))) + wide(
        [column_of(e * h * inv_s * inv_s * inv_s / spots)] * (genes // LANES)
    )
    pred = pred_ref[...]
    dpred = by_spatial * spatial_ref[...] + by_pred * pred
    inv = inv_ref[...]
    d_ref[:LANES, :] = dpred * wide([column_of(inv)] * (genes // LANES))
    own = exact(jnp.ones((8, genes), F32), pred * dpred, ((1,), (1,))) * inv
    d_ref[LANES:, :] = wide([own] * (genes // LANES))
    rows = lax.broadcasted_iota(jnp.int32, (8, LANES), 0)
    tot = jnp.where(rows == 0, jnp.sum(weights * a * inv_g), 0.0)
    tot = jnp.where(rows == 1, jnp.sum(e * inv_s), tot)
    tot = jnp.where(rows == 2, jnp.sum(f), tot)
    tot_ref[...] = jnp.where(rows == 3, wsum * share_gene, tot)


def dpred_scaled(spots, share_gene, *args):
    spatial = args[5]
    width, genes = spatial.shape
    return pl.pallas_call(
        functools.partial(dpred_kernel, spots, share_gene),
        out_shape=(
            jax.ShapeDtypeStruct((width + 8, genes), F32),
            jax.ShapeDtypeStruct((8, width), F32),
        ),
        name="dpred",
        compiler_params=room(12),
        cost_estimate=cost(10 * width * genes * 48, 4 * width * genes * 6),
    )(*args)


def dmap_kernel(ranges, n, *refs):
    xs, ds, outs = refs[:4], refs[4 : 4 + n], refs[-n:]
    parts = [split(d[:LANES, :]) for d in ds]
    d = tuple(jnp.concatenate([part[i] for part in parts], axis=0) for i in range(2))
    own = jnp.concatenate([d[LANES : LANES + 1, :LANES] for d in ds], axis=1)
    at = 0
    for x, first, count in ranges:
        here = pl.ds(first, count)
        value = three((xs[2 * x][here, :], xs[2 * x + 1][here, :]), d, ((1,), (1,))) - own
        for i, out in enumerate(outs):
            out[at : at + count, :] = value[:, i * LANES : (i + 1) * LANES]
        at += count
    if len(refs) > 4 + 2 * n:
        for out in outs:
            out[at:, :] = refs[4 + n][...]


def dmap_blocks(ranges, ds, xs, tail=()):
    width = ds[0].shape[0] - 8
    rows = sum(count for _, _, count in ranges) + 8 * len(tail)
    return pl.pallas_call(
        functools.partial(dmap_kernel, ranges, len(ds)),
        in_specs=[VMEM] * (4 + len(ds) + len(tail)),
        out_specs=(VMEM,) * len(ds),
        out_shape=(jax.ShapeDtypeStruct((rows, width), F32),) * len(ds),
        name="dmap",
        compiler_params=room(16),
        cost_estimate=cost(0, 0),
    )(*xs, *ds, *tail)


def egrad_kernel(scale, ks, step, wheres, n_add, at_ref, *refs):
    n = len(wheres)
    counts = [2 if isinstance(where, tuple) else 1 for where in wheres]
    ls, ds, adds, o_ref = refs[: sum(counts)], refs[sum(counts) : sum(counts) + n], refs[sum(counts) + n : -1], refs[-1]
    parts = [split(d[:LANES, :]) for d in ds]
    d = tuple(jnp.concatenate([part[i] for part in parts], axis=0) for i in range(2))
    for j, k in enumerate(ks):
        es, at = [], 0
        for where, number in zip(wheres, counts, strict=True):
            if number == 2:
                mine, others = (ls[at + i][at_rows(where[i], step), :] for i in range(2))
                l = jnp.where(at_ref[0] == k, mine, others)
            else:
                l = ls[at][at_rows(where + k, step), :]
            at += number
            es.append(jnp.exp(l))
        value = three(split(jnp.concatenate(es, axis=1)), d, ((1,), (0,))) * scale
        o_ref[at_rows(j, step), :] = value + adds[j][...] if n_add else value


def egrad_part(ks, step, wheres, scale, at, ls, ds, adds=()):
    genes = ds[0].shape[1]
    return pl.pallas_call(
        functools.partial(egrad_kernel, scale, ks, step, wheres, len(adds)),
        in_specs=[SMEM] + [VMEM] * (len(ls) + len(ds) + len(adds)),
        out_specs=VMEM,
        out_shape=jax.ShapeDtypeStruct((len(ks) * step, genes), F32),
        name="egrad",
        compiler_params=room(big(*ls, *ds, *adds) + 24),
        cost_estimate=cost(0, 0),
    )(at, *ls, *ds, *adds)


def ratio_kernel(spots, scale, cell_ref, density_ref, inv_ref, a_ref, _, ratio_ref, sum_ref, kl_ref, a, sems):
    inv = inv_ref[...]
    count, step = density_ref.shape

    def load(k):
        return pltpu.make_async_copy(a_ref.at[at_rows(k, step)], a.at[at_rows(k, step)], sems.at[k])

    for k in range(count):
        load(k).start()
    density = density_ref[...]
    target = density / jnp.sum(density)
    q = by_cell_rows(cell_ref, count, step)
    ratios = target / q / spots
    ratio_ref[...] = ratios
    kl_ref[...] = jnp.full(kl_ref.shape, jnp.sum(target * (jnp.log(target) - jnp.log(q))))
    rows = lax.broadcasted_iota(jnp.int32, (16, step), 0)
    total = jnp.zeros((1, LANES), F32)
    for k in range(count):
        load(k).wait()
        high, low = split(ratios[k : k + 1, :])
        lhs = jnp.where(rows == 0, high.astype(F32), jnp.where(rows == 1, low.astype(F32), 0.0)).astype(BF16)
        for part in split(a[at_rows(k, step), :]):
            sums = lax.dot_general(lhs, part, (((1,), (0,)), ((), ())), preferred_element_type=F32)
            total = total + (sums[0:1, :] + sums[1:2, :])
    sum_ref[...] = jnp.broadcast_to(total * (inv * inv * (1.0 / scale)), sum_ref.shape)


def ratio_part(spots, by_cell, density, inv, a):
    cells, width = a.shape
    return pl.pallas_call(
        functools.partial(ratio_kernel, spots, float(cells)),
        in_specs=[VMEM, VMEM, VMEM, HBM],
        out_specs=(HBM, VMEM, VMEM, VMEM),
        out_shape=(
            pltpu.HBM((cells, width), F32),
            jax.ShapeDtypeStruct(density.shape, F32),
            jax.ShapeDtypeStruct((8, width), F32),
            jax.ShapeDtypeStruct((8, width), F32),
        ),
        scratch_shapes=[pltpu.VMEM((cells, width), F32), pltpu.SemaphoreType.DMA((density.shape[0],))],
        input_output_aliases={3: 0},
        name="ratio",
        compiler_params=room(big(a) + 8),
        cost_estimate=cost(0, 0),
    )(by_cell, density, inv, a)


def join_kernel(a_ref, b_ref, o_ref):
    half = a_ref.shape[0]
    o_ref[:half, :] = a_ref[...]
    o_ref[half:, :] = b_ref[...]


def join(a, b):
    return pl.pallas_call(
        join_kernel,
        in_specs=[VMEM, VMEM],
        out_specs=VMEM,
        out_shape=jax.ShapeDtypeStruct((2 * a.shape[0], a.shape[1]), F32),
        name="join",
        compiler_params=room(8),
        cost_estimate=cost(0, 0),
    )(a, b)


def add_kernel(a_ref, b_ref, o_ref):
    o_ref[...] = a_ref[...] + b_ref[: o_ref.shape[0], :]


def plus(a, b):
    return pl.pallas_call(
        add_kernel,
        in_specs=[VMEM, VMEM],
        out_specs=VMEM,
        out_shape=jax.ShapeDtypeStruct(a.shape, F32),
        name="add",
        compiler_params=room(8),
        cost_estimate=cost(0, 0),
    )(a, b)


def add_all_kernel(*refs):
    total = refs[0][...]
    for ref in refs[1:-1]:
        total = total + ref[...]
    refs[-1][...] = total


def add_all(*arrays):
    return pl.pallas_call(
        add_all_kernel,
        in_specs=[VMEM] * len(arrays),
        out_specs=VMEM,
        out_shape=jax.ShapeDtypeStruct(arrays[0].shape, F32),
        name="add_all",
        compiler_params=room(8),
        cost_estimate=cost(0, 0),
    )(*arrays)


def next_kernel(cuts, end_ref, s_ref, y_ref, *refs):
    blocks, (t_ref, o_ref, c_ref) = refs[:-3], refs[-3:]
    total = s_ref[...] + y_ref[...]
    t_ref[...] = total
    at = 0
    for block, (first, count) in zip(blocks, cuts, strict=True):
        c_ref[at : at + count, :] = block[first : first + count, :]
        at += count
    own = c_ref[...]
    both = min(at, total.shape[0])
    o_ref[:both, :] = jnp.where(end_ref[0] == 1, own[:both, :], total[:both, :])
    if o_ref.shape[0] > both:
        o_ref[both:, :] = (own if at > both else total)[both:, :]


def next_piece(cuts, end, s, y, *blocks):
    size, width = sum(count for _, count in cuts), s.shape[1]
    return pl.pallas_call(
        functools.partial(next_kernel, cuts),
        in_specs=[SMEM] + [VMEM] * (2 + len(blocks)),
        out_specs=(VMEM, VMEM, VMEM),
        out_shape=(
            jax.ShapeDtypeStruct(s.shape, F32),
            jax.ShapeDtypeStruct((max(size, s.shape[0]), width), F32),
            jax.ShapeDtypeStruct((size, width), F32),
        ),
        name="next",
        compiler_params=room(10),
        cost_estimate=cost(0, 0),
    )(end, s, y, *blocks)


def final_kernel(place, cuts, step, end_ref, at_ref, *refs):
    n, m = len(cuts), 1 + max(k for half in cuts for k, _, _ in half)
    rxs, ss = refs[:m], refs[m : 2 * m]
    ratio_ref, sum_ref, inv_ref, a_ref, _, _, o_ref, a, b, sems = refs[2 * m :]
    load = pltpu.make_async_copy(a_ref.at[at_rows(at_ref[place], step, n)], a, sems.at[n])
    load.start()
    rows = lax.broadcasted_iota(jnp.int32, (16, step), 0)
    ones = (lax.broadcasted_iota(jnp.int32, (16, LANES), 0) < 3).astype(BF16)
    stores = []
    for k in range(n):
        at, here = at_ref[place] + k, at_rows(k, step)
        ratio = ratio_ref[pl.ds(at, 1), :]
        high = ratio.astype(BF16).astype(F32)
        mid = (ratio - high).astype(BF16).astype(F32)
        terms = jnp.where(rows == 0, high, jnp.where(rows == 1, mid, jnp.where(rows == 2, ratio - high - mid, 0.0)))
        column = lax.dot_general(terms.astype(BF16), ones, (((0,), (0,)), ((), ())), preferred_element_type=F32)
        whole = jnp.concatenate(
            [
                jnp.where(end_ref[0] == 1, rxs[i][first : first + count, :], ss[i][first : first + count, :])
                for i, first, count in cuts[k]
            ],
            axis=0,
        )
        value = whole + (sum_ref[0:1, :] - column * inv_ref[...])
        if k == 0:
            load.wait()
        b[here, :] = a[here, :] * value
        stores.append(pltpu.make_async_copy(b.at[here], o_ref.at[at_rows(at, step)], sems.at[k]))
        stores[-1].start()
    for store in stores:
        store.wait()


def final_block(step, cuts, place, end, at, rxs, ss, ratio, ratio_sum, inv, a, grad):
    width = a.shape[1]
    n, m = len(cuts), len(ss)
    return pl.pallas_call(
        functools.partial(final_kernel, place, cuts, step),
        in_specs=[SMEM, SMEM] + [VMEM] * (2 * m + 3) + [HBM, HBM],
        out_specs=(HBM, HBM),
        out_shape=(pltpu.HBM(a.shape, F32), pltpu.HBM(grad.shape, F32)),
        scratch_shapes=[pltpu.VMEM((n * step, width), F32)] * 2 + [pltpu.SemaphoreType.DMA((1 + n,))],
        input_output_aliases={5 + 2 * m: 0, 6 + 2 * m: 1},
        name="final",
        compiler_params=room(12),
        cost_estimate=cost(0, 0),
    )(end, at, *rxs, *ss, ratio, ratio_sum, inv, a, grad)


def blank(shape):
    return pl.pallas_call(lambda o_ref: None, out_specs=HBM, out_shape=pltpu.HBM(shape, F32), name="blank")()


def scalars_kernel(n, cells, spots, step, end_ref, *refs):
    sums = [refs[k][-8:, :] for k in range(n)]
    rx_ref, s_ref, q_ref, kl_ref, loss_ref, map_ref, pred_ref = refs[n:]
    while len(sums) > 1:
        sums = [a + b for a, b in zip(sums[::2], sums[1::2], strict=True)]
    by_gene = jnp.where(end_ref[0] == 1, rx_ref[step : step + 8, :], s_ref[step : step + 8, :])
    cosine, fitted, wsum, scos = by_gene[0:1, :], sums[0][2:3, :], by_gene[3:4, :], sums[0][1:2, :]
    loss = -cosine / wsum - scos / spots + kl_ref[0:1, :]
    rms_map = jnp.sqrt(q_ref[q_ref.shape[0] - 1 :, q_ref.shape[1] - 8 :] / (cells * spots))
    rms_pred = jnp.sqrt(fitted / (spots * GENES))
    for ref, value in zip((loss_ref, map_ref, pred_ref), (loss, rms_map, rms_pred), strict=True):
        ref[0, 0] = jnp.max(value)


def scalar_results(n, cells, spots, step, end, *args):
    return pl.pallas_call(
        functools.partial(scalars_kernel, n, cells, spots, step),
        in_specs=[SMEM] + [VMEM] * len(args),
        out_specs=(SMEM,) * 3,
        out_shape=(jax.ShapeDtypeStruct((1, 1), F32),) * 3,
        name="scalars",
        compiler_params=room(24),
        cost_estimate=cost(0, 0),
    )(end, *args)


def shards(logits, expression, spatial, density, gene_mask, gene_counts, slide_ids):
    n_blk = lax.axis_size("blk")
    n_gene = lax.axis_size("gene")
    me = lax.axis_index("blk")
    plane = lax.axis_index("gene")
    cells, width = logits.shape
    rows, genes = expression.shape
    half = rows // 2
    spots = width * n_blk
    order = Order()

    def swap(x, m):
        return lax.ppermute(x, "blk", [(i, i ^ m) for i in range(n_blk)])

    def across(x, m):
        return lax.ppermute(x, "gene", [(i, i ^ m) for i in range(n_gene)])

    def cut(l, r, first, size):
        return lax.dynamic_slice_in_dim(l, (me ^ r) * rows + first, size, 0)

    far = sorted(range(2, n_blk, 2), key=lambda m: (m.bit_count(), m))
    side = plane % 2
    at = jnp.stack([side, 1 - side, *[(me ^ r) * 2 + k for r in range(n_blk) for k in range(2)]]
        + [(me ^ r) * 2 + side for r in range(n_blk)]).astype(jnp.int32)

    def whole(r):
        return (2 + 2 * r, 3 + 2 * r)

    def mine(r):
        return (2 + 2 * n_blk + r,)

    sent, passed, held = {}, {}, {}

    other = swap(expression, 1)
    constants = (slide_ids[None, :], gene_mask, gene_counts[None, :])
    n_q = cells // genes

    def add_pred(jobs, n_acc, ls, given=(), tail=()):
        n, g = len(ls), len(given)

        def run(*a):
            return pred_sums_of(jobs, n_acc, half, at, a[:n], a[n + g : n + g + 4], a[n : n + g], a[n + g + 4 :])

        return order(run, (*ls, *given), (*own_x, *other_x, *tail))

    def cuts(*layout):
        return order(lambda l: cut_blocks(layout, half, at, l), (logits,))

    if n_blk == 8 and n_gene == 4:
        near3, near5 = order(
            lambda l: [lax.dynamic_slice_in_dim(l, (me ^ r) * rows + side * half, half, 0) for r in (3, 5)], (logits,)
        )
        sent[3], sent[5] = swap(near3, 2), swap(near5, 4)
        own_x = order(lambda x: parts_of(x, half), (expression,))
        both, near2, near4, stay = cuts(mine(6) + mine(7), whole(2), whole(4), whole(0) + whole(1))
        passed[3] = across(order(join, (sent[3], sent[5])), 1)
        sent[6], sent[2], sent[4] = swap(order.here(both), 6), swap(order.here(near2), 2), swap(order.here(near4), 4)
        inv, by_cell, scale = order(functools.partial(softmax_sums, spots, genes, half), (logits,))
        other_x = order(lambda x: parts_of(x, half), (other,))
        (acc0,) = add_pred(((0, 0, 0, 0, 0, 0, 2), (0, 0, 0, 2, 1, 0, 2)), 1, (stay,))
        acc2, acc4 = add_pred(((0, 0, 0, 0, 1, [0], 1), (1, 0, 1, 0, 1, [0], 1)), 2, (sent[3], sent[5]))
        cell_moved = swap(order.here(by_cell), 1)
        passed[6] = across(order.here(sent[6]), 1)
        (acc6,) = add_pred(((0, 0, 0, 0, 0, [0], 1), (0, 0, 0, 1, 1, [0], 1)), 1, (sent[6],))
        acc2, acc4 = add_pred(
            ((0, 1, 0, 0, 1, [1], 1), (1, 2, 0, 1, 1, [1], 1)), 2, (passed[3],), (acc2, acc4)
        )
        by_cell = order(plus, (by_cell, cell_moved))
        (acc2,) = add_pred(((0, 1, 0, 0, 0, 0, 2),), 1, (sent[2],), (acc2,), (by_cell,))
        moved = {2: swap(acc2, 2)}
        (acc4,) = add_pred(((0, 1, 0, 0, 0, 0, 2),), 1, (sent[4],), (acc4,), (by_cell,))
        moved[4] = swap(acc4, 4)
        (acc6,) = add_pred(((0, 1, 0, 0, 0, [1], 1), (0, 0, 0, 1, 1, [1], 1)), 1, (passed[6],), (acc6,), (by_cell,))
        moved[6] = swap(acc6, 6)
        held = {
            2: ((sent[2],), 0),
            3: ((sent[3], passed[3]), (0, 0)),
            4: ((sent[4],), 0),
            5: ((sent[5], passed[3]), (0, 1)),
            6: ((sent[6], passed[6]), (0, 0)),
            7: ((sent[6], passed[6]), (1, 1)),
        }
    else:
        inv, by_cell, scale = order(functools.partial(softmax_sums, spots, genes, half), (logits,))
        by_cell = order(plus, (by_cell, swap(by_cell, 1)))
        own_x = order(lambda x: parts_of(x, half), (expression,))
        other_x = order(lambda x: parts_of(x, half), (other,))
        (stay,) = cuts(whole(0) + whole(1))
        (acc0,) = add_pred(((0, 0, 0, 0, 0, 0, 2), (0, 0, 0, 2, 1, 0, 2)), 1, (stay,))
        moved = {}
        for m in far:
            blocks = cuts(whole(m), whole(m + 1))
            for r in (m, m + 1):
                sent[r] = swap(blocks[r - m], m)
                held[r] = ((sent[r],), 0)
            (acc,) = add_pred(((0, 0, 0, 0, 0, 0, 2), (0, 0, 1, 0, 1, 0, 2)), 1, (sent[m], sent[m + 1]), (), (by_cell,))
            moved[m] = swap(acc, m)
    held[0], held[1] = ((stay,), 0), ((stay,), 2)

    parts = [acc0] + [moved[m] for m in far]
    pred, wide, spot, by_cell = order(
        functools.partial(pred_sums, len(parts)), parts, (by_cell, inv, spatial, *constants)
    )
    density = density.reshape(cells // half, half)
    state = {"scale": scale, "grad": blank((cells, width))}

    spot_moved = across(spot, 1)
    m = 1
    while 2 * m < n_blk:
        wide = order(plus, (wide, swap(wide, m)))
        m *= 2
        if m == 2:
            spot = order(add_all, (spot, spot_moved))
            spot_moved = across(spot, 2)
    wide_moved = swap(wide, m)
    grad, tot = order(
        functools.partial(dpred_scaled, spots, 1.0 / n_gene),
        (wide, wide_moved, spot, spot_moved),
        (pred, spatial, *constants, inv),
    )
    grads, back, tails = {0: grad}, {}, {}

    def dmap(ms, ranges, wait=(), tail=()):
        outs = order(
            lambda *a: dmap_blocks(ranges, a[: len(ms)], a[len(ms) : len(ms) + 4], a[len(ms) + 4 :]),
            [grads[m] for m in ms],
            (*own_x, *other_x, *tail),
            wait,
        )
        if tail and ms != (0,):
            tails.update({m: swap(d, m) for m, d in zip(ms, outs, strict=True)})
            return [tails[m] for m in ms]
        return [swap(d, m) if m else d for m, d in zip(ms, outs, strict=True)]

    def block_rows(odd):
        return ((odd, 0, half), (odd, half, half))

    blocks = [0, 1, 2, 4, 3, 5, 6, 7] if n_blk == 8 else [r for m in [0, *far] for r in (m, m + 1)]
    long = 848
    short = 2 * rows // 3 // 16 * 16
    sizes = [2 * rows - 2 * short, short, short] + [long] * ((cells - 2 * rows) // long)
    sizes += [n for n in [cells - sum(sizes)] if n]
    starts = [sum(sizes[:t]) for t in range(len(sizes))]
    count, lag = len(sizes), 3
    assert starts[3] == 2 * rows and sum(sizes) == cells

    def overlap(first, size, cuts_at, cuts_size):
        found = []
        for k, (a, n) in enumerate(zip(cuts_at, cuts_size, strict=True)):
            low, high = max(first, a), min(first + size, a + n)
            if low < high:
                found.append((k, low - a, high - low))
        return found

    block_starts, block_sizes = [rows * k for k in range(len(blocks))], [rows] * len(blocks)
    part, total_of, mid, got, own = {}, {}, {}, {}, {}
    end = jnp.reshape((plane == 0) | (plane == n_gene - 1), (1,)).astype(jnp.int32)

    def send(t):
        if t >= count + lag:
            return
        if t < lag:
            ranges = overlap(starts[t], sizes[t], (0, rows), (rows, rows))
            own[t] = buffer = dmap((0,), tuple(ranges), (), (tot,) if t == 0 else ())[0]
        elif t < count:
            found = overlap(starts[t], sizes[t], block_starts, block_sizes)
            cuts = tuple((back[blocks[k]][1] + first, n) for k, first, n in found)
            total_of[t - lag], buffer, own[t] = order(
                lambda s, y, *b: next_piece(cuts, end, s, y, *b),
                (part[t - lag], mid[t - lag], *[back[blocks[k]][0] for k, _, _ in found]),
            )
        else:
            buffer = total_of[t - lag] = order(plus, (part[t - lag], mid[t - lag]))
        got[t] = lax.ppermute(buffer, "gene", PAIR)

    def finish(k):
        halves = [overlap(block_starts[k] + half * h, half, starts, sizes) for h in range(2)]
        ts = sorted({t for found in halves for t, _, _ in found})
        cuts = tuple(tuple((ts.index(t), first, n) for t, first, n in found) for found in halves)
        m = len(ts)
        state["scale"], state["grad"] = order(
            lambda *a: final_block(half, cuts, 2 + 2 * blocks[k], end, at, a[:m], a[m : 2 * m], *a[2 * m :]),
            (*[got[t + lag] for t in ts], *[total_of[t] for t in ts]),
            (state["ratio"], state["ratio_sum"], inv, state["scale"], state["grad"]),
        )

    last_piece = [max(t for t, _, _ in overlap(a, rows, starts, sizes)) for a in block_starts]

    def expr_part(odd, ks, adds=()):
        ms = [0, *far]
        ls = [l for m in ms for l in held[m + odd][0]]
        wheres = [held[m + odd][1] for m in ms]
        n, m = len(ls), len(adds)
        return order(
            lambda d, *a: egrad_part(ks, half, wheres, float(cells), at, a[m : m + n], (d, *a[m + n :]), a[:m]),
            (grads[0], *adds),
            (*ls, *[grads[m] for m in far]),
        )

    def first_dmap():
        if n_blk == 8:
            for r, d in zip((2, 4), dmap((2, 4), block_rows(0)), strict=True):
                back[r] = (d, 0)
        else:
            tails[0] = order(plus, (tot, tot_moved))
            for m in far:
                (d,) = dmap((m,), block_rows(0) + block_rows(1), (), (tails[0],))
                back[m], back[m + 1] = (d, 0), (d, rows)

    def second_dmap():
        if n_blk == 8:
            tails[0] = order(plus, (tot, tot_moved))
            for r, d in zip((3, 5), dmap((2, 4), block_rows(1), (back[2][0], back[4][0]), (tails[0],)), strict=True):
                back[r] = (d, 0)

    def third_dmap():
        if n_blk == 8:
            back[6] = (dmap((6,), block_rows(0), (back[3][0], back[5][0]))[0], 0)

    def fourth_dmap():
        if n_blk == 8:
            back[7] = (dmap((6,), block_rows(1), (), (tails[0],))[0], 0)

    def kl():
        state["scale"], state["ratio"], state["ratio_sum"], state["kl"] = order(
            functools.partial(ratio_part, spots), (by_cell,), (density, inv, state["scale"])
        )

    def egrad(k):
        state["swapped", k] = swap(expr_part(1, (k,)), 1)

    def scalars():
        state["scalars"] = order(
            functools.partial(scalar_results, n_blk // 2, cells, spots, sizes[0], end),
            (*[tails[m] for m in range(0, n_blk, 2)], got[lag], total_of[0], by_cell),
            (state["kl"],),
        )

    def expr():
        state["expr"] = expr_part(0, (0, 1), (state["swapped", 0], state["swapped", 1]))

    plan = {
        (0, "between"): [first_dmap],
        (1, "after"): [kl],
        (2, "between"): [second_dmap],
        (5, "between"): [third_dmap],
        (7, "between"): [fourth_dmap, functools.partial(egrad, 0)],
        (8, "between"): [functools.partial(egrad, 1)],
        (count, "between"): [scalars],
        (count + 1, "between"): [expr],
    }
    for k in range(len(blocks)):
        t = last_piece[k] + lag + 1
        if t < count + lag:
            plan.setdefault((t, "between"), []).append(functools.partial(finish, k))

    def extra(t, place):
        for step in plan.get((t, place), ()):
            step()

    send(0)
    for m in far:
        grads[m] = swap(order.here(grad), m)
    tot_moved = swap(order.here(tot), 1)
    for t in range(count + lag):
        extra(t, "before")
        send(t + 1)
        extra(t, "between")
        if t < count:
            part[t] = order(plus, (own[t], got[t]))
            mid[t] = lax.ppermute(part[t], "gene", MIDDLE)
        extra(t, "after")
    for k in range(len(blocks)):
        if last_piece[k] + lag + 1 >= count + lag:
            finish(k)
    loss, rms_map, rms_pred = (x[0, 0] for x in state["scalars"])
    return (loss, state["grad"], state["expr"], rms_map, rms_pred)


def solution(mesh):
    placed = (
        P(None, "blk"),
        P("blk", "gene"),
        P("blk", "gene"),
        P(),
        P(None, "gene"),
        P("gene"),
        P("blk"),
    )
    return jax.shard_map(
        shards,
        mesh=mesh,
        in_specs=placed,
        out_specs=(P(), P(None, "blk"), P("blk", "gene"), P(), P()),
        check_vma=False,
    )
```
